32 devices in a mesh: dp: 4 (over x, core), seq: 8 (over z, y).
Axes of the slice: x: 2, y: 2, z: 4, core: 2. Of those that a mesh axis runs over, the one named last changes fastest.
Arguments:
- inputs: bfloat16 [8192, 512], P(('dp', 'seq')), may hold values from -6 to 6
- qkv_weight: float32 [512, 1536], P(None, ('dp', 'seq')), may hold values from -0.25 to 0.25
- out_weight: float32 [512, 512], P(None, ('dp', 'seq')), may hold values from -1.5 to 1.5
- up_weight: float32 [512, 2048], P(None, ('dp', 'seq')), may hold values from -0.25 to 0.25
- down_weight: float32 [2048, 512], P(None, ('dp', 'seq')), may hold values from -0.125 to 0.125
- biases: float32 [4, 512], P(None, ('dp', 'seq')), may hold values from -3 to 3
- up_bias: float32 [2048], P(('dp', 'seq')), may hold values from -3 to 3
- norms: float32 [4, 512], P(None, ('dp', 'seq')), may hold values from -1 to 1.5, as said below
- cotangent: bfloat16 [8192, 512], P(('dp', 'seq')), may hold values from -6 to 6
- prefix: int32 [4], P('dp'), may hold values from 204 to 1024, as said below
Outputs:
- output: bfloat16 [8192, 512], P(('dp', 'seq'))
- input_grad: float32 [8192, 512], P(('dp', 'seq'))
- grad_qkv: float32 [512, 1536], P(None, ('dp', 'seq'))
- grad_out: float32 [512, 512], P(None, ('dp', 'seq'))
- grad_up: float32 [512, 2048], P(None, ('dp', 'seq'))
- grad_down: float32 [2048, 512], P(None, ('dp', 'seq'))
- grad_biases: float32 [4, 512], P(None, ('dp', 'seq'))
- grad_up_bias: float32 [2048], P(('dp', 'seq'))
- grad_norms: float32 [4, 512], P(None, ('dp', 'seq'))
The draws below stay inside these ranges and needn't reach their ends.
Inputs may be any that keep to these rules, and one draw needn't show every extreme that they name: prefix of a sequence counts its leading positions that every position of the sequence sees; some sequence has exactly 1024 and some exactly 204. `norms`: rows 0 and 2 are gains, rows 1 and 3 shifts.
All inputs are finite; a program needn't handle non-finite values.
Results may differ from the reference program's by a relative error of at most 0.017.
The reference program's roundings to bfloat16 on the way count: a program that leaves them out, or rounds other values in their place, can miss the bound.
Values may be sent and summed in bfloat16 or wider, within the bound.
A program may use at most 192 MiB of HBM per device.

```python
import jax
import jax.numpy as jnp
from jax import lax

D = 512
HEADS = 8
FF = 2048
SEQ_LEN = 2048
SEQS = 4
TOKENS = 8192


def draw_norms(key, part):
    first_key, second_key = jax.random.split(jax.random.fold_in(key, 11))
    gains = jax.random.uniform(first_key, (4, D), jnp.float32, 0.5, 1.5)
    shifts = jnp.clip(0.3 * jax.random.normal(second_key, (4, D), jnp.float32), -1.0, 1.0)
    parity = jnp.arange(4, dtype=jnp.int32)[:, None] % 2
    return jnp.where(parity == 0, gains, shifts).astype(jnp.float32)


def draw_prefix(key, part):
    first_key, second_key = jax.random.split(jax.random.fold_in(key, 23))
    lowest = SEQ_LEN // 10
    highest = SEQ_LEN // 2
    values = jax.random.randint(first_key, (SEQS,), lowest, highest + 1, dtype=jnp.int32)
    order = jax.random.permutation(second_key, SEQS)
    index = jnp.arange(SEQS, dtype=jnp.int32)
    values = jnp.where(index == order[0], highest, values)
    values = jnp.where(index == order[1], lowest, values)
    return values.astype(jnp.int32)


def shard_levels(stream_key, dims, pieces, smallest, high):
    factor_of = 1.0
    for position, blocks in pieces:
        steps = jax.random.uniform(jax.random.fold_in(jax.random.fold_in(stream_key, 6), position), (blocks,), jnp.float32, smallest / len(pieces), high / len(pieces))
        factor_of = factor_of * jnp.repeat(jnp.exp(steps), dims[position] // blocks).reshape((-1,) + (1,) * (len(dims) - 1 - position))
    return factor_of


def centred(key, dims, width, bound, cuts=(), kind=jnp.bfloat16):
    array = jax.random.normal(key, dims, jnp.float32) * width
    if len(cuts) > 0:
        array = shard_levels(key, dims, cuts, -0.22, 0.18) * array
    return jnp.clip(array, min=-bound, max=bound).astype(kind)


def setup_inputs(seed: int = 0) -> dict:
    arg_keys = jax.random.split(jax.random.key(seed), 11)
    inputs = centred(arg_keys[0], (TOKENS, D), 1.0, 6.0, ((0, 32),))
    qkv_weight = centred(arg_keys[1], (D, 3 * D), D ** -0.5, 0.25, ((1, 32),), jnp.float32)
    out_weight = centred(arg_keys[2], (D, D), (max(D // 32, 1)) ** -0.5, 1.5, ((1, 32),), jnp.float32)
    up_weight = centred(arg_keys[3], (D, FF), D ** -0.5, 0.25, ((1, 32),), jnp.float32)
    down_weight = centred(arg_keys[4], (FF, D), FF ** -0.5, 0.125, ((1, 32),), jnp.float32)
    biases = centred(arg_keys[5], (4, D), 0.5, 3.0, ((1, 32),), jnp.float32)
    up_bias = centred(arg_keys[6], (FF,), 0.5, 3.0, ((0, 32),), jnp.float32)
    norms = draw_norms(jax.random.fold_in(arg_keys[10], 71), 0)
    cotangent = centred(arg_keys[8], (TOKENS, D), 1.0, 6.0, ((0, 32),))
    prefix = draw_prefix(jax.random.fold_in(arg_keys[10], 71), 0)
    return dict(inputs=inputs, qkv_weight=qkv_weight, out_weight=out_weight, up_weight=up_weight, down_weight=down_weight, biases=biases, up_bias=up_bias, norms=norms, cotangent=cotangent, prefix=prefix)


EPSILON = 1e-05
NEGATIVE = -1e+30
SCORE_SCALE = 0.125
PRECISE = lax.Precision.HIGHEST

@jax.custom_vjp
def low(v):
    return lax.optimization_barrier(v.astype(jnp.bfloat16)).astype(jnp.float32)

@jax.custom_vjp
def low_back(v):
    return v

def low_keep(v):
    return (low(v), None)

def low_pass(kept, grad):
    return (grad,)

def back_keep(v):
    return (v, None)

def back_low(kept, grad):
    return (low(grad),)
low.defvjp(low_keep, low_pass)
low_back.defvjp(back_keep, back_low)

def matmul(first_op, second_op):
    return jnp.dot(first_op, second_op, precision=PRECISE, preferred_element_type=jnp.float32)

def layer_norm(values, gain_vec, shift_vec):
    centre = values - lax.optimization_barrier(jnp.mean(values, axis=1, keepdims=True))
    inv_std = lax.rsqrt(lax.optimization_barrier(jnp.mean(centre * centre, axis=1, keepdims=True)) + EPSILON)
    return centre * inv_std * gain_vec + shift_vec

def attend_block(query_block, start, keys, values, prefix_len):
    block_rows = query_block.shape[0]
    key_count = keys.shape[0]
    scores = jnp.einsum('qhd,khd->hqk', query_block, keys, precision=PRECISE) * SCORE_SCALE
    scores = low_back(scores)
    row_index = start + jnp.arange(block_rows, dtype=jnp.int32)
    key_index = jnp.arange(key_count, dtype=jnp.int32)
    visible = (key_index[None, :] <= row_index[:, None]) | (key_index[None, :] < prefix_len)
    scores = jnp.where(visible[None], scores, NEGATIVE)
    probability = low(jax.nn.softmax(scores, axis=-1))
    attended = jnp.einsum('hqk,khd->qhd', probability, values, precision=PRECISE)
    return attended.reshape(block_rows, -1)

def attention(queries, keys, values, prefix_len):
    seq_len, features = queries.shape
    head_dim = features // HEADS
    block_rows = min(512, seq_len)
    blocks = queries.reshape(seq_len // block_rows, block_rows, HEADS, head_dim)
    starts = jnp.arange(seq_len // block_rows, dtype=jnp.int32) * block_rows
    keys_heads = keys.reshape(seq_len, HEADS, head_dim)
    values_heads = values.reshape(seq_len, HEADS, head_dim)

    def one_block(query_block, start):
        return attend_block(query_block, start, keys_heads, values_heads, prefix_len)
    checked = jax.checkpoint(one_block)

    def apply_block(members):
        return checked(members[0], members[1])
    result = lax.map(apply_block, (blocks, starts))
    return result.reshape(seq_len, features)

def layer_ref(stream, weights, prefix_len):
    w_qkv, w_out, w_up, w_down, vec_bias, b_up, vec_norm = weights
    features = stream.shape[1]
    bias_row = jnp.concatenate([vec_bias[0], jnp.zeros_like(vec_bias[0]), vec_bias[1]])
    qkv = low(low_back(matmul(low(stream), w_qkv) + bias_row))
    attended = attention(qkv[:, :features], qkv[:, features:2 * features], qkv[:, 2 * features:], prefix_len)
    attended = low(low_back(attended))
    branch = low_back(matmul(attended, w_out) + vec_bias[2])
    normed = layer_norm(stream + branch, vec_norm[0], vec_norm[1])
    hidden = low_back(matmul(low(normed), w_up) + b_up)
    active = low(jax.nn.gelu(hidden, approximate=False))
    second = low_back(matmul(active, w_down) + vec_bias[3])
    return layer_norm(normed + second, vec_norm[2], vec_norm[3])

def reference(inputs, qkv_weight, out_weight, up_weight, down_weight, biases, up_bias, norms, cotangent, prefix):
    masters = (qkv_weight, out_weight, up_weight, down_weight, biases, up_bias, norms)
    streams = inputs.astype(jnp.float32).reshape(SEQS, SEQ_LEN, D)
    cotangents = cotangent.astype(jnp.float32).reshape(SEQS, SEQ_LEN, D)

    def one_sequence(carried, members):
        stream, grad_output, prefix_len = members

        def forward(stream_in, *weight_in):
            lowered = tuple((low(tensor) for tensor in weight_in))
            middle = layer_ref(stream_in, lowered, prefix_len)
            return layer_ref(middle, lowered, prefix_len)
        result, pullback = jax.vjp(forward, stream, *masters)
        gradients = pullback(grad_output)
        updated = tuple((prior + fresh for prior, fresh in zip(carried, gradients[1:])))
        return (updated, (result, gradients[0]))
    start_sums = tuple((jnp.zeros_like(tensor) for tensor in masters))
    totals, (results, input_grads) = lax.scan(one_sequence, start_sums, (streams, cotangents, prefix))
    return (results.reshape(TOKENS, D).astype(jnp.bfloat16), input_grads.reshape(TOKENS, D), totals[0], totals[1], totals[2], totals[3], totals[4], totals[5], totals[6])
```

```python
import math

import jax
import jax.numpy as jnp
from jax import lax
from jax.experimental import pallas as pl
from jax.experimental.pallas import tpu as pltpu
from jax.sharding import PartitionSpec as P

HEADS = 8


EPSILON = 1e-05
NEGATIVE = -1e30
SCORE_SCALE = 0.125
ROOT_HALF = 1.0 / math.sqrt(2.0)
DENSITY_SCALE = 1.0 / math.sqrt(2.0 * math.pi)


def dot_rows(first_op, second_op):
    return lax.dot_general(
        first_op, second_op, (((1,), (1,)), ((), ())), preferred_element_type=jnp.float32
    )


def dot_cols(first_op, second_op):
    return lax.dot_general(
        first_op, second_op, (((0,), (0,)), ((), ())), preferred_element_type=jnp.float32
    )


def split_heads(tensor_in):
    return tensor_in.reshape(tensor_in.shape[0], HEADS, -1).transpose(1, 0, 2)


def merge_heads(stacked):
    return stacked.transpose(1, 0, 2).reshape(stacked.shape[1], -1)


def cast_all(masters):
    return tuple((tensor.astype(jnp.bfloat16) for tensor in masters))


def fetch_forward(masters):
    casted = cast_all(masters)
    return (
        lax.all_gather(casted[0], ("dp", "seq"), axis=1, tiled=True),
        lax.all_gather(casted[1], ("dp", "seq"), axis=1, tiled=True),
        lax.all_gather(casted[2], ("dp", "seq"), axis=1, tiled=True),
        lax.all_gather(casted[3], ("dp", "seq"), axis=1, tiled=True),
        lax.all_gather(casted[4], ("dp", "seq"), axis=1, tiled=True),
        lax.all_gather(casted[5], ("dp", "seq"), axis=0, tiled=True),
        lax.all_gather(casted[6], ("dp", "seq"), axis=1, tiled=True),
    )


def fetch_backward(masters):
    casted = cast_all(masters)
    return (
        lax.all_gather(casted[0], ("dp", "seq"), axis=1, tiled=True),
        lax.all_gather(casted[1], ("dp", "seq"), axis=1, tiled=True),
        lax.all_gather(casted[2], ("dp", "seq"), axis=1, tiled=True),
        lax.all_gather(casted[3], ("dp", "seq"), axis=1, tiled=True),
        lax.all_gather(casted[4], ("dp", "seq"), axis=1, tiled=True),
        lax.all_gather(casted[5], ("dp", "seq"), axis=0, tiled=True),
        lax.all_gather(casted[6], ("dp", "seq"), axis=1, tiled=True),
    )


def gelu_slope(values):
    normal_cdf = 0.5 * (1.0 + jax.scipy.special.erf(values * ROOT_HALF))
    return normal_cdf + values * jnp.exp(-0.5 * values * values) * DENSITY_SCALE


def layer_norm(values, gain_vec, shift_vec):
    centre = values - jnp.mean(values, axis=1, keepdims=True)
    inv_std = lax.rsqrt(jnp.mean(centre * centre, axis=1, keepdims=True) + EPSILON)
    centred = centre * inv_std
    return (centred * gain_vec + shift_vec, centred, inv_std)


def norm_back(grad_out, centred, inv_std, gain_vec):
    scaled = grad_out * gain_vec
    grad_gain = jnp.sum(grad_out * centred, axis=0)
    grad_shift = jnp.sum(grad_out, axis=0)
    grad_in = inv_std * (
        scaled
        - jnp.mean(scaled, axis=1, keepdims=True)
        - centred * jnp.mean(scaled * centred, axis=1, keepdims=True)
    )
    return (grad_in, grad_gain, grad_shift)


def attend_forward(queries, gathered, visible):
    features = queries.shape[1]
    head_q = split_heads(queries)
    head_k = split_heads(gathered[:, :features])
    head_v = split_heads(gathered[:, features:])

    def one_head(members):
        head_query, head_keys, head_values = members
        scores = jnp.where(visible, dot_rows(head_query, head_keys) * SCORE_SCALE, NEGATIVE)
        largest = jnp.max(scores, axis=1, keepdims=True)
        exponent = jnp.exp(scores - largest)
        row_total = jnp.sum(exponent, axis=1, keepdims=True)
        probability = (exponent / row_total).astype(jnp.bfloat16)
        head_out = jnp.dot(probability, head_values, preferred_element_type=jnp.float32)
        return (head_out, (largest + jnp.log(row_total))[:, 0])

    head_outs, log_totals = lax.map(one_head, (head_q, head_k, head_v))
    return (merge_heads(head_outs), log_totals)


def attend_backward(queries, gathered, visible, grad_att, log_totals):
    features = queries.shape[1]
    head_q = split_heads(queries)
    head_k = split_heads(gathered[:, :features])
    head_v = split_heads(gathered[:, features:])
    head_g = split_heads(grad_att)

    def one_head(members):
        head_query, head_keys, head_values, head_grad, head_logs = members
        scores = jnp.where(visible, dot_rows(head_query, head_keys) * SCORE_SCALE, NEGATIVE)
        probability = jnp.exp(scores - head_logs[:, None])
        grad_prob = dot_rows(head_grad, head_values)
        row_delta = jnp.sum(probability * grad_prob, axis=1)
        grad_score = (probability * (grad_prob - row_delta[:, None])).astype(jnp.bfloat16)
        grad_query = (
            jnp.dot(grad_score, head_keys, preferred_element_type=jnp.float32) * SCORE_SCALE
        )
        grad_keys = dot_cols(grad_score, head_query) * SCORE_SCALE
        grad_values = dot_cols(probability.astype(jnp.bfloat16), head_grad)
        return (grad_query, grad_keys, grad_values)

    results = lax.map(one_head, (head_q, head_k, head_v, head_g, log_totals))
    grad_query = merge_heads(results[0])
    return (grad_query, jnp.concatenate([merge_heads(results[1]), merge_heads(results[2])], axis=1))


def layer_forward(stream, weights, visible):
    w_qkv, w_out, w_up, w_down, vec_bias, b_up, vec_norm = weights
    vec_bias = vec_bias.astype(jnp.float32)
    b_up = b_up.astype(jnp.float32)
    vec_norm = vec_norm.astype(jnp.float32)
    features = stream.shape[1]
    stream_low = stream.astype(jnp.bfloat16)
    bias_row = jnp.concatenate([vec_bias[0], jnp.zeros_like(vec_bias[0]), vec_bias[1]])
    qkv = (jnp.dot(stream_low, w_qkv, preferred_element_type=jnp.float32) + bias_row).astype(
        jnp.bfloat16
    )
    queries = qkv[:, :features]
    local_kv = qkv[:, features:]
    gathered = lax.all_gather(local_kv, "seq", axis=0, tiled=True)
    attended, log_totals = attend_forward(queries, gathered, visible)
    att_low = attended.astype(jnp.bfloat16)
    branch = jnp.dot(att_low, w_out, preferred_element_type=jnp.float32) + vec_bias[2]
    normed, centred_one, inv_std_one = layer_norm(stream + branch, vec_norm[0], vec_norm[1])
    normed_low = normed.astype(jnp.bfloat16)
    hidden = jnp.dot(normed_low, w_up, preferred_element_type=jnp.float32) + b_up
    active = jax.nn.gelu(hidden, approximate=False).astype(jnp.bfloat16)
    second = jnp.dot(active, w_down, preferred_element_type=jnp.float32) + vec_bias[3]
    result, centred_two, inv_std_two = layer_norm(normed + second, vec_norm[2], vec_norm[3])
    cache = (
        stream_low,
        queries,
        local_kv,
        None,
        att_low,
        log_totals,
        centred_one,
        inv_std_one,
        normed_low,
        hidden,
        active,
        centred_two,
        inv_std_two,
    )
    return (result, cache)


def layer_backward(gradient, cache, weights, visible):
    w_qkv, w_out, w_up, w_down, vec_bias, b_up, vec_norm = weights
    vec_norm = vec_norm.astype(jnp.float32)
    (
        stream_low,
        queries,
        local_kv,
        kept_kv,
        att_low,
        log_totals,
        centred_one,
        inv_std_one,
        normed_low,
        hidden,
        active,
        centred_two,
        inv_std_two,
    ) = cache
    features = queries.shape[1]
    gathered = lax.all_gather(local_kv, "seq", axis=0, tiled=True)
    grad_two, gain_two, shift_two = norm_back(gradient, centred_two, inv_std_two, vec_norm[2])
    grad_second = grad_two.astype(jnp.bfloat16)
    bias_down = jnp.sum(grad_second.astype(jnp.float32), axis=0)
    grad_w_down = dot_cols(active, grad_second)
    grad_active = dot_rows(grad_second, w_down)
    grad_hidden = (grad_active * gelu_slope(hidden)).astype(jnp.bfloat16)
    bias_upper = jnp.sum(grad_hidden.astype(jnp.float32), axis=0)
    grad_w_up = dot_cols(normed_low, grad_hidden)
    grad_normed = grad_two + dot_rows(grad_hidden, w_up)
    grad_one, gain_one, shift_one = norm_back(grad_normed, centred_one, inv_std_one, vec_norm[0])
    grad_branch = grad_one.astype(jnp.bfloat16)
    bias_output = jnp.sum(grad_branch.astype(jnp.float32), axis=0)
    grad_w_out = dot_cols(att_low, grad_branch)
    grad_att = dot_rows(grad_branch, w_out).astype(jnp.bfloat16)
    grad_query, kv_terms = attend_backward(queries, gathered, visible, grad_att, log_totals)
    kv_grad = lax.psum_scatter(
        kv_terms.astype(jnp.bfloat16), "seq", scatter_dimension=0, tiled=True
    ).astype(jnp.float32)
    grad_qkv = jnp.concatenate([grad_query, kv_grad], axis=1).astype(jnp.bfloat16)
    qkv_sums = jnp.sum(grad_qkv.astype(jnp.float32), axis=0)
    grad_w_qkv = dot_cols(stream_low, grad_qkv)
    grad_stream = grad_one + dot_rows(grad_qkv, w_qkv)
    grad_bias = jnp.stack([qkv_sums[:features], qkv_sums[2 * features :], bias_output, bias_down])
    grad_norm = jnp.stack([gain_one, shift_one, gain_two, shift_two])
    return (
        grad_stream,
        (grad_w_qkv, grad_w_out, grad_w_up, grad_w_down, grad_bias, bias_upper, grad_norm),
    )


def local(
    inputs,
    qkv_weight,
    out_weight,
    up_weight,
    down_weight,
    biases,
    up_bias,
    norms,
    cotangent,
    prefix,
):
    masters = (qkv_weight, out_weight, up_weight, down_weight, biases, up_bias, norms)
    row_count = inputs.shape[0]
    key_count = row_count * lax.axis_size("seq")
    rows_here = lax.axis_index("seq") * row_count + jnp.arange(row_count, dtype=jnp.int32)
    all_index = jnp.arange(key_count, dtype=jnp.int32)
    visible = (all_index[None, :] <= rows_here[:, None]) | (all_index[None, :] < prefix[0])
    stream = inputs.astype(jnp.float32)
    caches = []
    for position in range(2):
        weights = fetch_forward(masters)
        stream, cache = layer_forward(stream, weights, visible)
        caches.append(cache)
    gradient = cotangent.astype(jnp.float32)
    accumulated = None
    for position in range(2):
        weights = fetch_backward(masters)
        gradient, grad_parts = layer_backward(gradient, caches[1 - position], weights, visible)
        if accumulated is None:
            accumulated = grad_parts
        else:
            accumulated = tuple((prior + fresh for prior, fresh in zip(accumulated, grad_parts)))
    reduced = (
        lax.psum_scatter(accumulated[0], ("dp", "seq"), scatter_dimension=1, tiled=True),
        lax.psum_scatter(accumulated[1], ("dp", "seq"), scatter_dimension=1, tiled=True),
        lax.psum_scatter(accumulated[2], ("dp", "seq"), scatter_dimension=1, tiled=True),
        lax.psum_scatter(accumulated[3], ("dp", "seq"), scatter_dimension=1, tiled=True),
        lax.psum_scatter(accumulated[4], ("dp", "seq"), scatter_dimension=1, tiled=True),
        lax.psum_scatter(accumulated[5], ("dp", "seq"), scatter_dimension=0, tiled=True),
        lax.psum_scatter(accumulated[6], ("dp", "seq"), scatter_dimension=1, tiled=True),
    )
    return (
        stream.astype(jnp.bfloat16),
        gradient,
        reduced[0],
        reduced[1],
        reduced[2],
        reduced[3],
        reduced[4],
        reduced[5],
        reduced[6],
    )


F32 = jnp.float32
BF16 = jnp.bfloat16
MESH = pl.DeviceIdType.MESH
LOG2E = math.log2(math.e)
EXP2_SCALE = SCORE_SCALE * LOG2E


def mm_nn(a, b):
    return lax.dot_general(a, b, (((1,), (0,)), ((), ())), preferred_element_type=F32)


def mm_nt(a, b):
    return lax.dot_general(a, b, (((1,), (1,)), ((), ())), preferred_element_type=F32)


def mm_tn(a, b):
    return lax.dot_general(a, b, (((0,), (0,)), ((), ())), preferred_element_type=F32)


def fused_step(tokens, d_model, d_ff, heads):
    hd = d_model // heads
    seq_len = tokens * 8
    fixed = (seq_len // 2) // tokens
    class Group:
        def __init__(self, rows, cols, halves, kept=BF16):
            self.rows, self.cols, self.halves = rows, cols, halves
            self.whole = (halves, 2, 2, 4, 2, rows, cols)
            self.weight = vm(self.whole, BF16)
            self.grad = vm(self.whole, kept)
            one = (halves, 2, 4, 2, rows, cols)
            two = ((4, 2, rows, cols), (2, 4, rows, cols))[:halves]
            self.send1, self.recv1 = vm(one, BF16), vm(one, BF16)
            self.send2, self.recv2 = [vm(t, BF16) for t in two], [vm(t, BF16) for t in two]
            three_ = (4, rows, cols)
            self.send3, self.recv3 = [vm(three_, BF16) for t in two], [vm(three_, BF16) for t in two]
            self.sum3 = vm((4, halves, rows, cols), F32)
            self.send4, self.recv4 = vm((3, halves, rows, cols), BF16), vm((3, halves, rows, cols), BF16)

    chunk = d_ff // 4
    three = 3 * hd
    scratch = []
    count = [0]

    def take(number):
        first = count[0]
        count[0] += number
        return first

    def vm(shape, dtype):
        scratch.append(pltpu.VMEM(shape, dtype))
        return len(scratch) - 1

    def per_layer(shape, dtype):
        return [vm(shape, dtype) for _ in range(2)]

    g_qkv = Group(3 * d_model // 32, d_model // 2, 2)
    g_out = Group(d_model // 32, d_model // 2, 2)
    g_up = Group(d_ff // 32, d_model // 2, 2)
    g_down = Group(d_model // 32, d_ff // 2, 2)
    g_vec = Group(d_model // 32, 128, 1, F32)
    ag_order = (g_qkv, g_vec, g_out, g_up, g_down)
    rs_order = (g_down, g_up, g_out, g_qkv, g_vec)
    pack = vm((128, 16), F32)
    s_in, c_in = vm((tokens, d_model), BF16), vm((tokens, d_model), BF16)
    p_out, p_in = vm((8, 128), jnp.int32), vm((8, 128), jnp.int32)
    o_send, i_send, i_recv = (vm((tokens, d_model), BF16) for _ in range(3))
    x32, h1_ = vm((d_model, tokens), F32), vm((d_model, tokens), F32)
    xlow, hlow = per_layer((d_model, tokens), BF16), per_layer((d_model, tokens), BF16)
    xh1, xh2 = per_layer((d_model, tokens), F32), per_layer((d_model, tokens), F32)
    rs1, rs2 = per_layer((8, tokens), F32), per_layer((8, tokens), F32)
    slope, act = per_layer((d_ff, tokens), F32), per_layer((d_ff, tokens), BF16)
    lse, o32 = per_layer((8, 8, tokens), F32), per_layer((8, hd, tokens), F32)
    send1, send3 = vm((8, hd, tokens), BF16), vm((8, three, tokens), BF16)
    qr, ar = per_layer((8, three, tokens), BF16), per_layer((8, hd, tokens), BF16)
    dr, er = vm((8, hd, tokens), BF16), vm((8, three, tokens), BF16)
    kt, vt, qt, dt = (vm((seq_len, hd), BF16) for _ in range(4))
    dk, dv = vm((seq_len, hd), F32), vm((seq_len, hd), F32)
    df_ = vm((d_ff, tokens), BF16)
    gv = vm((d_model, 128), F32)

    def body(ins, outs, R, SS, RS):
        (in_ref, wqkv, wout, wup, wdown, biases, upb, norms, cot_ref, pref_ref) = ins
        (o_out, o_ig, o_qkv, o_gout, o_up, o_down, o_bias, o_upb, o_norms) = outs
        dp, sq = lax.axis_index("dp"), lax.axis_index("seq")
        x, c = dp // 2, dp % 2
        z, y = sq // 2, sq % 2
        zh, zl = z // 2, z % 2
        rank = 4 * c + 2 * zl + y

        def dev(x_, c_, z_, y_):
            return (x_ * 2 + c_, z_ * 2 + y_)

        def remote(src, dst, idx, device):
            return pltpu.make_async_remote_copy(
                src_ref=src, dst_ref=dst, send_sem=SS.at[idx], recv_sem=RS.at[idx],
                device_id=device, device_id_type=MESH,
            )

        def peer(k):
            c_ = (c + k // 4) % 2
            zl_ = (zl + (k // 2) % 2) % 2
            y_ = (y + k % 2) % 2
            return dev(x, c_, 2 * zh + zl_, y_), 4 * c_ + 2 * zl_ + y_

        sends = []

        barrier = pltpu.get_barrier_semaphore()
        swap_dev = dev(x, 1 - c, 2 * (1 - zh) + zl, y)
        greet = [peer(k)[0] for k in range(1, 8)]
        greet += [dev(1 - x, c, z, y), swap_dev]
        greet += [dev(x, c, 2 * (1 - zh) + zl_, y) for zl_ in range(2)]
        for d in greet:
            pl.semaphore_signal(barrier, inc=1, device_id=d, device_id_type=MESH)

        def place(n, value):
            for h in range(n.halves):
                R[n.weight][h, x, c, z, y] = value[:, h * n.cols : (h + 1) * n.cols]

        place(g_qkv, wqkv[...].T.astype(BF16))
        R[pack][0:4, :] = biases[...]
        R[pack][4:8, :] = norms[...]
        R[pack][8:12, :] = upb[...]
        R[pack][12:128, :] = jnp.zeros((116, 16), F32)
        place(g_vec, R[pack][...].T.astype(BF16))
        R[p_out][...] = jnp.full((8, 128), pref_ref[0], jnp.int32)
        place(g_out, wout[...].T.astype(BF16))
        place(g_up, wup[...].T.astype(BF16))
        place(g_down, wdown[...].T.astype(BF16))
        pl.semaphore_wait(barrier, len(greet))

        swapped = c != zh

        def swap(src, dst, idx):
            return remote(src, dst, idx, swap_dev)

        s_idx, c_idx, p_idx, so_idx, si_idx = (take(1) for _ in range(5))

        @pl.when(swapped)
        def _():
            swap(in_ref, R[s_in], s_idx).start()
            swap(R[p_out], R[p_in], p_idx).start()

        ag = {}
        for n in ag_order:
            ag[n] = (take(3), take(2), take(2), take(1))

        def ag_z(n):
            w = R[n.weight]
            cps = []
            for j in range(1, 4):
                own = w.at[:, x, c, z, y]
                cps.append(remote(own, own, ag[n][0] + j - 1, dev(x, c, (z + j) % 4, y)))
            for cp in cps:
                cp.start()
            sends.extend(cps)
            return cps

        def ag_a(n, waits):
            for cp in waits:
                cp.wait_recv()
            w = R[n.weight]
            cps = []
            part = w.at[0, x, c, :, y]
            cps.append(remote(part, part, ag[n][1], dev(x, c, z, 1 - y)))
            if n.halves == 2:
                part = w.at[1, x, c, :, y]
                cps.append(remote(part, part, ag[n][1] + 1, dev(1 - x, c, z, y)))
            for cp in cps:
                cp.start()
            sends.extend(cps)
            return cps

        def ag_b(n, waits):
            w = R[n.weight]
            cps = []
            waits[0].wait_recv()
            part = w.at[0, x, c]
            cps.append(remote(part, part, ag[n][2], dev(1 - x, c, z, y)))
            cps[-1].start()
            if n.halves == 2:
                waits[1].wait_recv()
                part = w.at[1, :, c, :, y]
                cps.append(remote(part, part, ag[n][2] + 1, dev(x, c, z, 1 - y)))
                cps[-1].start()
            sends.extend(cps)
            return cps

        def ag_c(n, waits):
            for cp in waits:
                cp.wait_recv()
            part = R[n.weight].at[:, :, c]
            cp = remote(part, part, ag[n][3], dev(x, 1 - c, z, y))
            cp.start()
            sends.append(cp)
            return [cp]

        state = {}
        for n in ag_order:
            state[n] = ag_z(n)
        for n in ag_order:
            state[n] = ag_a(n, state[n])
        for n in ag_order:
            state[n] = ag_b(n, state[n])
        for n in ag_order:
            state[n] = ag_c(n, state[n])

        @pl.when(swapped)
        def _():
            swap(cot_ref, R[c_in], c_idx).start()

        @pl.when(swapped)
        def _():
            swap(in_ref, R[s_in], s_idx).wait()
            swap(R[p_out], R[p_in], p_idx).wait()

        @pl.when(jnp.logical_not(swapped))
        def _():
            R[s_in][...] = in_ref[...]
            R[p_in][...] = R[p_out][...]

        for n in ag_order:
            for cp in state[n]:
                cp.wait_recv()

        def weight(n, h):
            return R[n.weight][h].reshape(32 * n.rows, n.cols)

        def vec(i):
            return R[g_vec.weight][0, :, :, :, :, :, i : i + 1].reshape(d_model, 1).astype(F32)

        def up_bias(i):
            lanes = [
                R[g_vec.weight][0, i // 2, i % 2, :, :, :, 8 + b : 9 + b].reshape(8, 1, 16, 1).astype(F32)
                for b in range(4)
            ]
            return jnp.concatenate(lanes, axis=1).reshape(chunk, 1)

        def spread(src, dst):
            base = take(8)
            cps = []
            for k in range(1, 8):
                device, other = peer(k)
                cps.append(remote(src.at[other], dst.at[rank], base + k, device))
                cps[-1].start()
            dst[rank] = src[rank]
            return cps

        def finish(cps):
            for cp in cps:
                cp.wait()

        def ext(qb):
            return max(fixed, qb + 1)

        def span(first, last=None):
            return slice(first * tokens, (first + 1 if last is None else last) * tokens)

        def masked(s, qb):
            if qb < fixed:
                kk = lax.broadcasted_iota(jnp.int32, s.shape, 0)
                qq = qb * tokens + lax.broadcasted_iota(jnp.int32, s.shape, 1)
                return jnp.where((kk <= qq) | (kk < R[p_in][0:1, 0:1]), s, NEGATIVE)
            low = s[qb * tokens :]
            kk = lax.broadcasted_iota(jnp.int32, low.shape, 0)
            qq = lax.broadcasted_iota(jnp.int32, low.shape, 1)
            low = jnp.where(kk <= qq, low, NEGATIVE)
            return jnp.concatenate([s[: qb * tokens], low], axis=0)

        def norm(r, gain, shift):
            centre = r - jnp.mean(r, axis=0, keepdims=True)
            inv = lax.rsqrt(jnp.mean(centre * centre, axis=0, keepdims=True) + EPSILON)
            xh = centre * inv
            return xh * gain + shift, xh, inv

        def forward(l):
            low = R[xlow[l]][...]
            wa, wb = weight(g_qkv, 0), weight(g_qkv, 1)
            half = d_model // 2
            for part in range(3):
                rows = slice(part * d_model, (part + 1) * d_model)
                t = mm_nn(wa[rows], low[:half]) + mm_nn(wb[rows], low[half:])
                if part != 1:
                    t = t + vec(part // 2)
                R[send3][:, part * hd : (part + 1) * hd, :] = t.astype(BF16).reshape(8, hd, tokens)
            finish(spread(R[send3], R[qr[l]]))
            qkv_all = R[qr[l]]
            for b in range(8):
                R[kt][span(b), :] = qkv_all[b, hd : 2 * hd, :].T
                R[vt][span(b), :] = qkv_all[b, 2 * hd :, :].T
            for qb in range(8):
                n = ext(qb)
                s = masked(mm_nn(R[kt][span(0, n), :], qkv_all[qb, 0:hd, :]) * EXP2_SCALE, qb)
                m = jnp.max(s, axis=0, keepdims=True)
                p = jnp.exp2(s - m)
                total = jnp.sum(p, axis=0, keepdims=True)
                o = mm_tn(p.astype(BF16), R[vt][span(0, n), :]).T / total
                R[o32[l]][qb] = o
                R[send1][qb] = o.astype(BF16)
                R[lse[l]][qb] = jnp.broadcast_to(m + jnp.log2(total), (8, tokens))
            finish(spread(R[send1], R[ar[l]]))
            att = R[ar[l]][...].reshape(d_model, tokens)
            r1 = R[x32][...] + vec(2)
            r1 = r1 + mm_nn(weight(g_out, 0), att[:half]) + mm_nn(weight(g_out, 1), att[half:])
            h1, xh, inv = norm(r1, vec(4), vec(5))
            R[h1_][...] = h1
            R[xh1[l]][...] = xh
            R[rs1[l]][...] = jnp.broadcast_to(inv, (8, tokens))
            R[hlow[l]][...] = h1.astype(BF16)
            for i in range(4):
                rows = slice(i * chunk, (i + 1) * chunk)
                g = g_up
                f = up_bias(i)
                for h in range(2):
                    w = R[g_up.weight][h, i // 2, i % 2].reshape(chunk, g.cols)
                    f = f + mm_nn(w, R[hlow[l]][h * half : (h + 1) * half, :])
                cdf = 0.5 * (1.0 + lax.erf(f * ROOT_HALF))
                R[act[l]][rows, :] = (f * cdf).astype(BF16)
                R[slope[l]][rows, :] = cdf + f * (jnp.exp(-0.5 * f * f) * DENSITY_SCALE)
            r2 = R[h1_][...] + vec(3)
            for h in range(2):
                r2 = r2 + mm_nn(weight(g_down, h), R[act[l]][h * d_ff // 2 : (h + 1) * d_ff // 2, :])
            out, xh, inv = norm(r2, vec(6), vec(7))
            R[xh2[l]][...] = xh
            R[rs2[l]][...] = jnp.broadcast_to(inv, (8, tokens))
            return out

        def grad_vec(lane, column):
            lanes = lax.broadcasted_iota(jnp.int32, (d_model, 128), 1)
            R[gv][...] += jnp.where(lanes == lane, column, 0.0)

        def add_grad(n, h, value, l):
            shape = n.whole[1:]
            value = value.reshape(shape)
            if l == 0:
                value = value + R[n.grad][h].astype(F32)
            R[n.grad][h] = value.astype(BF16)

        def norm_grad(g, xh, inv, gain, lane):
            grad_vec(lane, jnp.sum(g * xh, axis=1, keepdims=True))
            grad_vec(lane + 1, jnp.sum(g, axis=1, keepdims=True))
            s = g * gain
            return inv * (
                s - jnp.mean(s, axis=0, keepdims=True) - xh * jnp.mean(s * xh, axis=0, keepdims=True)
            )

        def backward(l, g):
            half = d_model // 2
            dr2 = norm_grad(g, R[xh2[l]][...], R[rs2[l]][0:1, :], vec(6), 6)
            dz2 = dr2.astype(BF16)
            grad_vec(3, jnp.sum(dz2.astype(F32), axis=1, keepdims=True))
            for h in range(2):
                add_grad(g_down, h, mm_nt(dz2, R[act[l]][h * d_ff // 2 : (h + 1) * d_ff // 2, :]), l)
            for i in range(4):
                rows = slice(i * chunk, (i + 1) * chunk)
                h, lo = i // 2, (i % 2) * chunk
                w = R[g_down.weight][h].reshape(d_model, d_ff // 2)[:, lo : lo + chunk]
                df = (mm_tn(w, dz2) * R[slope[l]][rows, :]).astype(BF16)
                R[df_][rows, :] = df
                sums = jnp.sum(df.astype(F32), axis=1, keepdims=True).reshape(8, 4, 16, 1)
                for b in range(4):
                    lanes = lax.broadcasted_iota(jnp.int32, (128, 128), 1)
                    place_ = slice(i * 128, (i + 1) * 128)
                    R[gv][place_, :] += jnp.where(lanes == 8 + b, sums[:, b].reshape(128, 1), 0.0)
            dh = []
            for h in range(2):
                hl = R[hlow[l]][h * half : (h + 1) * half, :]
                add_grad(g_up, h, mm_nt(R[df_][...], hl), l)
                dh.append(mm_tn(weight(g_up, h), R[df_][...]))
            dh1 = dr2 + jnp.concatenate(dh, axis=0)
            dr1 = norm_grad(dh1, R[xh1[l]][...], R[rs1[l]][0:1, :], vec(4), 4)
            dz = dr1.astype(BF16)
            R[x32][...] = dr1
            grad_vec(2, jnp.sum(dz.astype(F32), axis=1, keepdims=True))
            for h in range(2):
                datt = mm_tn(weight(g_out, h), dz).astype(BF16)
                R[send1][h * 4 : (h + 1) * 4] = datt.reshape(4, hd, tokens)
            cps = spread(R[send1], R[dr])
            att = R[ar[l]][...].reshape(d_model, tokens)
            for h in range(2):
                add_grad(g_out, h, mm_nt(dz, att[h * half : (h + 1) * half]), l)
            finish(cps)
            qkv_all, datt_all = R[qr[l]], R[dr]
            for b in range(8):
                R[qt][span(b), :] = qkv_all[b, 0:hd, :].T
                R[kt][span(b), :] = qkv_all[b, hd : 2 * hd, :].T
                R[vt][span(b), :] = qkv_all[b, 2 * hd :, :].T
                R[dt][span(b), :] = datt_all[b].T
            R[dk][...] = jnp.zeros((seq_len, hd), F32)
            R[dv][...] = jnp.zeros((seq_len, hd), F32)
            es = R[send3]
            for qb in range(7, -1, -1):
                n = ext(qb)
                keys = span(0, n)
                delta = jnp.sum(datt_all[qb].astype(F32) * R[o32[l]][qb], axis=0, keepdims=True)
                s = masked(mm_nn(R[kt][keys, :], qkv_all[qb, 0:hd, :]) * EXP2_SCALE, qb)
                p = jnp.exp2(s - R[lse[l]][qb, 0:1, :])
                dprob = mm_nn(R[vt][keys, :], datt_all[qb])
                dsc = (p * (dprob - delta)).astype(BF16)
                R[dv][keys, :] += mm_nn(p.astype(BF16), R[dt][span(qb), :])
                R[dk][keys, :] += mm_nn(dsc, R[qt][span(qb), :])
                es[qb, 0:hd, :] = (mm_tn(R[kt][keys, :], dsc) * SCORE_SCALE).astype(BF16)
            for b in range(8):
                es[b, hd : 2 * hd, :] = (R[dk][span(b), :] * SCORE_SCALE).T.astype(BF16)
                es[b, 2 * hd :, :] = R[dv][span(b), :].T.astype(BF16)
            finish(spread(R[send3], R[er]))
            back = R[er]
            grads = [back[:, part * hd : (part + 1) * hd, :].reshape(d_model, tokens) for part in range(3)]
            grad_vec(0, jnp.sum(grads[0].astype(F32), axis=1, keepdims=True))
            grad_vec(1, jnp.sum(grads[2].astype(F32), axis=1, keepdims=True))
            dx = []
            for h in range(2):
                w = weight(g_qkv, h)
                low = R[xlow[l]][h * half : (h + 1) * half, :]
                t = R[x32][h * half : (h + 1) * half, :]
                gw = []
                for part in range(3):
                    rows = slice(part * d_model, (part + 1) * d_model)
                    t = t + mm_tn(w[rows], grads[part])
                    gw.append(mm_nt(grads[part], low))
                add_grad(g_qkv, h, jnp.concatenate(gw, axis=0), l)
                dx.append(t)
            return jnp.concatenate(dx, axis=0)

        first = R[s_in][...].T
        R[xlow[0]][...] = first
        R[x32][...] = first.astype(F32)
        mid = forward(0)
        R[x32][...] = mid
        R[xlow[1]][...] = mid.astype(BF16)
        last = forward(1)
        R[o_send][...] = last.astype(BF16).T

        @pl.when(swapped)
        def _():
            swap(R[o_send], o_out, so_idx).start()
            swap(cot_ref, R[c_in], c_idx).wait()

        @pl.when(jnp.logical_not(swapped))
        def _():
            o_out[...] = R[o_send][...]
            R[c_in][...] = cot_ref[...]

        R[gv][...] = jnp.zeros((d_model, 128), F32)
        g = R[c_in][...].T.astype(F32)
        g = backward(1, g)
        g = backward(0, g)
        R[i_send][...] = g.astype(BF16).T

        @pl.when(swapped)
        def _():
            swap(R[i_send], R[i_recv], si_idx).start()

        @pl.when(jnp.logical_not(swapped))
        def _():
            o_ig[...] = g.T

        R[g_vec.grad][0] = R[gv][...].reshape(g_vec.whole[1:])

        idx = {n: (take(1), take(2), take(2), take(3)) for n in rs_order}

        def rs_c(n):
            r1s, r1r = R[n.send1], R[n.recv1]
            r1s[...] = R[n.grad][:, :, 1 - c].astype(BF16)
            cp = remote(r1s, r1r, idx[n][0], dev(x, 1 - c, z, y))
            cp.start()
            sends.append(cp)
            return [cp]

        def rs_a(n, waits):
            waits[0].wait_recv()
            g_, r1r = R[n.grad], R[n.recv1]
            cps = []
            R[n.send2[0]][...] = (g_[0, 1 - x, c].astype(F32) + r1r[0, 1 - x].astype(F32)).astype(BF16)
            cps.append(remote(R[n.send2[0]], R[n.recv2[0]], idx[n][1], dev(1 - x, c, z, y)))
            cps[-1].start()
            if n.halves == 2:
                R[n.send2[1]][...] = (g_[1, :, c, :, 1 - y].astype(F32) + r1r[1, :, :, 1 - y].astype(F32)).astype(BF16)
                cps.append(remote(R[n.send2[1]], R[n.recv2[1]], idx[n][1] + 1, dev(x, c, z, 1 - y)))
                cps[-1].start()
            sends.extend(cps)
            return cps

        def rs_b(n, waits):
            g_, r1r = R[n.grad], R[n.recv1]
            cps = []
            waits[0].wait_recv()
            r2 = R[n.recv2[0]]
            R[n.send3[0]][...] = (
                g_[0, x, c, :, 1 - y].astype(F32) + r1r[0, x, :, 1 - y].astype(F32) + r2[:, 1 - y].astype(F32)
            ).astype(BF16)
            cps.append(remote(R[n.send3[0]], R[n.recv3[0]], idx[n][2], dev(x, c, z, 1 - y)))
            cps[-1].start()
            if n.halves == 2:
                waits[1].wait_recv()
                r2 = R[n.recv2[1]]
                R[n.send3[1]][...] = (
                    g_[1, 1 - x, c, :, y].astype(F32) + r1r[1, 1 - x, :, y].astype(F32) + r2[1 - x].astype(F32)
                ).astype(BF16)
                cps.append(remote(R[n.send3[1]], R[n.recv3[1]], idx[n][2] + 1, dev(1 - x, c, z, y)))
                cps[-1].start()
            sends.extend(cps)
            return cps

        def rs_z(n, waits):
            g_, r1r, a3 = R[n.grad], R[n.recv1], R[n.sum3]
            for h in range(n.halves):
                waits[h].wait_recv()
                r2 = R[n.recv2[h]]
                kept = r2[:, y] if h == 0 else r2[x]
                a3[:, h] = (
                    g_[h, x, c, :, y].astype(F32)
                    + r1r[h, x, :, y].astype(F32)
                    + kept.astype(F32)
                    + R[n.recv3[h]][...].astype(F32)
                )
            cps = []
            for j in range(1, 4):
                to = (z + j) % 4
                R[n.send4][j - 1] = a3[to].astype(BF16)
                cps.append(
                    remote(R[n.send4].at[j - 1], R[n.recv4].at[j - 1], idx[n][3] + j - 1, dev(x, c, to, y))
                )
                cps[-1].start()
            sends.extend(cps)
            return cps

        def rs_end(n, waits):
            for cp in waits:
                cp.wait_recv()
            total = R[n.sum3][z]
            for j in range(3):
                total = total + R[n.recv4][j].astype(F32)
            return total

        red = {n: rs_c(n) for n in rs_order}
        for step in (rs_a, rs_b, rs_z):
            for n in rs_order:
                red[n] = step(n, red[n])
        for n, ref in ((g_down, o_down), (g_up, o_up), (g_out, o_gout), (g_qkv, o_qkv)):
            t = rs_end(n, red[n])
            ref[...] = jnp.concatenate([t[0], t[1]], axis=1).T
        t = rs_end(g_vec, red[g_vec])[0].T
        o_bias[...] = t[0:4]
        o_norms[...] = t[4:8]
        o_upb[...] = t[8:12]

        @pl.when(swapped)
        def _():
            swap(R[o_send], o_out, so_idx).wait()
            swap(R[i_send], R[i_recv], si_idx).wait()
            o_ig[...] = R[i_recv][...].astype(F32)

        for cp in sends:
            cp.wait_send()

    n_sems = 5 + 5 * 8 + 8 * 8 + 5 * 8

    def kernel(*refs):
        count[0] = 0
        body(refs[:10], refs[10:19], refs[19:-2], refs[-2], refs[-1])
        assert count[0] <= n_sems

    def call(inputs, qkv_w, out_w, up_w, down_w, biases, up_bias, norms, cotangent, prefix):
        shards = (qkv_w, out_w, up_w, down_w, biases, norms)
        results = pl.pallas_call(
            kernel,
            out_shape=(
                jax.ShapeDtypeStruct((tokens, d_model), BF16),
                jax.ShapeDtypeStruct((tokens, d_model), F32),
                *(jax.ShapeDtypeStruct(w.shape, F32) for w in shards[:5]),
                jax.ShapeDtypeStruct((4, 16), F32),
                jax.ShapeDtypeStruct(norms.shape, F32),
            ),
            in_specs=[pl.BlockSpec(memory_space=pltpu.VMEM)] * 9
            + [pl.BlockSpec(memory_space=pltpu.SMEM)],
            out_specs=[pl.BlockSpec(memory_space=pltpu.VMEM)] * 9,
            scratch_shapes=[
                *scratch,
                pltpu.SemaphoreType.DMA((n_sems,)),
                pltpu.SemaphoreType.DMA((n_sems,)),
            ],
            compiler_params=pltpu.CompilerParams(
                collective_id=0, has_side_effects=True, vmem_limit_bytes=62 * 2**20
            ),
        )(inputs, qkv_w, out_w, up_w, down_w, biases, up_bias.reshape(4, 16), norms, cotangent, prefix)
        return (*results[:7], results[7].reshape(up_bias.shape), results[8])

    return call


def fused_fits(mesh, args):
    if tuple(mesh.shape.items()) != (("dp", 4), ("seq", 8)) or HEADS != 8:
        return False
    total, d_model = args[0].shape
    d_ff = args[3].shape[1]
    return total % (32 * 128) == 0 and total // 32 == 256 and d_model == 512 and d_ff == 2048


def solution(mesh):
    specs = dict(
        mesh=mesh,
        in_specs=(
            P(("dp", "seq"), None),
            P(None, ("dp", "seq")),
            P(None, ("dp", "seq")),
            P(None, ("dp", "seq")),
            P(None, ("dp", "seq")),
            P(None, ("dp", "seq")),
            P(("dp", "seq")),
            P(None, ("dp", "seq")),
            P(("dp", "seq"), None),
            P("dp"),
        ),
        out_specs=(
            P(("dp", "seq"), None),
            P(("dp", "seq"), None),
            P(None, ("dp", "seq")),
            P(None, ("dp", "seq")),
            P(None, ("dp", "seq")),
            P(None, ("dp", "seq")),
            P(None, ("dp", "seq")),
            P(("dp", "seq")),
            P(None, ("dp", "seq")),
        ),
        check_vma=False,
    )

    def run(*args):
        if fused_fits(mesh, args):
            d_model = args[0].shape[1]
            step = fused_step(args[0].shape[0] // 32, d_model, args[3].shape[1], HEADS)
            return jax.shard_map(step, **specs)(*args)
        return jax.shard_map(local, **specs)(*args)

    return run
```

```python
import math

import jax
import jax.numpy as jnp
from jax import lax
from jax.experimental import pallas as pl
from jax.experimental.pallas import tpu as pltpu
from jax.sharding import PartitionSpec as P

HEADS = 8


EPSILON = 1e-05
NEGATIVE = -1e30
SCORE_SCALE = 0.125
ROOT_HALF = 1.0 / math.sqrt(2.0)
DENSITY_SCALE = 1.0 / math.sqrt(2.0 * math.pi)


def dot_rows(first_op, second_op):
    return lax.dot_general(
        first_op, second_op, (((1,), (1,)), ((), ())), preferred_element_type=jnp.float32
    )


def dot_cols(first_op, second_op):
    return lax.dot_general(
        first_op, second_op, (((0,), (0,)), ((), ())), preferred_element_type=jnp.float32
    )


def split_heads(tensor_in):
    return tensor_in.reshape(tensor_in.shape[0], HEADS, -1).transpose(1, 0, 2)


def merge_heads(stacked):
    return stacked.transpose(1, 0, 2).reshape(stacked.shape[1], -1)


def cast_all(masters):
    return tuple((tensor.astype(jnp.bfloat16) for tensor in masters))


def fetch_forward(masters):
    casted = cast_all(masters)
    return (
        lax.all_gather(casted[0], ("dp", "seq"), axis=1, tiled=True),
        lax.all_gather(casted[1], ("dp", "seq"), axis=1, tiled=True),
        lax.all_gather(casted[2], ("dp", "seq"), axis=1, tiled=True),
        lax.all_gather(casted[3], ("dp", "seq"), axis=1, tiled=True),
        lax.all_gather(casted[4], ("dp", "seq"), axis=1, tiled=True),
        lax.all_gather(casted[5], ("dp", "seq"), axis=0, tiled=True),
        lax.all_gather(casted[6], ("dp", "seq"), axis=1, tiled=True),
    )


def fetch_backward(masters):
    casted = cast_all(masters)
    return (
        lax.all_gather(casted[0], ("dp", "seq"), axis=1, tiled=True),
        lax.all_gather(casted[1], ("dp", "seq"), axis=1, tiled=True),
        lax.all_gather(casted[2], ("dp", "seq"), axis=1, tiled=True),
        lax.all_gather(casted[3], ("dp", "seq"), axis=1, tiled=True),
        lax.all_gather(casted[4], ("dp", "seq"), axis=1, tiled=True),
        lax.all_gather(casted[5], ("dp", "seq"), axis=0, tiled=True),
        lax.all_gather(casted[6], ("dp", "seq"), axis=1, tiled=True),
    )


def gelu_slope(values):
    normal_cdf = 0.5 * (1.0 + jax.scipy.special.erf(values * ROOT_HALF))
    return normal_cdf + values * jnp.exp(-0.5 * values * values) * DENSITY_SCALE


def layer_norm(values, gain_vec, shift_vec):
    centre = values - jnp.mean(values, axis=1, keepdims=True)
    inv_std = lax.rsqrt(jnp.mean(centre * centre, axis=1, keepdims=True) + EPSILON)
    centred = centre * inv_std
    return (centred * gain_vec + shift_vec, centred, inv_std)


def norm_back(grad_out, centred, inv_std, gain_vec):
    scaled = grad_out * gain_vec
    grad_gain = jnp.sum(grad_out * centred, axis=0)
    grad_shift = jnp.sum(grad_out, axis=0)
    grad_in = inv_std * (
        scaled
        - jnp.mean(scaled, axis=1, keepdims=True)
        - centred * jnp.mean(scaled * centred, axis=1, keepdims=True)
    )
    return (grad_in, grad_gain, grad_shift)


def attend_forward(queries, gathered, visible):
    features = queries.shape[1]
    head_q = split_heads(queries)
    head_k = split_heads(gathered[:, :features])
    head_v = split_heads(gathered[:, features:])

    def one_head(members):
        head_query, head_keys, head_values = members
        scores = jnp.where(visible, dot_rows(head_query, head_keys) * SCORE_SCALE, NEGATIVE)
        largest = jnp.max(scores, axis=1, keepdims=True)
        exponent = jnp.exp(scores - largest)
        row_total = jnp.sum(exponent, axis=1, keepdims=True)
        probability = (exponent / row_total).astype(jnp.bfloat16)
        head_out = jnp.dot(probability, head_values, preferred_element_type=jnp.float32)
        return (head_out, (largest + jnp.log(row_total))[:, 0])

    head_outs, log_totals = lax.map(one_head, (head_q, head_k, head_v))
    return (merge_heads(head_outs), log_totals)


def attend_backward(queries, gathered, visible, grad_att, log_totals):
    features = queries.shape[1]
    head_q = split_heads(queries)
    head_k = split_heads(gathered[:, :features])
    head_v = split_heads(gathered[:, features:])
    head_g = split_heads(grad_att)

    def one_head(members):
        head_query, head_keys, head_values, head_grad, head_logs = members
        scores = jnp.where(visible, dot_rows(head_query, head_keys) * SCORE_SCALE, NEGATIVE)
        probability = jnp.exp(scores - head_logs[:, None])
        grad_prob = dot_rows(head_grad, head_values)
        row_delta = jnp.sum(probability * grad_prob, axis=1)
        grad_score = (probability * (grad_prob - row_delta[:, None])).astype(jnp.bfloat16)
        grad_query = (
            jnp.dot(grad_score, head_keys, preferred_element_type=jnp.float32) * SCORE_SCALE
        )
        grad_keys = dot_cols(grad_score, head_query) * SCORE_SCALE
        grad_values = dot_cols(probability.astype(jnp.bfloat16), head_grad)
        return (grad_query, grad_keys, grad_values)

    results = lax.map(one_head, (head_q, head_k, head_v, head_g, log_totals))
    grad_query = merge_heads(results[0])
    return (grad_query, jnp.concatenate([merge_heads(results[1]), merge_heads(results[2])], axis=1))


def layer_forward(stream, weights, visible):
    w_qkv, w_out, w_up, w_down, vec_bias, b_up, vec_norm = weights
    vec_bias = vec_bias.astype(jnp.float32)
    b_up = b_up.astype(jnp.float32)
    vec_norm = vec_norm.astype(jnp.float32)
    features = stream.shape[1]
    stream_low = stream.astype(jnp.bfloat16)
    bias_row = jnp.concatenate([vec_bias[0], jnp.zeros_like(vec_bias[0]), vec_bias[1]])
    qkv = (jnp.dot(stream_low, w_qkv, preferred_element_type=jnp.float32) + bias_row).astype(
        jnp.bfloat16
    )
    queries = qkv[:, :features]
    local_kv = qkv[:, features:]
    gathered = lax.all_gather(local_kv, "seq", axis=0, tiled=True)
    attended, log_totals = attend_forward(queries, gathered, visible)
    att_low = attended.astype(jnp.bfloat16)
    branch = jnp.dot(att_low, w_out, preferred_element_type=jnp.float32) + vec_bias[2]
    normed, centred_one, inv_std_one = layer_norm(stream + branch, vec_norm[0], vec_norm[1])
    normed_low = normed.astype(jnp.bfloat16)
    hidden = jnp.dot(normed_low, w_up, preferred_element_type=jnp.float32) + b_up
    active = jax.nn.gelu(hidden, approximate=False).astype(jnp.bfloat16)
    second = jnp.dot(active, w_down, preferred_element_type=jnp.float32) + vec_bias[3]
    result, centred_two, inv_std_two = layer_norm(normed + second, vec_norm[2], vec_norm[3])
    cache = (
        stream_low,
        queries,
        local_kv,
        None,
        att_low,
        log_totals,
        centred_one,
        inv_std_one,
        normed_low,
        hidden,
        active,
        centred_two,
        inv_std_two,
    )
    return (result, cache)


def layer_backward(gradient, cache, weights, visible):
    w_qkv, w_out, w_up, w_down, vec_bias, b_up, vec_norm = weights
    vec_norm = vec_norm.astype(jnp.float32)
    (
        stream_low,
        queries,
        local_kv,
        kept_kv,
        att_low,
        log_totals,
        centred_one,
        inv_std_one,
        normed_low,
        hidden,
        active,
        centred_two,
        inv_std_two,
    ) = cache
    features = queries.shape[1]
    gathered = lax.all_gather(local_kv, "seq", axis=0, tiled=True)
    grad_two, gain_two, shift_two = norm_back(gradient, centred_two, inv_std_two, vec_norm[2])
    grad_second = grad_two.astype(jnp.bfloat16)
    bias_down = jnp.sum(grad_second.astype(jnp.float32), axis=0)
    grad_w_down = dot_cols(active, grad_second)
    grad_active = dot_rows(grad_second, w_down)
    grad_hidden = (grad_active * gelu_slope(hidden)).astype(jnp.bfloat16)
    bias_upper = jnp.sum(grad_hidden.astype(jnp.float32), axis=0)
    grad_w_up = dot_cols(normed_low, grad_hidden)
    grad_normed = grad_two + dot_rows(grad_hidden, w_up)
    grad_one, gain_one, shift_one = norm_back(grad_normed, centred_one, inv_std_one, vec_norm[0])
    grad_branch = grad_one.astype(jnp.bfloat16)
    bias_output = jnp.sum(grad_branch.astype(jnp.float32), axis=0)
    grad_w_out = dot_cols(att_low, grad_branch)
    grad_att = dot_rows(grad_branch, w_out).astype(jnp.bfloat16)
    grad_query, kv_terms = attend_backward(queries, gathered, visible, grad_att, log_totals)
    kv_grad = lax.psum_scatter(
        kv_terms.astype(jnp.bfloat16), "seq", scatter_dimension=0, tiled=True
    ).astype(jnp.float32)
    grad_qkv = jnp.concatenate([grad_query, kv_grad], axis=1).astype(jnp.bfloat16)
    qkv_sums = jnp.sum(grad_qkv.astype(jnp.float32), axis=0)
    grad_w_qkv = dot_cols(stream_low, grad_qkv)
    grad_stream = grad_one + dot_rows(grad_qkv, w_qkv)
    grad_bias = jnp.stack([qkv_sums[:features], qkv_sums[2 * features :], bias_output, bias_down])
    grad_norm = jnp.stack([gain_one, shift_one, gain_two, shift_two])
    return (
        grad_stream,
        (grad_w_qkv, grad_w_out, grad_w_up, grad_w_down, grad_bias, bias_upper, grad_norm),
    )


def local(
    inputs,
    qkv_weight,
    out_weight,
    up_weight,
    down_weight,
    biases,
    up_bias,
    norms,
    cotangent,
    prefix,
):
    masters = (qkv_weight, out_weight, up_weight, down_weight, biases, up_bias, norms)
    row_count = inputs.shape[0]
    key_count = row_count * lax.axis_size("seq")
    rows_here = lax.axis_index("seq") * row_count + jnp.arange(row_count, dtype=jnp.int32)
    all_index = jnp.arange(key_count, dtype=jnp.int32)
    visible = (all_index[None, :] <= rows_here[:, None]) | (all_index[None, :] < prefix[0])
    stream = inputs.astype(jnp.float32)
    caches = []
    for position in range(2):
        weights = fetch_forward(masters)
        stream, cache = layer_forward(stream, weights, visible)
        caches.append(cache)
    gradient = cotangent.astype(jnp.float32)
    accumulated = None
    for position in range(2):
        weights = fetch_backward(masters)
        gradient, grad_parts = layer_backward(gradient, caches[1 - position], weights, visible)
        if accumulated is None:
            accumulated = grad_parts
        else:
            accumulated = tuple((prior + fresh for prior, fresh in zip(accumulated, grad_parts)))
    reduced = (
        lax.psum_scatter(accumulated[0], ("dp", "seq"), scatter_dimension=1, tiled=True),
        lax.psum_scatter(accumulated[1], ("dp", "seq"), scatter_dimension=1, tiled=True),
        lax.psum_scatter(accumulated[2], ("dp", "seq"), scatter_dimension=1, tiled=True),
        lax.psum_scatter(accumulated[3], ("dp", "seq"), scatter_dimension=1, tiled=True),
        lax.psum_scatter(accumulated[4], ("dp", "seq"), scatter_dimension=1, tiled=True),
        lax.psum_scatter(accumulated[5], ("dp", "seq"), scatter_dimension=0, tiled=True),
        lax.psum_scatter(accumulated[6], ("dp", "seq"), scatter_dimension=1, tiled=True),
    )
    return (
        stream.astype(jnp.bfloat16),
        gradient,
        reduced[0],
        reduced[1],
        reduced[2],
        reduced[3],
        reduced[4],
        reduced[5],
        reduced[6],
    )


F32 = jnp.float32
BF16 = jnp.bfloat16
MESH = pl.DeviceIdType.MESH
LOG2E = math.log2(math.e)
EXP2_SCALE = SCORE_SCALE * LOG2E


def mm_nn(a, b):
    return lax.dot_general(a, b, (((1,), (0,)), ((), ())), preferred_element_type=F32)


def mm_nt(a, b):
    return lax.dot_general(a, b, (((1,), (1,)), ((), ())), preferred_element_type=F32)


def mm_tn(a, b):
    return lax.dot_general(a, b, (((0,), (0,)), ((), ())), preferred_element_type=F32)


def fused_step(tokens, d_model, d_ff, heads):
    hd = d_model // heads
    seq_len = tokens * 8
    fixed = (seq_len // 2) // tokens
    class Group:
        def __init__(self, rows, cols, x_first, reduced=True):
            halves = len(x_first)
            self.x_first = x_first
            self.rows, self.cols, self.halves = rows, cols, halves
            self.whole = (halves, 2, 2, 4, 2, rows, cols)
            self.weight = vm(self.whole, BF16)
            if not reduced:
                return
            self.grad = vm(self.whole, BF16)
            one = (halves, 2, 4, 2, rows, cols)
            two = [(4, 2, rows, cols) if first else (2, 4, rows, cols) for first in x_first]
            self.recv1 = vm(one, BF16)
            self.send2, self.recv2 = [vm(t, BF16) for t in two], [vm(t, BF16) for t in two]
            three_ = (4, rows, cols)
            self.send3, self.recv3 = [vm(three_, BF16) for t in two], [vm(three_, BF16) for t in two]
            self.sum3 = vm((4, halves, rows, cols), F32)
            self.send4, self.recv4 = vm((3, halves, rows, cols), BF16), vm((3, halves, rows, cols), BF16)

    chunk = d_ff // 4
    three = 3 * hd
    scratch = []
    count = [0]

    def take(number):
        first = count[0]
        count[0] += number
        return first

    def vm(shape, dtype):
        scratch.append(pltpu.VMEM(shape, dtype))
        return len(scratch) - 1

    def per_layer(shape, dtype):
        return [vm(shape, dtype) for _ in range(2)]

    g_qkv = Group(3 * d_model // 32, d_model // 2, (True, True), reduced=False)
    g_out = Group(d_model // 32, d_model // 2, (False, True))
    g_up = Group(d_ff // 32, d_model // 2, (True, False))
    g_down = Group(d_model // 32, d_ff // 2, (True, True))
    g_vec = Group(d_model // 32, 128, (True,))
    everything = (g_qkv, g_vec, g_out, g_up, g_down)
    own_q, head_w = vm((3, 16, d_model), BF16), vm((3, 4, 16, d_model), BF16)
    head_g = vm((three, d_model), F32)
    tile_s, tile_r = vm((3, 4, 16, d_model), BF16), vm((3, 4, 16, d_model), BF16)
    s_all = per_layer((8, tokens, d_model), BF16)
    pack = vm((128, 16), F32)
    c_in = vm((tokens, d_model), BF16)
    p_out, p_in = vm((8, 128), jnp.int32), vm((8, 128), jnp.int32)
    o_send, i_send, i_recv = (vm((tokens, d_model), BF16) for _ in range(3))
    x32, h1_ = vm((d_model, tokens), F32), vm((d_model, tokens), F32)
    hlow = per_layer((d_model, tokens), BF16)
    xh1, xh2 = per_layer((d_model, tokens), F32), per_layer((d_model, tokens), F32)
    rs1, rs2 = per_layer((8, tokens), F32), per_layer((8, tokens), F32)
    slope, act = per_layer((d_ff, tokens), F32), per_layer((d_ff, tokens), BF16)
    lse, o32 = per_layer((8, 8, tokens), F32), per_layer((8, hd, tokens), F32)
    send1, send3 = vm((8, hd, tokens), BF16), vm((8, three, tokens), BF16)
    qr, ar = per_layer((8, three, tokens), BF16), per_layer((8, hd, tokens), BF16)
    dr, er = per_layer((8, hd, tokens), BF16), per_layer((8, three, tokens), BF16)
    g32, dh32 = vm((d_model, tokens), F32), vm((d_model, tokens), F32)
    dz_, dz2_ = vm((d_model, tokens), BF16), vm((d_model, tokens), BF16)
    kt, vt, qt, dt = (vm((seq_len, hd), BF16) for _ in range(4))
    dk, dv = vm((seq_len, hd), F32), vm((seq_len, hd), F32)
    df_ = vm((d_ff, tokens), BF16)
    gv = vm((d_model, 128), F32)

    def body(ins, outs, R, SS, RS):
        (in_ref, wqkv, wout, wup, wdown, biases, upb, norms, cot_ref, pref_ref) = ins
        (o_out, o_ig, o_qkv, o_gout, o_up, o_down, o_bias, o_upb, o_norms) = outs
        dp, sq = lax.axis_index("dp"), lax.axis_index("seq")
        x, c = dp // 2, dp % 2
        z, y = sq // 2, sq % 2
        zh, zl = z // 2, z % 2
        rank = 4 * c + 2 * zl + y

        def dev(x_, c_, z_, y_):
            return (x_ * 2 + c_, z_ * 2 + y_)

        def remote(src, dst, idx, device, arrival=None):
            return pltpu.make_async_remote_copy(
                src_ref=src,
                dst_ref=dst,
                send_sem=SS.at[idx],
                recv_sem=RS.at[idx if arrival is None else arrival],
                device_id=device,
                device_id_type=MESH,
            )

        def peer(k):
            c_ = (c + k // 4) % 2
            zl_ = (zl + (k // 2) % 2) % 2
            y_ = (y + k % 2) % 2
            return dev(x, c_, 2 * zh + zl_, y_), 4 * c_ + 2 * zl_ + y_

        sends = []

        barrier = pltpu.get_barrier_semaphore()
        swap_dev = dev(x, 1 - c, 2 * (1 - zh) + zl, y)
        me = dp * 8 + sq

        def greet(i, carry):
            other = (me + i) % 32
            pl.semaphore_signal(barrier, inc=1, device_id=(other // 8, other % 8), device_id_type=MESH)
            return carry

        lax.fori_loop(1, 32, greet, 0)

        def place(n, value):
            for h in range(n.halves):
                R[n.weight][h, x, c, z, y] = value[:, h * n.cols : (h + 1) * n.cols]

        R[own_q][...] = wqkv[...].astype(BF16).reshape(3, 16, d_model)
        place(g_qkv, wqkv[...].astype(BF16))
        R[pack][0:4, :] = biases[...]
        R[pack][4:8, :] = norms[...]
        for b in range(4):
            R[pack][8 + b : 9 + b, :] = upb[:, 16 * b : 16 * (b + 1)]
        R[pack][12:128, :] = jnp.zeros((116, 16), F32)
        place(g_vec, R[pack][...].T.astype(BF16))
        R[p_out][...] = jnp.full((8, 128), pref_ref[0], jnp.int32)
        place(g_out, wout[...].astype(BF16))
        place(g_up, wup[...].astype(BF16))
        place(g_down, wdown[...].astype(BF16))
        pl.semaphore_wait(barrier, 31)

        swapped = c != zh

        def swap(src, dst, idx):
            return remote(src, dst, idx, swap_dev)

        s_idx, c_idx, p_idx, so_idx, si_idx = (take(1) for _ in range(5))

        w_base, t_base = take(12), take(12)

        def head_of(i, block):
            t = 3 * me + i
            h = (t % 32) // 4
            device = dev(block // 2, h // 4, 2 * (block % 2) + (h // 2) % 2, h % 2)
            return t, device, (h == rank) & (block == 2 * x + zh)

        def owner_of(n):
            t = (n // 4) * 32 + 4 * rank + n % 4
            return t // 3, t % 3

        def weight_copy(n):
            i, block = n // 4, n % 4
            t, device, here = head_of(i, block)
            part, sub = t // 32, t % 4
            dst = R[head_w].at[part, sub]
            return remote(R[own_q].at[i], dst, w_base + n, device, w_base + 4 * part + sub), here, (i, part, sub)

        def weight_send(n, carry):
            copy, here, (i, part, sub) = weight_copy(n)

            @pl.when(jnp.logical_not(here))
            def _():
                copy.start()

            @pl.when(here)
            def _():
                R[head_w][part, sub] = R[own_q][i]

            return carry

        def weight_wait(n, carry):
            copy, here, _ = weight_copy(n)

            @pl.when(jnp.logical_not(here))
            def _():
                copy.wait_send()

            owner, _ = owner_of(n)

            @pl.when(owner != me)
            def _():
                remote(R[own_q].at[0], R[head_w].at[n // 4, n % 4], w_base + n, swap_dev).wait_recv()

            return carry

        def tile_copy(n):
            owner, i = owner_of(n)
            block = 2 * x + zh
            src, dst = R[tile_s].at[n // 4, n % 4], R[tile_r].at[i, block]
            device = (owner // 8, owner % 8)
            return remote(src, dst, t_base + n, device, t_base + 4 * i + block), owner == me, (i, block)

        def tile_send(n, carry):
            copy, here, (i, block) = tile_copy(n)

            @pl.when(jnp.logical_not(here))
            def _():
                copy.start()

            @pl.when(here)
            def _():
                R[tile_r][i, block] = R[tile_s][n // 4, n % 4]

            return carry

        def tile_wait(n, carry):
            copy, here, _ = tile_copy(n)

            @pl.when(jnp.logical_not(here))
            def _():
                copy.wait_send()

            _, _, from_us = head_of(n // 4, n % 4)

            @pl.when(jnp.logical_not(from_us))
            def _():
                remote(R[tile_s].at[0, 0], R[tile_r].at[n // 4, n % 4], t_base + n, swap_dev).wait_recv()

            return carry

        s_base = [take(9), take(9)]

        def rank_of(c_, zl_, y_):
            return 4 * c_ + 2 * zl_ + y_

        x_dev = dev(1 - x, c, z, y)
        y_dev, z_dev, c_dev = dev(x, c, z, 1 - y), dev(x, c, 2 * zh + 1 - zl, y), dev(x, 1 - c, z, y)
        top, low_rows = slice(0, tokens // 2), slice(tokens // 2, tokens)

        def s_copy(l, i):
            py, pz, pd = rank_of(c, zl, 1 - y), rank_of(c, 1 - zl, y), rank_of(c, 1 - zl, 1 - y)
            r = R[s_all[l]]
            ref, device = (
                (r.at[rank], y_dev),
                (r.at[rank], z_dev),
                (r.at[rank], c_dev),
                (r.at[py, top], z_dev),
                (r.at[pz, low_rows], y_dev),
                (r.at[py], c_dev),
                (r.at[pz], c_dev),
                (r.at[pd, top], c_dev),
                (r.at[pd, low_rows], c_dev),
            )[i]
            return remote(ref, ref, s_base[l] + i, device)

        def s_start(l, *which):
            for i in which:
                s_copy(l, i).start()

        def s_got(l, *which):
            for i in which:
                s_copy(l, i).wait_recv()

        own_rank = R[s_all[0]].at[rank]
        swap_rank = R[s_all[0]].at[rank_of(1 - c, zl, y)]
        lax.fori_loop(0, 12, weight_send, 0)

        @pl.when(swapped)
        def _():
            swap(in_ref, swap_rank, s_idx).start()
            swap(R[p_out], R[p_in], p_idx).start()

        @pl.when(jnp.logical_not(swapped))
        def _():
            own_rank[...] = in_ref[...]
            R[p_in][...] = R[p_out][...]

        ag = {}
        for n in everything:
            ag[n] = (take(3), take(2), take(2), take(1))

        def ag_z(n, _):
            w = R[n.weight]
            cps = []
            for j in range(1, 4):
                own = w.at[:, x, c, z, y]
                cps.append(remote(own, own, ag[n][0] + j - 1, dev(x, c, (z + j) % 4, y)))
            for cp in cps:
                cp.start()
            sends.extend(cps)
            return cps

        def ag_a(n, waits):
            for cp in waits:
                cp.wait_recv()
            w = R[n.weight]
            cps = []
            part = w.at[0, x, c, :, y]
            cps.append(remote(part, part, ag[n][1], dev(x, c, z, 1 - y)))
            if n.halves == 2:
                part = w.at[1, x, c, :, y]
                cps.append(remote(part, part, ag[n][1] + 1, dev(1 - x, c, z, y)))
            for cp in cps:
                cp.start()
            sends.extend(cps)
            return cps

        def ag_b(n, waits):
            w = R[n.weight]
            cps = []
            waits[0].wait_recv()
            part = w.at[0, x, c]
            cps.append(remote(part, part, ag[n][2], dev(1 - x, c, z, y)))
            cps[-1].start()
            if n.halves == 2:
                waits[1].wait_recv()
                part = w.at[1, :, c, :, y]
                cps.append(remote(part, part, ag[n][2] + 1, dev(x, c, z, 1 - y)))
                cps[-1].start()
            sends.extend(cps)
            return cps

        def ag_c(n, waits):
            for cp in waits:
                cp.wait_recv()
            part = R[n.weight].at[:, :, c]
            cp = remote(part, part, ag[n][3], dev(x, 1 - c, z, y))
            cp.start()
            sends.append(cp)
            return [cp]

        state = {}

        def step(stage, n):
            state[n] = stage(n, state.get(n))

        def arrived(n):
            for cp in state[n]:
                cp.wait_recv()

        step(ag_z, g_vec)

        @pl.when(swapped)
        def _():
            swap(in_ref, swap_rank, s_idx).wait()
            swap(R[p_out], R[p_in], p_idx).wait()

        s_start(0, 0, 1, 2)
        step(ag_a, g_vec)
        step(ag_z, g_up)
        step(ag_z, g_out)
        s_got(0, 0)
        s_start(0, 3, 5)
        s_got(0, 1)
        s_start(0, 4, 6)
        step(ag_b, g_vec)
        step(ag_z, g_down)
        s_got(0, 3)
        s_start(0, 7)
        s_got(0, 4)
        s_start(0, 8)
        step(ag_c, g_vec)
        step(ag_a, g_up)
        R[x32][...] = own_rank[...].T.astype(F32)
        s_got(0, 2, 5, 6, 7, 8)
        lax.fori_loop(0, 12, weight_wait, 0)
        arrived(g_vec)

        def weight(n, h):
            return R[n.weight][h].reshape(32 * n.rows, n.cols)

        def vec(i):
            return R[g_vec.weight][0, :, :, :, :, :, i : i + 1].reshape(d_model, 1).astype(F32)

        def up_bias(i):
            lanes = [
                R[g_vec.weight][0, i // 2, i % 2, :, :, :, 8 + b : 9 + b].reshape(8, 1, 16, 1).astype(F32)
                for b in range(4)
            ]
            return jnp.concatenate(lanes, axis=1).reshape(chunk, 1)

        def spread(src, dst):
            base = take(8)
            cps = []
            for k in range(1, 8):
                device, other = peer(k)
                cps.append(remote(src.at[other], dst.at[rank], base + k, device))
                cps[-1].start()
            dst[rank] = src[rank]
            return cps

        def batch(src, dst, base, core):
            def go(ks):
                for k in ks:
                    device, other = peer(k)
                    remote(src.at[other], dst.at[rank], base + k, device).start()

            @pl.when(c == core)
            def _():
                go(range(1, 4))
                dst[rank] = src[rank]

            @pl.when(c != core)
            def _():
                go(range(4, 8))

        def sent(src, dst, base):
            for k in range(1, 8):
                remote(src.at[0], dst.at[0], base + k, peer(k)[0]).wait()

        def finish(cps):
            for cp in cps:
                cp.wait()

        def ext(qb):
            return max(fixed, qb + 1)

        def span(first, last=None):
            return slice(first * tokens, (first + 1 if last is None else last) * tokens)

        def masked(s, qb):
            if qb < fixed:
                kk = lax.broadcasted_iota(jnp.int32, s.shape, 0)
                qq = qb * tokens + lax.broadcasted_iota(jnp.int32, s.shape, 1)
                return jnp.where((kk <= qq) | (kk < R[p_in][0:1, 0:1]), s, NEGATIVE)
            low = s[qb * tokens :]
            kk = lax.broadcasted_iota(jnp.int32, low.shape, 0)
            qq = lax.broadcasted_iota(jnp.int32, low.shape, 1)
            low = jnp.where(kk <= qq, low, NEGATIVE)
            return jnp.concatenate([s[: qb * tokens], low], axis=0)

        def norm(r, gain, shift):
            centre = r - jnp.mean(r, axis=0, keepdims=True)
            inv = lax.rsqrt(jnp.mean(centre * centre, axis=0, keepdims=True) + EPSILON)
            xh = centre * inv
            return xh * gain + shift, xh, inv

        def forward(l):
            rows_all, qkv_all = R[s_all[l]], R[qr[l]]
            if l == 1:
                s_start(1, 0, 1, 2)
                step(ag_a, g_qkv)
                s_got(1, 0)
                s_start(1, 3, 5)
                s_got(1, 1)
                s_start(1, 4, 6)
                s_got(1, 3)
                s_start(1, 7)
                s_got(1, 4)
                s_start(1, 8)
                s_got(1, 2, 5, 6, 7, 8)
            packed = R[g_vec.weight][0, rank // 4, (rank // 2) % 2, pl.ds(2 * (rank % 2), 2)]
            packed = packed.reshape(hd, 128).astype(F32)
            bias = jnp.concatenate([packed[:, 0:1], jnp.zeros((hd, 1), F32), packed[:, 1:2]], axis=0)
            w = R[head_w][...].reshape(three, d_model)
            for b in range(8):
                qkv_all[b] = (mm_nt(w, rows_all[b]) + bias).astype(BF16)
            for b in range(8):
                R[kt][span(b), :] = qkv_all[b, hd : 2 * hd, :].T
                R[vt][span(b), :] = qkv_all[b, 2 * hd :, :].T
            base = take(8)
            for qb in range(8):
                n = ext(qb)
                s = masked(mm_nn(R[kt][span(0, n), :], qkv_all[qb, 0:hd, :]) * EXP2_SCALE, qb)
                m = jnp.max(s, axis=0, keepdims=True)
                p = jnp.exp2(s - m)
                total = jnp.sum(p, axis=0, keepdims=True)
                o = mm_tn(p.astype(BF16), R[vt][span(0, n), :]).T / total
                R[o32[l]][qb] = o
                R[send1][qb] = o.astype(BF16)
                R[lse[l]][qb] = jnp.broadcast_to(m + jnp.log2(total), (8, tokens))
                if qb == 3:
                    batch(R[send1], R[ar[l]], base, 0)
                if l == 0 and qb == 1:
                    step(ag_a, g_out)
                if l == 0 and qb == 4:
                    step(ag_a, g_down)
                    step(ag_b, g_up)
                if l == 0 and qb == 6:
                    step(ag_b, g_out)
            batch(R[send1], R[ar[l]], base, 1)
            if l == 0:
                step(ag_b, g_down)
                step(ag_c, g_up)
                step(ag_c, g_out)
            if l == 1:
                step(ag_b, g_qkv)
            sent(R[send1], R[ar[l]], base)
            if l == 0:
                arrived(g_out)
            att = R[ar[l]][...].reshape(d_model, tokens)
            half = d_model // 2
            r1 = R[x32][...] + vec(2)
            r1 = r1 + mm_nn(weight(g_out, 0), att[:half]) + mm_nn(weight(g_out, 1), att[half:])
            h1, xh, inv = norm(r1, vec(4), vec(5))
            R[h1_][...] = h1
            R[xh1[l]][...] = xh
            R[rs1[l]][...] = jnp.broadcast_to(inv, (8, tokens))
            R[hlow[l]][...] = h1.astype(BF16)
            if l == 0:
                step(ag_c, g_down)
                arrived(g_up)
            for i in range(4):
                rows = slice(i * chunk, (i + 1) * chunk)
                g = g_up
                f = up_bias(i)
                for h in range(2):
                    w = R[g_up.weight][h, i // 2, i % 2].reshape(chunk, g.cols)
                    f = f + mm_nn(w, R[hlow[l]][h * half : (h + 1) * half, :])
                cdf = 0.5 * (1.0 + lax.erf(f * ROOT_HALF))
                R[act[l]][rows, :] = (f * cdf).astype(BF16)
                R[slope[l]][rows, :] = cdf + f * (jnp.exp(-0.5 * f * f) * DENSITY_SCALE)
            if l == 0:
                arrived(g_down)
            r2 = R[h1_][...] + vec(3)
            for h in range(2):
                r2 = r2 + mm_nn(weight(g_down, h), R[act[l]][h * d_ff // 2 : (h + 1) * d_ff // 2, :])
            out, xh, inv = norm(r2, vec(6), vec(7))
            R[xh2[l]][...] = xh
            R[rs2[l]][...] = jnp.broadcast_to(inv, (8, tokens))
            return out

        idx = {n: (take(1), take(2), take(2), take(3)) for n in everything[1:]}

        def rs_c(n, _):
            cp = remote(R[n.grad].at[:, :, 1 - c], R[n.recv1], idx[n][0], dev(x, 1 - c, z, y))
            cp.start()
            sends.append(cp)
            return [cp]

        def rs_a(n, waits):
            waits[0].wait_recv()
            g_, r1 = R[n.grad], R[n.recv1]
            cps = []
            for h in range(n.halves):
                if n.x_first[h]:
                    value, device = g_[h, 1 - x, c].astype(F32) + r1[h, 1 - x].astype(F32), x_dev
                else:
                    value, device = g_[h, :, c, :, 1 - y].astype(F32) + r1[h, :, :, 1 - y].astype(F32), y_dev
                R[n.send2[h]][...] = value.astype(BF16)
                cps.append(remote(R[n.send2[h]], R[n.recv2[h]], idx[n][1] + h, device))
                cps[-1].start()
            sends.extend(cps)
            return cps

        def rs_b(n, waits):
            g_, r1 = R[n.grad], R[n.recv1]
            cps = []
            for h in range(n.halves):
                waits[h].wait_recv()
                r2 = R[n.recv2[h]]
                if n.x_first[h]:
                    value, device = g_[h, x, c, :, 1 - y].astype(F32) + r1[h, x, :, 1 - y].astype(F32), y_dev
                    value = value + r2[:, 1 - y].astype(F32)
                else:
                    value, device = g_[h, 1 - x, c, :, y].astype(F32) + r1[h, 1 - x, :, y].astype(F32), x_dev
                    value = value + r2[1 - x].astype(F32)
                R[n.send3[h]][...] = value.astype(BF16)
                cps.append(remote(R[n.send3[h]], R[n.recv3[h]], idx[n][2] + h, device))
                cps[-1].start()
            sends.extend(cps)
            return cps

        def rs_z(n, waits):
            g_, r1, sum3 = R[n.grad], R[n.recv1], R[n.sum3]
            for h in range(n.halves):
                waits[h].wait_recv()
                r2 = R[n.recv2[h]]
                kept = r2[:, y] if n.x_first[h] else r2[x]
                sum3[:, h] = (
                    g_[h, x, c, :, y].astype(F32)
                    + r1[h, x, :, y].astype(F32)
                    + kept.astype(F32)
                    + R[n.recv3[h]][...].astype(F32)
                )
            cps = []
            for j in range(1, 4):
                to = (z + j) % 4
                R[n.send4][j - 1] = sum3[to].astype(BF16)
                cps.append(
                    remote(R[n.send4].at[j - 1], R[n.recv4].at[j - 1], idx[n][3] + j - 1, dev(x, c, to, y))
                )
                cps[-1].start()
            sends.extend(cps)
            return cps

        def rs_end(n, waits):
            for cp in waits:
                cp.wait_recv()
            total = R[n.sum3][z]
            for j in range(3):
                total = total + R[n.recv4][j].astype(F32)
            return total

        def pick(lane, count_=1):
            rows = lax.broadcasted_iota(jnp.int32, (128, tokens), 0)
            return jnp.where((rows >= lane) & (rows < lane + count_), 1.0, 0.0).astype(BF16)

        def low_sum(lane, value):
            return mm_nt(value, pick(lane))

        def full_sum(lane, value):
            high = value.astype(BF16)
            return low_sum(lane, high) + low_sum(lane, (value - high.astype(F32)).astype(BF16))

        def add_grad(n, h, value, l):
            value = value.reshape(n.whole[1:])
            if l == 0:
                value = value + R[n.grad][h].astype(F32)
            R[n.grad][h] = value.astype(BF16)

        def norm_grad(g, xh, inv, gain):
            s = g * gain
            return inv * (
                s - jnp.mean(s, axis=0, keepdims=True) - xh * jnp.mean(s * xh, axis=0, keepdims=True)
            )

        half = d_model // 2

        def out_grad(l):
            att = R[ar[l]][...].reshape(d_model, tokens)
            for h in range(2):
                add_grad(g_out, h, mm_nt(R[dz_][...], att[h * half : (h + 1) * half]), l)

        def up_grad(l):
            for h in range(2):
                add_grad(g_up, h, mm_nt(R[df_][...], R[hlow[l]][h * half : (h + 1) * half, :]), l)

        def down_grad(l):
            for h in range(2):
                add_grad(g_down, h, mm_nt(R[dz2_][...], R[act[l]][h * d_ff // 2 : (h + 1) * d_ff // 2, :]), l)

        def head_grad(l):
            rows_all, back = R[s_all[l]], R[send3]
            t = mm_nn(back[0], rows_all[0])
            sums = low_sum(0, back[0, 0:hd]) + low_sum(1, back[0, 2 * hd :])
            for b in range(1, 8):
                t = t + mm_nn(back[b], rows_all[b])
                sums = sums + low_sum(0, back[b, 0:hd]) + low_sum(1, back[b, 2 * hd :])
            R[gv][pl.ds(pl.multiple_of(rank * hd, hd), hd), :] += sums
            if l == 1:
                R[head_g][...] = t
            else:
                R[tile_s][...] = (R[head_g][...] + t).astype(BF16).reshape(3, 4, 16, d_model)

        def dense_sums(l):
            t = full_sum(6, R[g32][...] * R[xh2[l]][...]) + full_sum(7, R[g32][...])
            t = t + full_sum(4, R[dh32][...] * R[xh1[l]][...]) + full_sum(5, R[dh32][...])
            t = t + low_sum(3, R[dz2_][...]) + low_sum(2, R[dz_][...])
            R[gv][...] += t
            ones = pick(8, 4)
            lanes = lax.broadcasted_iota(jnp.int32, (8, 16, 128), 2)
            for i in range(4):
                sums = mm_nt(R[df_][i * chunk : (i + 1) * chunk, :], ones).reshape(8, 4, 16, 128)
                t = jnp.where(lanes == 8, sums[:, 0], 0.0)
                for b in range(1, 4):
                    t = jnp.where(lanes == 8 + b, sums[:, b], t)
                R[gv][i * 128 : (i + 1) * 128, :] += t.reshape(128, 128)

        def backward(l):
            dr2 = norm_grad(R[g32][...], R[xh2[l]][...], R[rs2[l]][0:1, :], vec(6))
            R[dz2_][...] = dr2.astype(BF16)
            R[x32][...] = dr2
            for i in range(4):
                rows = slice(i * chunk, (i + 1) * chunk)
                h, lo = i // 2, (i % 2) * chunk
                w = R[g_down.weight][h].reshape(d_model, d_ff // 2)[:, lo : lo + chunk]
                R[df_][rows, :] = (mm_tn(w, R[dz2_][...]) * R[slope[l]][rows, :]).astype(BF16)
            for h in range(2):
                rows = slice(h * half, (h + 1) * half)
                R[dh32][rows, :] = R[x32][rows, :] + mm_tn(weight(g_up, h), R[df_][...])
            dr1 = norm_grad(R[dh32][...], R[xh1[l]][...], R[rs1[l]][0:1, :], vec(4))
            R[dz_][...] = dr1.astype(BF16)
            R[x32][...] = dr1
            for h in range(2):
                datt = mm_tn(weight(g_out, h), R[dz_][...]).astype(BF16)
                R[send1][h * 4 : (h + 1) * 4] = datt.reshape(4, hd, tokens)
            cps = spread(R[send1], R[dr[l]])
            down_grad(l)
            if l == 0:
                step(rs_c, g_down)
            up_grad(l)
            if l == 0:
                step(rs_c, g_up)
            out_grad(l)
            if l == 0:
                step(rs_c, g_out)
            dense_sums(l)
            if l == 0:
                step(rs_a, g_down)
                step(rs_a, g_up)
            finish(cps)
            qkv_all, datt_all = R[qr[l]], R[dr[l]]
            for b in range(8):
                R[qt][span(b), :] = qkv_all[b, 0:hd, :].T
                R[kt][span(b), :] = qkv_all[b, hd : 2 * hd, :].T
                R[vt][span(b), :] = qkv_all[b, 2 * hd :, :].T
                R[dt][span(b), :] = datt_all[b].T
            R[dk][...] = jnp.zeros((seq_len, hd), F32)
            R[dv][...] = jnp.zeros((seq_len, hd), F32)
            base = take(8)
            src, dst = R[send3], R[er[l]]

            def keys_out(b):
                src[b, hd : 2 * hd, :] = (R[dk][span(b), :] * SCORE_SCALE).T.astype(BF16)
                src[b, 2 * hd :, :] = R[dv][span(b), :].T.astype(BF16)

            for qb in range(7, -1, -1):
                n = ext(qb)
                keys = span(0, n)
                delta = jnp.sum(datt_all[qb].astype(F32) * R[o32[l]][qb], axis=0, keepdims=True)
                s = masked(mm_nn(R[kt][keys, :], qkv_all[qb, 0:hd, :]) * EXP2_SCALE, qb)
                p = jnp.exp2(s - R[lse[l]][qb, 0:1, :])
                dprob = mm_nn(R[vt][keys, :], datt_all[qb])
                dsc = (p * (dprob - delta)).astype(BF16)
                R[dv][keys, :] += mm_nn(p.astype(BF16), R[dt][span(qb), :])
                R[dk][keys, :] += mm_nn(dsc, R[qt][span(qb), :])
                src[qb, 0:hd, :] = (mm_tn(R[kt][keys, :], dsc) * SCORE_SCALE).astype(BF16)
                if qb == 4:
                    for b in range(4, 8):
                        keys_out(b)
                    batch(src, dst, base, 1)
            for b in range(4):
                keys_out(b)
            batch(src, dst, base, 0)
            head_grad(l)
            if l == 0:
                lax.fori_loop(0, 12, tile_send, 0)
                step(rs_a, g_out)
                R[g_vec.grad][0] = R[gv][...].astype(BF16).reshape(g_vec.whole[1:])
                step(rs_c, g_vec)
                step(rs_b, g_down)
            else:
                arrived(g_qkv)
            sent(src, dst, base)
            back = R[er[l]]
            for h in range(2):
                w = weight(g_qkv, h)
                t = R[x32][h * half : (h + 1) * half, :]
                for part in range(3):
                    grad = back[:, part * hd : (part + 1) * hd, :].reshape(d_model, tokens)
                    t = t + mm_tn(w[part * d_model : (part + 1) * d_model], grad)
                R[g32][h * half : (h + 1) * half, :] = t

        mid = forward(0)
        step(ag_z, g_qkv)

        @pl.when(swapped)
        def _():
            swap(cot_ref, R[c_in], c_idx).start()

        R[x32][...] = mid
        R[s_all[1]][rank] = mid.astype(BF16).T
        last = forward(1)
        step(ag_c, g_qkv)
        R[o_send][...] = last.astype(BF16).T

        @pl.when(swapped)
        def _():
            swap(R[o_send], o_out, so_idx).start()
            swap(cot_ref, R[c_in], c_idx).wait()

        @pl.when(jnp.logical_not(swapped))
        def _():
            o_out[...] = R[o_send][...]
            R[c_in][...] = cot_ref[...]

        R[gv][...] = jnp.zeros((d_model, 128), F32)
        R[g32][...] = R[c_in][...].T.astype(F32)
        backward(1)
        backward(0)
        R[i_send][...] = R[g32][...].astype(BF16).T

        @pl.when(swapped)
        def _():
            swap(R[i_send], R[i_recv], si_idx).start()

        @pl.when(jnp.logical_not(swapped))
        def _():
            o_ig[...] = R[g32][...].T

        step(rs_a, g_vec)
        step(rs_b, g_up)
        step(rs_z, g_down)
        step(rs_b, g_vec)
        step(rs_b, g_out)
        step(rs_z, g_vec)
        step(rs_z, g_up)
        step(rs_z, g_out)
        lax.fori_loop(0, 12, tile_wait, 0)
        t = R[tile_r][:, 0].astype(F32)
        for block in range(1, 4):
            t = t + R[tile_r][:, block].astype(F32)
        o_qkv[...] = t.reshape(48, d_model)
        for n, ref in ((g_down, o_down), (g_up, o_up), (g_out, o_gout)):
            t = rs_end(n, state[n])
            ref[...] = jnp.concatenate([t[0], t[1]], axis=1)
        t = rs_end(g_vec, state[g_vec])[0].T
        o_bias[...] = t[0:4]
        o_norms[...] = t[4:8]
        o_upb[...] = jnp.concatenate([t[8 + b : 9 + b] for b in range(4)], axis=1)

        @pl.when(swapped)
        def _():
            swap(R[o_send], o_out, so_idx).wait()
            swap(R[i_send], R[i_recv], si_idx).wait()
            o_ig[...] = R[i_recv][...].astype(F32)

        for cp in sends:
            cp.wait_send()
        for l in range(2):
            for i in range(9):
                s_copy(l, i).wait_send()

    n_sems = 5 + 2 * 12 + 2 * 9 + 5 * 8 + 6 * 8 + 4 * 8

    def kernel(*refs):
        count[0] = 0
        body(refs[:10], refs[10:19], refs[19:-2], refs[-2], refs[-1])
        assert count[0] <= n_sems

    def hand_on(*refs):
        for src, dst in zip(refs[:9], refs[9:]):
            dst[...] = src[...]

    def call(inputs, qkv_w, out_w, up_w, down_w, biases, up_bias, norms, cotangent, prefix):
        weights = [w.T for w in (qkv_w, out_w, up_w, down_w)]
        small = [biases, up_bias.reshape(1, -1), norms]
        out_shape = (
            jax.ShapeDtypeStruct((tokens, d_model), BF16),
            jax.ShapeDtypeStruct((tokens, d_model), F32),
            *(jax.ShapeDtypeStruct(w.shape, F32) for w in weights + small),
        )
        vmem = pl.BlockSpec(memory_space=pltpu.VMEM)
        results = pl.pallas_call(
            kernel,
            out_shape=out_shape,
            in_specs=[vmem] * 9 + [pl.BlockSpec(memory_space=pltpu.SMEM)],
            out_specs=[vmem] * 9,
            scratch_shapes=[
                *scratch,
                pltpu.SemaphoreType.DMA((n_sems,)),
                pltpu.SemaphoreType.DMA((n_sems,)),
            ],
            compiler_params=pltpu.CompilerParams(
                collective_id=0, has_side_effects=True, vmem_limit_bytes=62 * 2**20
            ),
        )(inputs, *weights, *small, cotangent, prefix)
        results = pl.pallas_call(
            hand_on, out_shape=out_shape, in_specs=[vmem] * 9, out_specs=[vmem] * 9
        )(*results)
        back = [w.T for w in results[2:6]]
        return (*results[:2], *back, results[6], results[7].reshape(up_bias.shape), results[8])

    return call


def fused_fits(mesh, args):
    if tuple(mesh.shape.items()) != (("dp", 4), ("seq", 8)) or HEADS != 8:
        return False
    total, d_model = args[0].shape
    d_ff = args[3].shape[1]
    return total % (32 * 128) == 0 and total // 32 == 256 and d_model == 512 and d_ff == 2048


def solution(mesh):
    specs = dict(
        mesh=mesh,
        in_specs=(
            P(("dp", "seq"), None),
            P(None, ("dp", "seq")),
            P(None, ("dp", "seq")),
            P(None, ("dp", "seq")),
            P(None, ("dp", "seq")),
            P(None, ("dp", "seq")),
            P(("dp", "seq")),
            P(None, ("dp", "seq")),
            P(("dp", "seq"), None),
            P("dp"),
        ),
        out_specs=(
            P(("dp", "seq"), None),
            P(("dp", "seq"), None),
            P(None, ("dp", "seq")),
            P(None, ("dp", "seq")),
            P(None, ("dp", "seq")),
            P(None, ("dp", "seq")),
            P(None, ("dp", "seq")),
            P(("dp", "seq")),
            P(None, ("dp", "seq")),
        ),
        check_vma=False,
    )

    def run(*args):
        if fused_fits(mesh, args):
            d_model = args[0].shape[1]
            step = fused_step(args[0].shape[0] // 32, d_model, args[3].shape[1], HEADS)
            return jax.shard_map(step, **specs)(*args)
        return jax.shard_map(local, **specs)(*args)

    return run
```

```python
import math

import jax
import jax.numpy as jnp
from jax import lax
from jax.experimental import pallas as pl
from jax.experimental.pallas import tpu as pltpu
from jax.sharding import PartitionSpec as P

HEADS = 8


EPSILON = 1e-05
NEGATIVE = -1e30
SCORE_SCALE = 0.125
ROOT_HALF = 1.0 / math.sqrt(2.0)
DENSITY_SCALE = 1.0 / math.sqrt(2.0 * math.pi)


def dot_rows(first_op, second_op):
    return lax.dot_general(
        first_op, second_op, (((1,), (1,)), ((), ())), preferred_element_type=jnp.float32
    )


def dot_cols(first_op, second_op):
    return lax.dot_general(
        first_op, second_op, (((0,), (0,)), ((), ())), preferred_element_type=jnp.float32
    )


def split_heads(tensor_in):
    return tensor_in.reshape(tensor_in.shape[0], HEADS, -1).transpose(1, 0, 2)


def merge_heads(stacked):
    return stacked.transpose(1, 0, 2).reshape(stacked.shape[1], -1)


def cast_all(masters):
    return tuple((tensor.astype(jnp.bfloat16) for tensor in masters))


def fetch_forward(masters):
    casted = cast_all(masters)
    return (
        lax.all_gather(casted[0], ("dp", "seq"), axis=1, tiled=True),
        lax.all_gather(casted[1], ("dp", "seq"), axis=1, tiled=True),
        lax.all_gather(casted[2], ("dp", "seq"), axis=1, tiled=True),
        lax.all_gather(casted[3], ("dp", "seq"), axis=1, tiled=True),
        lax.all_gather(casted[4], ("dp", "seq"), axis=1, tiled=True),
        lax.all_gather(casted[5], ("dp", "seq"), axis=0, tiled=True),
        lax.all_gather(casted[6], ("dp", "seq"), axis=1, tiled=True),
    )


def fetch_backward(masters):
    casted = cast_all(masters)
    return (
        lax.all_gather(casted[0], ("dp", "seq"), axis=1, tiled=True),
        lax.all_gather(casted[1], ("dp", "seq"), axis=1, tiled=True),
        lax.all_gather(casted[2], ("dp", "seq"), axis=1, tiled=True),
        lax.all_gather(casted[3], ("dp", "seq"), axis=1, tiled=True),
        lax.all_gather(casted[4], ("dp", "seq"), axis=1, tiled=True),
        lax.all_gather(casted[5], ("dp", "seq"), axis=0, tiled=True),
        lax.all_gather(casted[6], ("dp", "seq"), axis=1, tiled=True),
    )


def gelu_slope(values):
    normal_cdf = 0.5 * (1.0 + jax.scipy.special.erf(values * ROOT_HALF))
    return normal_cdf + values * jnp.exp(-0.5 * values * values) * DENSITY_SCALE


def layer_norm(values, gain_vec, shift_vec):
    centre = values - jnp.mean(values, axis=1, keepdims=True)
    inv_std = lax.rsqrt(jnp.mean(centre * centre, axis=1, keepdims=True) + EPSILON)
    centred = centre * inv_std
    return (centred * gain_vec + shift_vec, centred, inv_std)


def norm_back(grad_out, centred, inv_std, gain_vec):
    scaled = grad_out * gain_vec
    grad_gain = jnp.sum(grad_out * centred, axis=0)
    grad_shift = jnp.sum(grad_out, axis=0)
    grad_in = inv_std * (
        scaled
        - jnp.mean(scaled, axis=1, keepdims=True)
        - centred * jnp.mean(scaled * centred, axis=1, keepdims=True)
    )
    return (grad_in, grad_gain, grad_shift)


def attend_forward(queries, gathered, visible):
    features = queries.shape[1]
    head_q = split_heads(queries)
    head_k = split_heads(gathered[:, :features])
    head_v = split_heads(gathered[:, features:])

    def one_head(members):
        head_query, head_keys, head_values = members
        scores = jnp.where(visible, dot_rows(head_query, head_keys) * SCORE_SCALE, NEGATIVE)
        largest = jnp.max(scores, axis=1, keepdims=True)
        exponent = jnp.exp(scores - largest)
        row_total = jnp.sum(exponent, axis=1, keepdims=True)
        probability = (exponent / row_total).astype(jnp.bfloat16)
        head_out = jnp.dot(probability, head_values, preferred_element_type=jnp.float32)
        return (head_out, (largest + jnp.log(row_total))[:, 0])

    head_outs, log_totals = lax.map(one_head, (head_q, head_k, head_v))
    return (merge_heads(head_outs), log_totals)


def attend_backward(queries, gathered, visible, grad_att, log_totals):
    features = queries.shape[1]
    head_q = split_heads(queries)
    head_k = split_heads(gathered[:, :features])
    head_v = split_heads(gathered[:, features:])
    head_g = split_heads(grad_att)

    def one_head(members):
        head_query, head_keys, head_values, head_grad, head_logs = members
        scores = jnp.where(visible, dot_rows(head_query, head_keys) * SCORE_SCALE, NEGATIVE)
        probability = jnp.exp(scores - head_logs[:, None])
        grad_prob = dot_rows(head_grad, head_values)
        row_delta = jnp.sum(probability * grad_prob, axis=1)
        grad_score = (probability * (grad_prob - row_delta[:, None])).astype(jnp.bfloat16)
        grad_query = (
            jnp.dot(grad_score, head_keys, preferred_element_type=jnp.float32) * SCORE_SCALE
        )
        grad_keys = dot_cols(grad_score, head_query) * SCORE_SCALE
        grad_values = dot_cols(probability.astype(jnp.bfloat16), head_grad)
        return (grad_query, grad_keys, grad_values)

    results = lax.map(one_head, (head_q, head_k, head_v, head_g, log_totals))
    grad_query = merge_heads(results[0])
    return (grad_query, jnp.concatenate([merge_heads(results[1]), merge_heads(results[2])], axis=1))


def layer_forward(stream, weights, visible):
    w_qkv, w_out, w_up, w_down, vec_bias, b_up, vec_norm = weights
    vec_bias = vec_bias.astype(jnp.float32)
    b_up = b_up.astype(jnp.float32)
    vec_norm = vec_norm.astype(jnp.float32)
    features = stream.shape[1]
    stream_low = stream.astype(jnp.bfloat16)
    bias_row = jnp.concatenate([vec_bias[0], jnp.zeros_like(vec_bias[0]), vec_bias[1]])
    qkv = (jnp.dot(stream_low, w_qkv, preferred_element_type=jnp.float32) + bias_row).astype(
        jnp.bfloat16
    )
    queries = qkv[:, :features]
    local_kv = qkv[:, features:]
    gathered = lax.all_gather(local_kv, "seq", axis=0, tiled=True)
    attended, log_totals = attend_forward(queries, gathered, visible)
    att_low = attended.astype(jnp.bfloat16)
    branch = jnp.dot(att_low, w_out, preferred_element_type=jnp.float32) + vec_bias[2]
    normed, centred_one, inv_std_one = layer_norm(stream + branch, vec_norm[0], vec_norm[1])
    normed_low = normed.astype(jnp.bfloat16)
    hidden = jnp.dot(normed_low, w_up, preferred_element_type=jnp.float32) + b_up
    active = jax.nn.gelu(hidden, approximate=False).astype(jnp.bfloat16)
    second = jnp.dot(active, w_down, preferred_element_type=jnp.float32) + vec_bias[3]
    result, centred_two, inv_std_two = layer_norm(normed + second, vec_norm[2], vec_norm[3])
    cache = (
        stream_low,
        queries,
        local_kv,
        None,
        att_low,
        log_totals,
        centred_one,
        inv_std_one,
        normed_low,
        hidden,
        active,
        centred_two,
        inv_std_two,
    )
    return (result, cache)


def layer_backward(gradient, cache, weights, visible):
    w_qkv, w_out, w_up, w_down, vec_bias, b_up, vec_norm = weights
    vec_norm = vec_norm.astype(jnp.float32)
    (
        stream_low,
        queries,
        local_kv,
        kept_kv,
        att_low,
        log_totals,
        centred_one,
        inv_std_one,
        normed_low,
        hidden,
        active,
        centred_two,
        inv_std_two,
    ) = cache
    features = queries.shape[1]
    gathered = lax.all_gather(local_kv, "seq", axis=0, tiled=True)
    grad_two, gain_two, shift_two = norm_back(gradient, centred_two, inv_std_two, vec_norm[2])
    grad_second = grad_two.astype(jnp.bfloat16)
    bias_down = jnp.sum(grad_second.astype(jnp.float32), axis=0)
    grad_w_down = dot_cols(active, grad_second)
    grad_active = dot_rows(grad_second, w_down)
    grad_hidden = (grad_active * gelu_slope(hidden)).astype(jnp.bfloat16)
    bias_upper = jnp.sum(grad_hidden.astype(jnp.float32), axis=0)
    grad_w_up = dot_cols(normed_low, grad_hidden)
    grad_normed = grad_two + dot_rows(grad_hidden, w_up)
    grad_one, gain_one, shift_one = norm_back(grad_normed, centred_one, inv_std_one, vec_norm[0])
    grad_branch = grad_one.astype(jnp.bfloat16)
    bias_output = jnp.sum(grad_branch.astype(jnp.float32), axis=0)
    grad_w_out = dot_cols(att_low, grad_branch)
    grad_att = dot_rows(grad_branch, w_out).astype(jnp.bfloat16)
    grad_query, kv_terms = attend_backward(queries, gathered, visible, grad_att, log_totals)
    kv_grad = lax.psum_scatter(
        kv_terms.astype(jnp.bfloat16), "seq", scatter_dimension=0, tiled=True
    ).astype(jnp.float32)
    grad_qkv = jnp.concatenate([grad_query, kv_grad], axis=1).astype(jnp.bfloat16)
    qkv_sums = jnp.sum(grad_qkv.astype(jnp.float32), axis=0)
    grad_w_qkv = dot_cols(stream_low, grad_qkv)
    grad_stream = grad_one + dot_rows(grad_qkv, w_qkv)
    grad_bias = jnp.stack([qkv_sums[:features], qkv_sums[2 * features :], bias_output, bias_down])
    grad_norm = jnp.stack([gain_one, shift_one, gain_two, shift_two])
    return (
        grad_stream,
        (grad_w_qkv, grad_w_out, grad_w_up, grad_w_down, grad_bias, bias_upper, grad_norm),
    )


def local(
    inputs,
    qkv_weight,
    out_weight,
    up_weight,
    down_weight,
    biases,
    up_bias,
    norms,
    cotangent,
    prefix,
):
    masters = (qkv_weight, out_weight, up_weight, down_weight, biases, up_bias, norms)
    row_count = inputs.shape[0]
    key_count = row_count * lax.axis_size("seq")
    rows_here = lax.axis_index("seq") * row_count + jnp.arange(row_count, dtype=jnp.int32)
    all_index = jnp.arange(key_count, dtype=jnp.int32)
    visible = (all_index[None, :] <= rows_here[:, None]) | (all_index[None, :] < prefix[0])
    stream = inputs.astype(jnp.float32)
    caches = []
    for position in range(2):
        weights = fetch_forward(masters)
        stream, cache = layer_forward(stream, weights, visible)
        caches.append(cache)
    gradient = cotangent.astype(jnp.float32)
    accumulated = None
    for position in range(2):
        weights = fetch_backward(masters)
        gradient, grad_parts = layer_backward(gradient, caches[1 - position], weights, visible)
        if accumulated is None:
            accumulated = grad_parts
        else:
            accumulated = tuple((prior + fresh for prior, fresh in zip(accumulated, grad_parts)))
    reduced = (
        lax.psum_scatter(accumulated[0], ("dp", "seq"), scatter_dimension=1, tiled=True),
        lax.psum_scatter(accumulated[1], ("dp", "seq"), scatter_dimension=1, tiled=True),
        lax.psum_scatter(accumulated[2], ("dp", "seq"), scatter_dimension=1, tiled=True),
        lax.psum_scatter(accumulated[3], ("dp", "seq"), scatter_dimension=1, tiled=True),
        lax.psum_scatter(accumulated[4], ("dp", "seq"), scatter_dimension=1, tiled=True),
        lax.psum_scatter(accumulated[5], ("dp", "seq"), scatter_dimension=0, tiled=True),
        lax.psum_scatter(accumulated[6], ("dp", "seq"), scatter_dimension=1, tiled=True),
    )
    return (
        stream.astype(jnp.bfloat16),
        gradient,
        reduced[0],
        reduced[1],
        reduced[2],
        reduced[3],
        reduced[4],
        reduced[5],
        reduced[6],
    )


F32 = jnp.float32
BF16 = jnp.bfloat16
MESH = pl.DeviceIdType.MESH
LOG2E = math.log2(math.e)
EXP2_SCALE = SCORE_SCALE * LOG2E


def mm_nn(a, b):
    return lax.dot_general(a, b, (((1,), (0,)), ((), ())), preferred_element_type=F32)


def mm_nt(a, b):
    return lax.dot_general(a, b, (((1,), (1,)), ((), ())), preferred_element_type=F32)


def mm_tn(a, b):
    return lax.dot_general(a, b, (((0,), (0,)), ((), ())), preferred_element_type=F32)


def fused_step(tokens, d_model, d_ff, heads):
    hd = d_model // heads
    seq_len = tokens * 8
    fixed = (seq_len // 2) // tokens
    class Group:
        def __init__(self, rows, cols, x_first, y_first, reduced=True):
            halves = len(x_first)
            self.x_first = x_first
            self.y_first = y_first
            self.rows, self.cols, self.halves = rows, cols, halves
            self.whole = (halves, 2, 2, 2, 2, 2, rows, cols)
            self.weight = vm(self.whole, BF16)
            if not reduced:
                return
            self.grad = vm(self.whole, BF16)
            one = (halves, 2, 2, 2, 2, rows, cols)
            two = (2, 2, 2, rows, cols)
            self.recv1 = vm(one, BF16)
            self.send2, self.recv2 = [vm(two, BF16) for _ in x_first], [vm(two, BF16) for _ in x_first]
            two = (2, 2, rows, cols)
            self.send3, self.recv3 = [vm(two, BF16) for _ in x_first], [vm(two, BF16) for _ in x_first]
            self.sum3 = vm((2, 2, halves, rows, cols), F32)
            one = (2, halves, rows, cols)
            self.send4, self.recv4, self.sum4 = vm(one, BF16), vm(one, BF16), vm(one, F32)
            self.send5, self.recv5 = vm(one[1:], BF16), vm(one[1:], BF16)

    chunk = d_ff // 4
    three = 3 * hd
    scratch = []
    count = [0]

    def take(number):
        first = count[0]
        count[0] += number
        return first

    def vm(shape, dtype):
        scratch.append(pltpu.VMEM(shape, dtype))
        return len(scratch) - 1

    def per_layer(shape, dtype):
        return [vm(shape, dtype) for _ in range(2)]

    g_qkv = Group(3 * d_model // 32, d_model // 2, (True, True), (True, False), reduced=False)
    g_out = Group(d_model // 32, d_model // 2, (False, False), (True, False))
    g_up = Group(d_ff // 32, d_model // 2, (True, False), (True, False))
    g_down = Group(d_model // 32, d_ff // 2, (True, True), (True, False))
    v_own = vm((d_model // 32, 128), BF16)
    v_all, v_send, v_recv = (vm((32, d_model // 32, 128), BF16) for _ in range(3))
    everything = (g_qkv, g_out, g_up, g_down)
    own_q, head_w = vm((3, 16, d_model), BF16), vm((3, 4, 16, d_model), BF16)
    head_g = vm((three, d_model), F32)
    tile_s, tile_r = vm((3, 4, 16, d_model), BF16), vm((3, 4, 16, d_model), BF16)
    s_all = per_layer((8, tokens, d_model), BF16)
    pack = vm((128, 16), F32)
    c_in = vm((tokens, d_model), BF16)
    p_out, p_in = vm((8, 128), jnp.int32), vm((8, 128), jnp.int32)
    o_send, i_send, i_recv = (vm((tokens, d_model), BF16) for _ in range(3))
    x32, h1_ = vm((d_model, tokens), F32), vm((d_model, tokens), F32)
    hlow = per_layer((d_model, tokens), BF16)
    xh1, xh2 = per_layer((d_model, tokens), F32), per_layer((d_model, tokens), F32)
    rs1, rs2 = per_layer((8, tokens), F32), per_layer((8, tokens), F32)
    slope, act = per_layer((d_ff, tokens), F32), per_layer((d_ff, tokens), BF16)
    lse, o32 = per_layer((8, 8, tokens), F32), per_layer((8, hd, tokens), F32)
    send1, send3 = vm((8, hd, tokens), BF16), vm((8, three, tokens), BF16)
    qr, ar = per_layer((8, three, tokens), BF16), per_layer((8, hd, tokens), BF16)
    dr, er = per_layer((8, hd, tokens), BF16), per_layer((8, three, tokens), BF16)
    g32, dh32 = vm((d_model, tokens), F32), vm((d_model, tokens), F32)
    dz_, dz2_ = vm((d_model, tokens), BF16), vm((d_model, tokens), BF16)
    kt, vt, qt, dt = (vm((seq_len, hd), BF16) for _ in range(4))
    dk, dv = vm((seq_len, hd), F32), vm((seq_len, hd), F32)
    df_ = vm((d_ff, tokens), BF16)
    gv = vm((d_model, 128), F32)

    def body(ins, outs, R, SS, RS):
        (in_ref, wqkv, wout, wup, wdown, biases, upb, norms, cot_ref, pref_ref) = ins
        (o_out, o_ig, o_qkv, o_gout, o_up, o_down, o_bias, o_upb, o_norms) = outs
        dp, sq = lax.axis_index("dp"), lax.axis_index("seq")
        x, c = dp // 2, dp % 2
        z, y = sq // 2, sq % 2
        zh, zl = z // 2, z % 2
        rank = 4 * c + 2 * zl + y

        def dev(x_, c_, z_, y_):
            return (x_ * 2 + c_, z_ * 2 + y_)

        def remote(src, dst, idx, device, arrival=None):
            return pltpu.make_async_remote_copy(
                src_ref=src,
                dst_ref=dst,
                send_sem=SS.at[idx],
                recv_sem=RS.at[idx if arrival is None else arrival],
                device_id=device,
                device_id_type=MESH,
            )

        def peer(k):
            c_ = (c + k // 4) % 2
            zl_ = (zl + (k // 2) % 2) % 2
            y_ = (y + k % 2) % 2
            return dev(x, c_, 2 * zh + zl_, y_), 4 * c_ + 2 * zl_ + y_

        sends = []

        barrier = pltpu.get_barrier_semaphore()
        swap_dev = dev(x, 1 - c, 2 * (1 - zh) + zl, y)
        me = dp * 8 + sq

        def greet(i, carry):
            other = (me + i) % 32
            pl.semaphore_signal(barrier, inc=1, device_id=(other // 8, other % 8), device_id_type=MESH)
            return carry

        lax.fori_loop(1, 32, greet, 0)

        def place(n, value):
            for h in range(n.halves):
                R[n.weight][h, x, c, zh, zl, y] = value[:, h * n.cols : (h + 1) * n.cols]

        R[own_q][...] = wqkv[...].astype(BF16).reshape(3, 16, d_model)
        place(g_qkv, wqkv[...].astype(BF16))
        R[pack][0:4, :] = biases[...]
        R[pack][4:8, :] = norms[...]
        for b in range(4):
            R[pack][8 + b : 9 + b, :] = upb[:, 16 * b : 16 * (b + 1)]
        R[pack][12:128, :] = jnp.zeros((116, 16), F32)
        R[v_own][...] = R[pack][...].T.astype(BF16)
        R[p_out][...] = jnp.full((8, 128), pref_ref[0], jnp.int32)
        place(g_out, wout[...].astype(BF16))
        place(g_up, wup[...].astype(BF16))
        place(g_down, wdown[...].astype(BF16))
        pl.semaphore_wait(barrier, 31)

        swapped = c != zh

        def swap(src, dst, idx):
            return remote(src, dst, idx, swap_dev)

        s_idx, s2_idx, c_idx, p_idx, so_idx, si_idx = (take(1) for _ in range(6))

        w_base, t_base = take(13), take(13)

        def head_of(i, block):
            t = 3 * me + i
            h = (t % 32) // 4
            device = dev(block // 2, h // 4, 2 * (block % 2) + (h // 2) % 2, h % 2)
            return t, device, (h == rank) & (block == 2 * x + zh)

        def owner_of(n):
            t = (n // 4) * 32 + 4 * rank + n % 4
            return t // 3, t % 3

        def weight_copy(n):
            i, block = n // 4, n % 4
            t, device, here = head_of(i, block)
            part, sub = t // 32, t % 4
            dst = R[head_w].at[part, sub]
            return remote(R[own_q].at[i], dst, w_base + n, device, w_base + 12), here, (i, part, sub)

        v_base = take(2)

        def whole_copy(name, i):
            return pltpu.make_async_copy(R[name], R[name], RS.at[i])

        def vec_out(i, carry):
            other = (me + i) % 32
            remote(R[v_own], R[v_all].at[me], v_base, (other // 8, other % 8)).start()
            return carry

        def vec_back(i, carry):
            other = (me + i) % 32
            remote(R[v_send].at[other], R[v_recv].at[me], v_base + 1, (other // 8, other % 8)).start()
            return carry

        def weight_send(n, carry):
            copy, here, (i, part, sub) = weight_copy(n)

            @pl.when(jnp.logical_not(here))
            def _():
                copy.start()

            @pl.when(here)
            def _():
                pltpu.make_async_copy(R[own_q].at[i], R[head_w].at[part, sub], RS.at[w_base + 12]).start()

            return carry

        def weight_wait(n, carry):
            copy, here, _ = weight_copy(n)

            @pl.when(jnp.logical_not(here))
            def _():
                copy.wait_send()

            return carry

        def tile_copy(n):
            owner, i = owner_of(n)
            block = 2 * x + zh
            src, dst = R[tile_s].at[n // 4, n % 4], R[tile_r].at[i, block]
            device = (owner // 8, owner % 8)
            return remote(src, dst, t_base + n, device, t_base + 12), owner == me, (i, block)

        def tile_send(n, carry):
            copy, here, (i, block) = tile_copy(n)

            @pl.when(jnp.logical_not(here))
            def _():
                copy.start()

            @pl.when(here)
            def _():
                pltpu.make_async_copy(R[tile_s].at[n // 4, n % 4], R[tile_r].at[i, block], RS.at[t_base + 12]).start()

            return carry

        def tile_wait(n, carry):
            copy, here, _ = tile_copy(n)

            @pl.when(jnp.logical_not(here))
            def _():
                copy.wait_send()

            return carry

        s_base = [take(13), take(13)]

        def rank_of(c_, zl_, y_):
            return 4 * c_ + 2 * zl_ + y_

        x_dev, zz_dev = dev(1 - x, c, z, y), dev(x, c, (z + 2) % 4, y)
        y_dev, z_dev, c_dev = dev(x, c, z, 1 - y), dev(x, c, 2 * zh + 1 - zl, y), dev(x, 1 - c, z, y)
        top, low_rows = slice(0, tokens // 2), slice(tokens // 2, tokens)

        def s_copy(l, i):
            py, pz, pd = rank_of(c, zl, 1 - y), rank_of(c, 1 - zl, y), rank_of(c, 1 - zl, 1 - y)
            r = R[s_all[l]]
            ref, device = (
                (r.at[rank, top], y_dev),
                (r.at[rank, low_rows], y_dev),
                (r.at[rank, low_rows], z_dev),
                (r.at[rank, top], z_dev),
                (r.at[rank], c_dev),
                (r.at[py, top], z_dev),
                (r.at[pz, low_rows], y_dev),
                (r.at[py, top], c_dev),
                (r.at[py, low_rows], c_dev),
                (r.at[pz, low_rows], c_dev),
                (r.at[pz, top], c_dev),
                (r.at[pd, top], c_dev),
                (r.at[pd, low_rows], c_dev),
            )[i]
            return remote(ref, ref, s_base[l] + i, device)

        def s_start(l, *which):
            for i in which:
                s_copy(l, i).start()

        def s_got(l, *which):
            for i in which:
                s_copy(l, i).wait_recv()

        own_rank = R[s_all[0]].at[rank]
        swap_rank = R[s_all[0]].at[rank_of(1 - c, zl, y)]

        def swap_rows(rows, idx):
            return swap(in_ref.at[rows], swap_rank.at[rows], idx)

        @pl.when(swapped)
        def _():
            swap_rows(top, s_idx).start()
            swap_rows(low_rows, s2_idx).start()
            swap(R[p_out], R[p_in], p_idx).start()

        @pl.when(jnp.logical_not(swapped))
        def _():
            own_rank[...] = in_ref[...]
            R[p_in][...] = R[p_out][...]

        ag = {}
        for n in everything:
            ag[n] = (take(2), take(2), take(2), take(1))

        def ag_z(n, _):
            own = R[n.weight].at[:, x, c, zh, zl, y]
            cp = remote(own, own, ag[n][0], zz_dev)
            cp.start()
            sends.append(cp)
            return [cp]

        def ag_zz(n, waits):
            waits[0].wait_recv()
            part = R[n.weight].at[:, x, c, :, zl, y]
            cp = remote(part, part, ag[n][0] + 1, z_dev)
            cp.start()
            sends.append(cp)
            return [cp]

        def ag_a(n, waits):
            waits[0].wait_recv()
            w = R[n.weight]
            cps = []
            for h in range(n.halves):
                part = w.at[h, x, c, :, :, y]
                cps.append(remote(part, part, ag[n][1] + h, y_dev if n.y_first[h] else x_dev))
                cps[-1].start()
            sends.extend(cps)
            return cps

        def ag_b(n, waits):
            w = R[n.weight]
            cps = []
            for h in range(n.halves):
                waits[h].wait_recv()
                part = w.at[h, x, c] if n.y_first[h] else w.at[h, :, c, :, :, y]
                cps.append(remote(part, part, ag[n][2] + h, x_dev if n.y_first[h] else y_dev))
                cps[-1].start()
            sends.extend(cps)
            return cps

        def ag_c(n, waits):
            for cp in waits:
                cp.wait_recv()
            part = R[n.weight].at[:, :, c]
            cp = remote(part, part, ag[n][3], c_dev)
            cp.start()
            sends.append(cp)
            return [cp]

        state = {}

        def step(stage, n):
            state[n] = stage(n, state.get(n))

        def arrived(n):
            for cp in state[n]:
                cp.wait_recv()


        @pl.when(swapped)
        def _():
            swap_rows(top, s_idx).wait()
            s_start(0, 0, 3)
            swap_rows(low_rows, s2_idx).wait()
            s_start(0, 2, 1, 4)
            swap(R[p_out], R[p_in], p_idx).wait()

        @pl.when(jnp.logical_not(swapped))
        def _():
            s_start(0, 0, 2, 1, 3, 4)

        step(ag_z, g_up)
        step(ag_z, g_out)
        lax.fori_loop(0, 12, weight_send, 0)
        pltpu.make_async_copy(R[v_own], R[v_all].at[me], RS.at[v_base]).start()
        lax.fori_loop(1, 32, vec_out, 0)
        s_got(0, 0)
        s_start(0, 5, 7)
        s_got(0, 2)
        s_start(0, 6, 9)
        s_got(0, 1)
        s_start(0, 8)
        s_got(0, 3)
        s_start(0, 10)
        step(ag_zz, g_up)
        step(ag_zz, g_out)
        step(ag_z, g_down)
        s_got(0, 5)
        s_start(0, 11)
        s_got(0, 6)
        s_start(0, 12)
        step(ag_a, g_up)
        step(ag_zz, g_down)
        step(ag_a, g_out)
        R[x32][...] = own_rank[...].T.astype(F32)
        s_got(0, 4, 7, 8, 9, 10, 11, 12)
        whole_copy(head_w, w_base + 12).wait()
        whole_copy(v_all, v_base).wait()

        def weight(n, h):
            return R[n.weight][h].reshape(32 * n.rows, n.cols)

        def vec(i):
            return R[v_all][:, :, i : i + 1].reshape(d_model, 1).astype(F32)

        def up_bias(i):
            lanes = [
                R[v_all][8 * i : 8 * (i + 1), :, 8 + b : 9 + b].reshape(8, 1, 16, 1).astype(F32)
                for b in range(4)
            ]
            return jnp.concatenate(lanes, axis=1).reshape(chunk, 1)

        def spread(src, dst):
            base = take(8)
            cps = []
            for k in range(1, 8):
                device, other = peer(k)
                cps.append(remote(src.at[other], dst.at[rank], base + k, device))
                cps[-1].start()
            dst[rank] = src[rank]
            return cps

        def batch(src, dst, base, core):
            def go(ks):
                for k in ks:
                    device, other = peer(k)
                    remote(src.at[other], dst.at[rank], base + k, device).start()

            @pl.when(c == core)
            def _():
                go(range(1, 4))
                dst[rank] = src[rank]

            @pl.when(c != core)
            def _():
                go(range(4, 8))

        def sent(src, dst, base):
            for k in range(1, 8):
                remote(src.at[0], dst.at[0], base + k, peer(k)[0]).wait()

        def finish(cps):
            for cp in cps:
                cp.wait()

        def ext(qb):
            return max(fixed, qb + 1)

        def span(first, last=None):
            return slice(first * tokens, (first + 1 if last is None else last) * tokens)

        def masked(s, qb):
            if qb < fixed:
                kk = lax.broadcasted_iota(jnp.int32, s.shape, 0)
                qq = qb * tokens + lax.broadcasted_iota(jnp.int32, s.shape, 1)
                return jnp.where((kk <= qq) | (kk < R[p_in][0:1, 0:1]), s, NEGATIVE)
            low = s[qb * tokens :]
            kk = lax.broadcasted_iota(jnp.int32, low.shape, 0)
            qq = lax.broadcasted_iota(jnp.int32, low.shape, 1)
            low = jnp.where(kk <= qq, low, NEGATIVE)
            return jnp.concatenate([s[: qb * tokens], low], axis=0)

        def norm(r, gain, shift):
            centre = r - jnp.mean(r, axis=0, keepdims=True)
            inv = lax.rsqrt(jnp.mean(centre * centre, axis=0, keepdims=True) + EPSILON)
            xh = centre * inv
            return xh * gain + shift, xh, inv

        def forward(l):
            rows_all, qkv_all = R[s_all[l]], R[qr[l]]
            if l == 1:
                s_start(1, 0, 2, 1, 3, 4)
                s_got(1, 0)
                s_start(1, 5, 7)
                s_got(1, 2)
                s_start(1, 6, 9)
                s_got(1, 1)
                s_start(1, 8)
                s_got(1, 3)
                s_start(1, 10)
                s_got(1, 5)
                s_start(1, 11)
                s_got(1, 6)
                s_start(1, 12)
                s_got(1, 4, 7, 8, 9, 10, 11, 12)
                step(ag_z, g_qkv)

                @pl.when(swapped)
                def _():
                    swap(cot_ref, R[c_in], c_idx).start()

            packed = R[v_all][pl.ds(4 * rank, 4)]
            packed = packed.reshape(hd, 128).astype(F32)
            bias = jnp.concatenate([packed[:, 0:1], jnp.zeros((hd, 1), F32), packed[:, 1:2]], axis=0)
            w = R[head_w][...].reshape(three, d_model)
            for b in range(8):
                qkv_all[b] = (mm_nt(w, rows_all[b]) + bias).astype(BF16)
            for b in range(8):
                R[kt][span(b), :] = qkv_all[b, hd : 2 * hd, :].T
                R[vt][span(b), :] = qkv_all[b, 2 * hd :, :].T
            base = take(8)
            for qb in range(8):
                n = ext(qb)
                s = masked(mm_nn(R[kt][span(0, n), :], qkv_all[qb, 0:hd, :]) * EXP2_SCALE, qb)
                m = jnp.max(s, axis=0, keepdims=True)
                p = jnp.exp2(s - m)
                total = jnp.sum(p, axis=0, keepdims=True)
                o = mm_tn(p.astype(BF16), R[vt][span(0, n), :]).T / total
                R[o32[l]][qb] = o
                R[send1][qb] = o.astype(BF16)
                R[lse[l]][qb] = jnp.broadcast_to(m + jnp.log2(total), (8, tokens))
                if qb == 3:
                    batch(R[send1], R[ar[l]], base, 0)
                if l == 0 and qb == 1:
                    step(ag_b, g_up)
                    step(ag_a, g_down)
                if l == 0 and qb == 4:
                    step(ag_b, g_out)
                if l == 1 and qb == 4:
                    step(ag_zz, g_qkv)
            batch(R[send1], R[ar[l]], base, 1)
            if l == 0:
                step(ag_c, g_out)
                step(ag_b, g_down)
                step(ag_c, g_up)
                lax.fori_loop(0, 12, weight_wait, 0)
            sent(R[send1], R[ar[l]], base)
            if l == 1:
                step(ag_a, g_qkv)
            if l == 0:
                arrived(g_out)
            att = R[ar[l]][...].reshape(d_model, tokens)
            half = d_model // 2
            r1 = R[x32][...] + vec(2)
            r1 = r1 + mm_nn(weight(g_out, 0), att[:half]) + mm_nn(weight(g_out, 1), att[half:])
            h1, xh, inv = norm(r1, vec(4), vec(5))
            R[h1_][...] = h1
            R[xh1[l]][...] = xh
            R[rs1[l]][...] = jnp.broadcast_to(inv, (8, tokens))
            R[hlow[l]][...] = h1.astype(BF16)
            if l == 0:
                step(ag_c, g_down)
                arrived(g_up)
            for i in range(4):
                rows = slice(i * chunk, (i + 1) * chunk)
                g = g_up
                f = up_bias(i)
                for h in range(2):
                    w = R[g_up.weight][h, i // 2, i % 2].reshape(chunk, g.cols)
                    f = f + mm_nn(w, R[hlow[l]][h * half : (h + 1) * half, :])
                cdf = 0.5 * (1.0 + lax.erf(f * ROOT_HALF))
                R[act[l]][rows, :] = (f * cdf).astype(BF16)
                R[slope[l]][rows, :] = cdf + f * (jnp.exp(-0.5 * f * f) * DENSITY_SCALE)
            if l == 0:
                arrived(g_down)
            r2 = R[h1_][...] + vec(3)
            for h in range(2):
                r2 = r2 + mm_nn(weight(g_down, h), R[act[l]][h * d_ff // 2 : (h + 1) * d_ff // 2, :])
            out, xh, inv = norm(r2, vec(6), vec(7))
            R[xh2[l]][...] = xh
            R[rs2[l]][...] = jnp.broadcast_to(inv, (8, tokens))
            return out

        idx = {n: (take(1), take(2), take(2), take(2)) for n in everything[1:]}

        def rs_c(n, _):
            cp = remote(R[n.grad].at[:, :, 1 - c], R[n.recv1], idx[n][0], c_dev)
            cp.start()
            sends.append(cp)
            return [cp]

        def a_send(n, h):
            g_, r1 = R[n.grad], R[n.recv1]
            if n.x_first[h]:
                value, device = g_[h, 1 - x, c].astype(F32) + r1[h, 1 - x].astype(F32), x_dev
            else:
                value, device = g_[h, :, c, :, :, 1 - y].astype(F32) + r1[h, :, :, :, 1 - y].astype(F32), y_dev
            R[n.send2[h]][...] = value.astype(BF16)
            cp = remote(R[n.send2[h]], R[n.recv2[h]], idx[n][1] + h, device)
            cp.start()
            sends.append(cp)
            return cp

        def rs_a_first(n, waits):
            waits[0].wait_recv()
            return [a_send(n, 0)]

        def rs_a_second(n, waits):
            return waits + [a_send(n, 1)]

        def rs_a(n, waits):
            waits = rs_a_first(n, waits)
            return rs_a_second(n, waits) if n.halves == 2 else waits

        def rs_b(n, waits):
            g_, r1 = R[n.grad], R[n.recv1]
            cps = []
            for h in range(n.halves):
                waits[h].wait_recv()
                r2 = R[n.recv2[h]]
                if n.x_first[h]:
                    value, device = g_[h, x, c, :, :, 1 - y].astype(F32) + r1[h, x, :, :, 1 - y].astype(F32), y_dev
                    value = value + r2[:, :, 1 - y].astype(F32)
                else:
                    value, device = g_[h, 1 - x, c, :, :, y].astype(F32) + r1[h, 1 - x, :, :, y].astype(F32), x_dev
                    value = value + r2[1 - x].astype(F32)
                R[n.send3[h]][...] = value.astype(BF16)
                cps.append(remote(R[n.send3[h]], R[n.recv3[h]], idx[n][2] + h, device))
                cps[-1].start()
            sends.extend(cps)
            return cps

        def rs_z(n, waits):
            g_, r1, sum3 = R[n.grad], R[n.recv1], R[n.sum3]
            for h in range(n.halves):
                waits[h].wait_recv()
                r2 = R[n.recv2[h]]
                kept = r2[:, :, y] if n.x_first[h] else r2[x]
                sum3[:, :, h] = (
                    g_[h, x, c, :, :, y].astype(F32)
                    + r1[h, x, :, :, y].astype(F32)
                    + kept.astype(F32)
                    + R[n.recv3[h]][...].astype(F32)
                )
            R[n.send4][...] = sum3[:, 1 - zl].astype(BF16)
            cp = remote(R[n.send4], R[n.recv4], idx[n][3], z_dev)
            cp.start()
            sends.append(cp)
            return [cp]

        def rs_zz(n, waits):
            waits[0].wait_recv()
            R[n.sum4][...] = R[n.sum3][:, zl] + R[n.recv4][...].astype(F32)
            R[n.send5][...] = R[n.sum4][1 - zh].astype(BF16)
            cp = remote(R[n.send5], R[n.recv5], idx[n][3] + 1, zz_dev)
            cp.start()
            sends.append(cp)
            return [cp]

        def rs_end(n, waits):
            waits[0].wait_recv()
            return R[n.sum4][zh] + R[n.recv5][...].astype(F32)

        def pick(lane, count_=1):
            rows = lax.broadcasted_iota(jnp.int32, (128, tokens), 0)
            return jnp.where((rows >= lane) & (rows < lane + count_), 1.0, 0.0).astype(BF16)

        def low_sum(lane, value):
            return mm_nt(value, pick(lane))

        def full_sum(lane, value):
            high = value.astype(BF16)
            return low_sum(lane, high) + low_sum(lane, (value - high.astype(F32)).astype(BF16))

        def add_grad(n, h, value, l):
            value = value.reshape(n.whole[1:])
            if l == 0:
                value = value + R[n.grad][h].astype(F32)
            R[n.grad][h] = value.astype(BF16)

        def norm_grad(g, xh, inv, gain):
            s = g * gain
            return inv * (
                s - jnp.mean(s, axis=0, keepdims=True) - xh * jnp.mean(s * xh, axis=0, keepdims=True)
            )

        half = d_model // 2

        def out_grad(l):
            att = R[ar[l]][...].reshape(d_model, tokens)
            for h in range(2):
                add_grad(g_out, h, mm_nt(R[dz_][...], att[h * half : (h + 1) * half]), l)

        def up_grad(l):
            for h in range(2):
                add_grad(g_up, h, mm_nt(R[df_][...], R[hlow[l]][h * half : (h + 1) * half, :]), l)

        def down_grad(l):
            for h in range(2):
                add_grad(g_down, h, mm_nt(R[dz2_][...], R[act[l]][h * d_ff // 2 : (h + 1) * d_ff // 2, :]), l)

        def head_grad(l):
            rows_all, back = R[s_all[l]], R[send3]
            t = mm_nn(back[0], rows_all[0])
            sums = low_sum(0, back[0, 0:hd]) + low_sum(1, back[0, 2 * hd :])
            for b in range(1, 8):
                t = t + mm_nn(back[b], rows_all[b])
                sums = sums + low_sum(0, back[b, 0:hd]) + low_sum(1, back[b, 2 * hd :])
            R[gv][pl.ds(pl.multiple_of(rank * hd, hd), hd), :] += sums
            if l == 1:
                R[head_g][...] = t
            else:
                R[tile_s][...] = (R[head_g][...] + t).astype(BF16).reshape(3, 4, 16, d_model)

        def dense_sums(l):
            t = full_sum(6, R[g32][...] * R[xh2[l]][...]) + full_sum(7, R[g32][...])
            t = t + full_sum(4, R[dh32][...] * R[xh1[l]][...]) + full_sum(5, R[dh32][...])
            t = t + low_sum(3, R[dz2_][...]) + low_sum(2, R[dz_][...])
            R[gv][...] += t
            ones = pick(8, 4)
            lanes = lax.broadcasted_iota(jnp.int32, (8, 16, 128), 2)
            for i in range(4):
                sums = mm_nt(R[df_][i * chunk : (i + 1) * chunk, :], ones).reshape(8, 4, 16, 128)
                t = jnp.where(lanes == 8, sums[:, 0], 0.0)
                for b in range(1, 4):
                    t = jnp.where(lanes == 8 + b, sums[:, b], t)
                R[gv][i * 128 : (i + 1) * 128, :] += t.reshape(128, 128)

        def backward(l):
            dr2 = norm_grad(R[g32][...], R[xh2[l]][...], R[rs2[l]][0:1, :], vec(6))
            R[dz2_][...] = dr2.astype(BF16)
            R[x32][...] = dr2
            for i in range(4):
                rows = slice(i * chunk, (i + 1) * chunk)
                h, lo = i // 2, (i % 2) * chunk
                w = R[g_down.weight][h].reshape(d_model, d_ff // 2)[:, lo : lo + chunk]
                R[df_][rows, :] = (mm_tn(w, R[dz2_][...]) * R[slope[l]][rows, :]).astype(BF16)
            for h in range(2):
                rows = slice(h * half, (h + 1) * half)
                R[dh32][rows, :] = R[x32][rows, :] + mm_tn(weight(g_up, h), R[df_][...])
            dr1 = norm_grad(R[dh32][...], R[xh1[l]][...], R[rs1[l]][0:1, :], vec(4))
            R[dz_][...] = dr1.astype(BF16)
            R[x32][...] = dr1
            for h in range(2):
                datt = mm_tn(weight(g_out, h), R[dz_][...]).astype(BF16)
                R[send1][h * 4 : (h + 1) * 4] = datt.reshape(4, hd, tokens)
            cps = spread(R[send1], R[dr[l]])
            down_grad(l)
            if l == 0:
                step(rs_c, g_down)
            up_grad(l)
            if l == 0:
                step(rs_c, g_up)
            out_grad(l)
            if l == 0:
                step(rs_c, g_out)
            dense_sums(l)
            if l == 0:
                step(rs_a, g_down)
                step(rs_a_first, g_up)
            finish(cps)
            if l == 0:
                step(rs_a_second, g_up)
                step(rs_a, g_out)
            else:
                step(ag_b, g_qkv)

                @pl.when(swapped)
                def _():
                    swap(R[o_send], o_out, so_idx).start()

            qkv_all, datt_all = R[qr[l]], R[dr[l]]
            for b in range(8):
                R[qt][span(b), :] = qkv_all[b, 0:hd, :].T
                R[kt][span(b), :] = qkv_all[b, hd : 2 * hd, :].T
                R[vt][span(b), :] = qkv_all[b, 2 * hd :, :].T
                R[dt][span(b), :] = datt_all[b].T
            R[dk][...] = jnp.zeros((seq_len, hd), F32)
            R[dv][...] = jnp.zeros((seq_len, hd), F32)
            base = take(8)
            src, dst = R[send3], R[er[l]]

            def keys_out(b):
                src[b, hd : 2 * hd, :] = (R[dk][span(b), :] * SCORE_SCALE).T.astype(BF16)
                src[b, 2 * hd :, :] = R[dv][span(b), :].T.astype(BF16)

            for qb in range(7, -1, -1):
                n = ext(qb)
                keys = span(0, n)
                delta = jnp.sum(datt_all[qb].astype(F32) * R[o32[l]][qb], axis=0, keepdims=True)
                s = masked(mm_nn(R[kt][keys, :], qkv_all[qb, 0:hd, :]) * EXP2_SCALE, qb)
                p = jnp.exp2(s - R[lse[l]][qb, 0:1, :])
                dprob = mm_nn(R[vt][keys, :], datt_all[qb])
                dsc = (p * (dprob - delta)).astype(BF16)
                R[dv][keys, :] += mm_nn(p.astype(BF16), R[dt][span(qb), :])
                R[dk][keys, :] += mm_nn(dsc, R[qt][span(qb), :])
                src[qb, 0:hd, :] = (mm_tn(R[kt][keys, :], dsc) * SCORE_SCALE).astype(BF16)
                if qb == 4:
                    for b in range(4, 8):
                        keys_out(b)
                    batch(src, dst, base, 1)
            for b in range(4):
                keys_out(b)
            batch(src, dst, base, 0)
            if l == 1:
                step(ag_c, g_qkv)
            head_grad(l)
            if l == 0:
                lax.fori_loop(0, 12, tile_send, 0)
                R[v_send][...] = R[gv][...].astype(BF16).reshape(32, 16, 128)
                pltpu.make_async_copy(R[v_send].at[me], R[v_recv].at[me], RS.at[v_base + 1]).start()
                lax.fori_loop(1, 32, vec_back, 0)
                step(rs_b, g_down)
            else:
                arrived(g_qkv)
            sent(src, dst, base)
            back = R[er[l]]
            for h in range(2):
                w = weight(g_qkv, h)
                t = R[x32][h * half : (h + 1) * half, :]
                for part in range(3):
                    grad = back[:, part * hd : (part + 1) * hd, :].reshape(d_model, tokens)
                    t = t + mm_tn(w[part * d_model : (part + 1) * d_model], grad)
                R[g32][h * half : (h + 1) * half, :] = t

        mid = forward(0)
        R[x32][...] = mid
        R[s_all[1]][rank] = mid.astype(BF16).T
        last = forward(1)
        R[o_send][...] = last.astype(BF16).T

        @pl.when(swapped)
        def _():
            swap(cot_ref, R[c_in], c_idx).wait()

        @pl.when(jnp.logical_not(swapped))
        def _():
            o_out[...] = R[o_send][...]
            R[c_in][...] = cot_ref[...]

        R[gv][...] = jnp.zeros((d_model, 128), F32)
        R[g32][...] = R[c_in][...].T.astype(F32)
        backward(1)
        backward(0)
        R[i_send][...] = R[g32][...].astype(BF16).T

        @pl.when(swapped)
        def _():
            swap(R[i_send], R[i_recv], si_idx).start()

        @pl.when(jnp.logical_not(swapped))
        def _():
            o_ig[...] = R[g32][...].T

        step(rs_b, g_out)
        step(rs_z, g_down)
        step(rs_b, g_up)
        step(rs_z, g_out)
        step(rs_zz, g_down)
        step(rs_z, g_up)
        step(rs_zz, g_out)
        step(rs_zz, g_up)
        whole_copy(tile_r, t_base + 12).wait()
        lax.fori_loop(0, 12, tile_wait, 0)
        t = R[tile_r][:, 0].astype(F32)
        for block in range(1, 4):
            t = t + R[tile_r][:, block].astype(F32)
        o_qkv[...] = t.reshape(48, d_model)
        for n, ref in ((g_down, o_down), (g_up, o_up), (g_out, o_gout)):
            t = rs_end(n, state[n])
            ref[...] = jnp.concatenate([t[0], t[1]], axis=1)
        whole_copy(v_recv, v_base + 1).wait()
        t = R[v_recv][0].astype(F32)
        for i in range(1, 32):
            t = t + R[v_recv][i].astype(F32)
        t = t.T
        o_bias[...] = t[0:4]
        o_norms[...] = t[4:8]
        o_upb[...] = jnp.concatenate([t[8 + b : 9 + b] for b in range(4)], axis=1)

        @pl.when(swapped)
        def _():
            swap(R[o_send], o_out, so_idx).wait()
            swap(R[i_send], R[i_recv], si_idx).wait()
            o_ig[...] = R[i_recv][...].astype(F32)

        for cp in sends:
            cp.wait_send()
        for i in range(2):
            sent_vec = R[v_recv].at[0:31]
            pltpu.make_async_copy(sent_vec, sent_vec, SS.at[v_base + i]).wait()
        for l in range(2):
            for i in range(13):
                s_copy(l, i).wait_send()

    n_sems = 6 + 2 * 13 + 2 * 13 + 2 + 4 * 7 + 6 * 8 + 3 * 7

    def kernel(*refs):
        count[0] = 0
        body(refs[:10], refs[10:19], refs[19:-2], refs[-2], refs[-1])
        assert count[0] <= n_sems

    def hand_on(*refs):
        for src, dst in zip(refs[:9], refs[9:]):
            dst[...] = src[...]

    def call(inputs, qkv_w, out_w, up_w, down_w, biases, up_bias, norms, cotangent, prefix):
        weights = [w.T for w in (qkv_w, out_w, up_w, down_w)]
        small = [biases, up_bias.reshape(1, -1), norms]
        out_shape = (
            jax.ShapeDtypeStruct((tokens, d_model), BF16),
            jax.ShapeDtypeStruct((tokens, d_model), F32),
            *(jax.ShapeDtypeStruct(w.shape, F32) for w in weights + small),
        )
        vmem = pl.BlockSpec(memory_space=pltpu.VMEM)
        results = pl.pallas_call(
            kernel,
            out_shape=out_shape,
            in_specs=[vmem] * 9 + [pl.BlockSpec(memory_space=pltpu.SMEM)],
            out_specs=[vmem] * 9,
            scratch_shapes=[
                *scratch,
                pltpu.SemaphoreType.DMA((n_sems,)),
                pltpu.SemaphoreType.DMA((n_sems,)),
            ],
            compiler_params=pltpu.CompilerParams(
                collective_id=0, has_side_effects=True, vmem_limit_bytes=62 * 2**20
            ),
        )(inputs, *weights, *small, cotangent, prefix)
        results = pl.pallas_call(
            hand_on, out_shape=out_shape, in_specs=[vmem] * 9, out_specs=[vmem] * 9
        )(*results)
        back = [w.T for w in results[2:6]]
        return (*results[:2], *back, results[6], results[7].reshape(up_bias.shape), results[8])

    return call


def fused_fits(mesh, args):
    if tuple(mesh.shape.items()) != (("dp", 4), ("seq", 8)) or HEADS != 8:
        return False
    total, d_model = args[0].shape
    d_ff = args[3].shape[1]
    return total % (32 * 128) == 0 and total // 32 == 256 and d_model == 512 and d_ff == 2048


def solution(mesh):
    specs = dict(
        mesh=mesh,
        in_specs=(
            P(("dp", "seq"), None),
            P(None, ("dp", "seq")),
            P(None, ("dp", "seq")),
            P(None, ("dp", "seq")),
            P(None, ("dp", "seq")),
            P(None, ("dp", "seq")),
            P(("dp", "seq")),
            P(None, ("dp", "seq")),
            P(("dp", "seq"), None),
            P("dp"),
        ),
        out_specs=(
            P(("dp", "seq"), None),
            P(("dp", "seq"), None),
            P(None, ("dp", "seq")),
            P(None, ("dp", "seq")),
            P(None, ("dp", "seq")),
            P(None, ("dp", "seq")),
            P(None, ("dp", "seq")),
            P(("dp", "seq")),
            P(None, ("dp", "seq")),
        ),
        check_vma=False,
    )

    def run(*args):
        if fused_fits(mesh, args):
            d_model = args[0].shape[1]
            step = fused_step(args[0].shape[0] // 32, d_model, args[3].shape[1], HEADS)
            return jax.shard_map(step, **specs)(*args)
        return jax.shard_map(local, **specs)(*args)

    return run
```

```python
import math

import jax
import jax.numpy as jnp
from jax import lax
from jax.experimental import pallas as pl
from jax.experimental.pallas import tpu as pltpu
from jax.sharding import PartitionSpec as P

HEADS = 8


EPSILON = 1e-05
NEGATIVE = -1e30
SCORE_SCALE = 0.125
ROOT_HALF = 1.0 / math.sqrt(2.0)
DENSITY_SCALE = 1.0 / math.sqrt(2.0 * math.pi)


def dot_rows(first_op, second_op):
    return lax.dot_general(
        first_op, second_op, (((1,), (1,)), ((), ())), preferred_element_type=jnp.float32
    )


def dot_cols(first_op, second_op):
    return lax.dot_general(
        first_op, second_op, (((0,), (0,)), ((), ())), preferred_element_type=jnp.float32
    )


def split_heads(tensor_in):
    return tensor_in.reshape(tensor_in.shape[0], HEADS, -1).transpose(1, 0, 2)


def merge_heads(stacked):
    return stacked.transpose(1, 0, 2).reshape(stacked.shape[1], -1)


def cast_all(masters):
    return tuple((tensor.astype(jnp.bfloat16) for tensor in masters))


def fetch_forward(masters):
    casted = cast_all(masters)
    return (
        lax.all_gather(casted[0], ("dp", "seq"), axis=1, tiled=True),
        lax.all_gather(casted[1], ("dp", "seq"), axis=1, tiled=True),
        lax.all_gather(casted[2], ("dp", "seq"), axis=1, tiled=True),
        lax.all_gather(casted[3], ("dp", "seq"), axis=1, tiled=True),
        lax.all_gather(casted[4], ("dp", "seq"), axis=1, tiled=True),
        lax.all_gather(casted[5], ("dp", "seq"), axis=0, tiled=True),
        lax.all_gather(casted[6], ("dp", "seq"), axis=1, tiled=True),
    )


def fetch_backward(masters):
    casted = cast_all(masters)
    return (
        lax.all_gather(casted[0], ("dp", "seq"), axis=1, tiled=True),
        lax.all_gather(casted[1], ("dp", "seq"), axis=1, tiled=True),
        lax.all_gather(casted[2], ("dp", "seq"), axis=1, tiled=True),
        lax.all_gather(casted[3], ("dp", "seq"), axis=1, tiled=True),
        lax.all_gather(casted[4], ("dp", "seq"), axis=1, tiled=True),
        lax.all_gather(casted[5], ("dp", "seq"), axis=0, tiled=True),
        lax.all_gather(casted[6], ("dp", "seq"), axis=1, tiled=True),
    )


def gelu_slope(values):
    normal_cdf = 0.5 * (1.0 + jax.scipy.special.erf(values * ROOT_HALF))
    return normal_cdf + values * jnp.exp(-0.5 * values * values) * DENSITY_SCALE


def layer_norm(values, gain_vec, shift_vec):
    centre = values - jnp.mean(values, axis=1, keepdims=True)
    inv_std = lax.rsqrt(jnp.mean(centre * centre, axis=1, keepdims=True) + EPSILON)
    centred = centre * inv_std
    return (centred * gain_vec + shift_vec, centred, inv_std)


def norm_back(grad_out, centred, inv_std, gain_vec):
    scaled = grad_out * gain_vec
    grad_gain = jnp.sum(grad_out * centred, axis=0)
    grad_shift = jnp.sum(grad_out, axis=0)
    grad_in = inv_std * (
        scaled
        - jnp.mean(scaled, axis=1, keepdims=True)
        - centred * jnp.mean(scaled * centred, axis=1, keepdims=True)
    )
    return (grad_in, grad_gain, grad_shift)


def attend_forward(queries, gathered, visible):
    features = queries.shape[1]
    head_q = split_heads(queries)
    head_k = split_heads(gathered[:, :features])
    head_v = split_heads(gathered[:, features:])

    def one_head(members):
        head_query, head_keys, head_values = members
        scores = jnp.where(visible, dot_rows(head_query, head_keys) * SCORE_SCALE, NEGATIVE)
        largest = jnp.max(scores, axis=1, keepdims=True)
        exponent = jnp.exp(scores - largest)
        row_total = jnp.sum(exponent, axis=1, keepdims=True)
        probability = (exponent / row_total).astype(jnp.bfloat16)
        head_out = jnp.dot(probability, head_values, preferred_element_type=jnp.float32)
        return (head_out, (largest + jnp.log(row_total))[:, 0])

    head_outs, log_totals = lax.map(one_head, (head_q, head_k, head_v))
    return (merge_heads(head_outs), log_totals)


def attend_backward(queries, gathered, visible, grad_att, log_totals):
    features = queries.shape[1]
    head_q = split_heads(queries)
    head_k = split_heads(gathered[:, :features])
    head_v = split_heads(gathered[:, features:])
    head_g = split_heads(grad_att)

    def one_head(members):
        head_query, head_keys, head_values, head_grad, head_logs = members
        scores = jnp.where(visible, dot_rows(head_query, head_keys) * SCORE_SCALE, NEGATIVE)
        probability = jnp.exp(scores - head_logs[:, None])
        grad_prob = dot_rows(head_grad, head_values)
        row_delta = jnp.sum(probability * grad_prob, axis=1)
        grad_score = (probability * (grad_prob - row_delta[:, None])).astype(jnp.bfloat16)
        grad_query = (
            jnp.dot(grad_score, head_keys, preferred_element_type=jnp.float32) * SCORE_SCALE
        )
        grad_keys = dot_cols(grad_score, head_query) * SCORE_SCALE
        grad_values = dot_cols(probability.astype(jnp.bfloat16), head_grad)
        return (grad_query, grad_keys, grad_values)

    results = lax.map(one_head, (head_q, head_k, head_v, head_g, log_totals))
    grad_query = merge_heads(results[0])
    return (grad_query, jnp.concatenate([merge_heads(results[1]), merge_heads(results[2])], axis=1))


def layer_forward(stream, weights, visible):
    w_qkv, w_out, w_up, w_down, vec_bias, b_up, vec_norm = weights
    vec_bias = vec_bias.astype(jnp.float32)
    b_up = b_up.astype(jnp.float32)
    vec_norm = vec_norm.astype(jnp.float32)
    features = stream.shape[1]
    stream_low = stream.astype(jnp.bfloat16)
    bias_row = jnp.concatenate([vec_bias[0], jnp.zeros_like(vec_bias[0]), vec_bias[1]])
    qkv = (jnp.dot(stream_low, w_qkv, preferred_element_type=jnp.float32) + bias_row).astype(
        jnp.bfloat16
    )
    queries = qkv[:, :features]
    local_kv = qkv[:, features:]
    gathered = lax.all_gather(local_kv, "seq", axis=0, tiled=True)
    attended, log_totals = attend_forward(queries, gathered, visible)
    att_low = attended.astype(jnp.bfloat16)
    branch = jnp.dot(att_low, w_out, preferred_element_type=jnp.float32) + vec_bias[2]
    normed, centred_one, inv_std_one = layer_norm(stream + branch, vec_norm[0], vec_norm[1])
    normed_low = normed.astype(jnp.bfloat16)
    hidden = jnp.dot(normed_low, w_up, preferred_element_type=jnp.float32) + b_up
    active = jax.nn.gelu(hidden, approximate=False).astype(jnp.bfloat16)
    second = jnp.dot(active, w_down, preferred_element_type=jnp.float32) + vec_bias[3]
    result, centred_two, inv_std_two = layer_norm(normed + second, vec_norm[2], vec_norm[3])
    cache = (
        stream_low,
        queries,
        local_kv,
        None,
        att_low,
        log_totals,
        centred_one,
        inv_std_one,
        normed_low,
        hidden,
        active,
        centred_two,
        inv_std_two,
    )
    return (result, cache)


def layer_backward(gradient, cache, weights, visible):
    w_qkv, w_out, w_up, w_down, vec_bias, b_up, vec_norm = weights
    vec_norm = vec_norm.astype(jnp.float32)
    (
        stream_low,
        queries,
        local_kv,
        kept_kv,
        att_low,
        log_totals,
        centred_one,
        inv_std_one,
        normed_low,
        hidden,
        active,
        centred_two,
        inv_std_two,
    ) = cache
    features = queries.shape[1]
    gathered = lax.all_gather(local_kv, "seq", axis=0, tiled=True)
    grad_two, gain_two, shift_two = norm_back(gradient, centred_two, inv_std_two, vec_norm[2])
    grad_second = grad_two.astype(jnp.bfloat16)
    bias_down = jnp.sum(grad_second.astype(jnp.float32), axis=0)
    grad_w_down = dot_cols(active, grad_second)
    grad_active = dot_rows(grad_second, w_down)
    grad_hidden = (grad_active * gelu_slope(hidden)).astype(jnp.bfloat16)
    bias_upper = jnp.sum(grad_hidden.astype(jnp.float32), axis=0)
    grad_w_up = dot_cols(normed_low, grad_hidden)
    grad_normed = grad_two + dot_rows(grad_hidden, w_up)
    grad_one, gain_one, shift_one = norm_back(grad_normed, centred_one, inv_std_one, vec_norm[0])
    grad_branch = grad_one.astype(jnp.bfloat16)
    bias_output = jnp.sum(grad_branch.astype(jnp.float32), axis=0)
    grad_w_out = dot_cols(att_low, grad_branch)
    grad_att = dot_rows(grad_branch, w_out).astype(jnp.bfloat16)
    grad_query, kv_terms = attend_backward(queries, gathered, visible, grad_att, log_totals)
    kv_grad = lax.psum_scatter(
        kv_terms.astype(jnp.bfloat16), "seq", scatter_dimension=0, tiled=True
    ).astype(jnp.float32)
    grad_qkv = jnp.concatenate([grad_query, kv_grad], axis=1).astype(jnp.bfloat16)
    qkv_sums = jnp.sum(grad_qkv.astype(jnp.float32), axis=0)
    grad_w_qkv = dot_cols(stream_low, grad_qkv)
    grad_stream = grad_one + dot_rows(grad_qkv, w_qkv)
    grad_bias = jnp.stack([qkv_sums[:features], qkv_sums[2 * features :], bias_output, bias_down])
    grad_norm = jnp.stack([gain_one, shift_one, gain_two, shift_two])
    return (
        grad_stream,
        (grad_w_qkv, grad_w_out, grad_w_up, grad_w_down, grad_bias, bias_upper, grad_norm),
    )


def local(
    inputs,
    qkv_weight,
    out_weight,
    up_weight,
    down_weight,
    biases,
    up_bias,
    norms,
    cotangent,
    prefix,
):
    masters = (qkv_weight, out_weight, up_weight, down_weight, biases, up_bias, norms)
    row_count = inputs.shape[0]
    key_count = row_count * lax.axis_size("seq")
    rows_here = lax.axis_index("seq") * row_count + jnp.arange(row_count, dtype=jnp.int32)
    all_index = jnp.arange(key_count, dtype=jnp.int32)
    visible = (all_index[None, :] <= rows_here[:, None]) | (all_index[None, :] < prefix[0])
    stream = inputs.astype(jnp.float32)
    caches = []
    for position in range(2):
        weights = fetch_forward(masters)
        stream, cache = layer_forward(stream, weights, visible)
        caches.append(cache)
    gradient = cotangent.astype(jnp.float32)
    accumulated = None
    for position in range(2):
        weights = fetch_backward(masters)
        gradient, grad_parts = layer_backward(gradient, caches[1 - position], weights, visible)
        if accumulated is None:
            accumulated = grad_parts
        else:
            accumulated = tuple((prior + fresh for prior, fresh in zip(accumulated, grad_parts)))
    reduced = (
        lax.psum_scatter(accumulated[0], ("dp", "seq"), scatter_dimension=1, tiled=True),
        lax.psum_scatter(accumulated[1], ("dp", "seq"), scatter_dimension=1, tiled=True),
        lax.psum_scatter(accumulated[2], ("dp", "seq"), scatter_dimension=1, tiled=True),
        lax.psum_scatter(accumulated[3], ("dp", "seq"), scatter_dimension=1, tiled=True),
        lax.psum_scatter(accumulated[4], ("dp", "seq"), scatter_dimension=1, tiled=True),
        lax.psum_scatter(accumulated[5], ("dp", "seq"), scatter_dimension=0, tiled=True),
        lax.psum_scatter(accumulated[6], ("dp", "seq"), scatter_dimension=1, tiled=True),
    )
    return (
        stream.astype(jnp.bfloat16),
        gradient,
        reduced[0],
        reduced[1],
        reduced[2],
        reduced[3],
        reduced[4],
        reduced[5],
        reduced[6],
    )


F32 = jnp.float32
BF16 = jnp.bfloat16
MESH = pl.DeviceIdType.MESH
LOG2E = math.log2(math.e)
EXP2_SCALE = SCORE_SCALE * LOG2E


def mm_nn(a, b):
    return lax.dot_general(a, b, (((1,), (0,)), ((), ())), preferred_element_type=F32)


def mm_nt(a, b):
    return lax.dot_general(a, b, (((1,), (1,)), ((), ())), preferred_element_type=F32)


def mm_tn(a, b):
    return lax.dot_general(a, b, (((0,), (0,)), ((), ())), preferred_element_type=F32)


def fused_step(tokens, d_model, d_ff, heads):
    hd = d_model // heads
    seq_len = tokens * 8
    fixed = (seq_len // 2) // tokens
    class Group:
        def __init__(self, rows, cols, x_first, y_first, reduced=True):
            halves = len(x_first)
            self.x_first = x_first
            self.y_first = y_first
            self.rows, self.cols, self.halves = rows, cols, halves
            self.whole = (halves, 2, 2, 2, 2, 2, rows, cols)
            self.weight = vm(self.whole, BF16)
            if not reduced:
                return
            self.grad = vm(self.whole, BF16)
            one = (halves, 2, 2, 2, 2, rows, cols)
            two = (2, 2, 2, rows, cols)
            self.recv1 = vm(one, BF16)
            self.send2, self.recv2 = [vm(two, BF16) for _ in x_first], [vm(two, BF16) for _ in x_first]
            two = (2, 2, rows, cols)
            self.send3, self.recv3 = [vm(two, BF16) for _ in x_first], [vm(two, BF16) for _ in x_first]
            self.sum3 = vm((2, 2, halves, rows, cols), F32)
            one = (2, halves, rows, cols)
            self.send4, self.recv4, self.sum4 = vm(one, BF16), vm(one, BF16), vm(one, F32)
            self.send5, self.recv5 = vm(one[1:], BF16), vm(one[1:], BF16)

    chunk = d_ff // 4
    three = 3 * hd
    scratch = []
    count = [0]

    def take(number):
        first = count[0]
        count[0] += number
        return first

    def vm(shape, dtype):
        scratch.append(pltpu.VMEM(shape, dtype))
        return len(scratch) - 1

    def per_layer(shape, dtype):
        return [vm(shape, dtype) for _ in range(2)]

    g_qkv = Group(3 * d_model // 32, d_model // 2, (True, True), (True, False), reduced=False)
    g_out = Group(d_model // 32, d_model // 2, (False, False), (True, False))
    g_up = Group(d_ff // 32, d_model // 2, (True, True), (True, False))
    g_down = Group(d_model // 32, d_ff // 2, (True, True), (True, False))
    v_own = vm((d_model // 32, 128), BF16)
    v_all, v_send, v_recv = (vm((32, d_model // 32, 128), BF16) for _ in range(3))
    everything = (g_qkv, g_out, g_up, g_down)
    own_q, head_w = vm((3, 16, d_model), BF16), vm((3, 4, 16, d_model), BF16)
    head_g = vm((three, d_model), F32)
    tile_s, tile_r = vm((3, 4, 16, d_model), BF16), vm((3, 4, 16, d_model), BF16)
    s_all = per_layer((8, tokens, d_model), BF16)
    pack = vm((128, 16), F32)
    c_in = vm((tokens, d_model), BF16)
    p_out, p_in = vm((8, 128), jnp.int32), vm((8, 128), jnp.int32)
    o_send, i_send, i_recv = (vm((tokens, d_model), BF16) for _ in range(3))
    x32, h1_ = vm((d_model, tokens), F32), vm((d_model, tokens), F32)
    hlow = per_layer((d_model, tokens), BF16)
    xh1, xh2 = per_layer((d_model, tokens), F32), per_layer((d_model, tokens), F32)
    rs1, rs2 = per_layer((8, tokens), F32), per_layer((8, tokens), F32)
    slope, act = per_layer((d_ff, tokens), F32), per_layer((d_ff, tokens), BF16)
    lse, o32 = per_layer((8, 8, tokens), F32), per_layer((8, hd, tokens), F32)
    send1, send3 = vm((8, hd, tokens), BF16), vm((8, three, tokens), BF16)
    qr, ar = per_layer((8, three, tokens), BF16), per_layer((8, hd, tokens), BF16)
    dr, er = per_layer((8, hd, tokens), BF16), per_layer((8, three, tokens), BF16)
    g32, dh32 = vm((d_model, tokens), F32), vm((d_model, tokens), F32)
    dz_, dz2_ = vm((d_model, tokens), BF16), vm((d_model, tokens), BF16)
    kt, vt, qt, dt = (vm((seq_len, hd), BF16) for _ in range(4))
    dk, dv = vm((seq_len, hd), F32), vm((seq_len, hd), F32)
    df_ = vm((d_ff, tokens), BF16)
    gv = vm((d_model, 128), F32)

    def body(ins, outs, R, SS, RS, word):
        (in_ref, wqkv, wout, wup, wdown, biases, upb, norms, cot_ref, pref_ref) = ins
        (o_out, o_ig, o_qkv, o_gout, o_up, o_down, o_bias, o_upb, o_norms) = outs
        dp, sq = lax.axis_index("dp"), lax.axis_index("seq")
        x, c = dp // 2, dp % 2
        z, y = sq // 2, sq % 2
        zh, zl = z // 2, z % 2
        rank = 4 * c + 2 * zl + y

        def dev(x_, c_, z_, y_):
            return (x_ * 2 + c_, z_ * 2 + y_)

        def remote(src, dst, idx, device, arrival=None):
            return pltpu.make_async_remote_copy(
                src_ref=src,
                dst_ref=dst,
                send_sem=SS.at[idx],
                recv_sem=RS.at[idx if arrival is None else arrival],
                device_id=device,
                device_id_type=MESH,
            )

        def peer(k):
            c_ = (c + k // 4) % 2
            zl_ = (zl + (k // 2) % 2) % 2
            y_ = (y + k % 2) % 2
            return dev(x, c_, 2 * zh + zl_, y_), 4 * c_ + 2 * zl_ + y_

        sends = []

        barrier = pltpu.get_barrier_semaphore()
        swap_dev = dev(x, 1 - c, 2 * (1 - zh) + zl, y)
        me = dp * 8 + sq

        x_dev, zz_dev = dev(1 - x, c, z, y), dev(x, c, (z + 2) % 4, y)
        y_dev, z_dev, c_dev = dev(x, c, z, 1 - y), dev(x, c, 2 * zh + 1 - zl, y), dev(x, 1 - c, z, y)
        near = (x_dev, y_dev, z_dev, zz_dev, c_dev, swap_dev)
        for device in near:
            pl.semaphore_signal(barrier, inc=1, device_id=device, device_id_type=MESH)

        def all_in():
            for i, device in enumerate((c_dev, y_dev, z_dev, x_dev, zz_dev)):
                pl.semaphore_signal(word.at[i], inc=1, device_id=device, device_id_type=MESH)
                pl.semaphore_wait(word.at[i], 1)

        def place(n, value):
            for h in range(n.halves):
                R[n.weight][h, x, c, zh, zl, y] = value[:, h * n.cols : (h + 1) * n.cols]

        R[own_q][...] = wqkv[...].astype(BF16).reshape(3, 16, d_model)
        place(g_qkv, wqkv[...].astype(BF16))
        R[pack][0:4, :] = biases[...]
        R[pack][4:8, :] = norms[...]
        for b in range(4):
            R[pack][8 + b : 9 + b, :] = upb[:, 16 * b : 16 * (b + 1)]
        R[pack][12:128, :] = jnp.zeros((116, 16), F32)
        R[v_own][...] = R[pack][...].T.astype(BF16)
        R[p_out][...] = jnp.full((8, 128), pref_ref[0], jnp.int32)
        place(g_out, wout[...].astype(BF16))
        place(g_up, wup[...].astype(BF16))
        place(g_down, wdown[...].astype(BF16))
        pl.semaphore_wait(barrier, len(near))

        swapped = c != zh

        def swap(src, dst, idx):
            return remote(src, dst, idx, swap_dev)

        s_idx, s2_idx, c_idx, p_idx, so_idx, si_idx = (take(1) for _ in range(6))

        w_base, t_base = take(13), take(13)

        def head_of(i, block):
            t = 3 * me + i
            h = (t % 32) // 4
            device = dev(block // 2, h // 4, 2 * (block % 2) + (h // 2) % 2, h % 2)
            return t, device, (h == rank) & (block == 2 * x + zh)

        def owner_of(n):
            t = (n // 4) * 32 + 4 * rank + n % 4
            return t // 3, t % 3

        def weight_copy(n):
            i, block = n // 4, n % 4
            t, device, here = head_of(i, block)
            part, sub = t // 32, t % 4
            dst = R[head_w].at[part, sub]
            return remote(R[own_q].at[i], dst, w_base + n, device, w_base + 12), here, (i, part, sub)

        v_base = take(2)

        def whole_copy(name, i):
            return pltpu.make_async_copy(R[name], R[name], RS.at[i])

        def vec_out(i, carry):
            other = (me + i) % 32
            remote(R[v_own], R[v_all].at[me], v_base, (other // 8, other % 8)).start()
            return carry

        def vec_back(i, carry):
            other = (me + i) % 32
            remote(R[v_send].at[other], R[v_recv].at[me], v_base + 1, (other // 8, other % 8)).start()
            return carry

        def weight_send(n, carry):
            copy, here, (i, part, sub) = weight_copy(n)

            @pl.when(jnp.logical_not(here))
            def _():
                copy.start()

            @pl.when(here)
            def _():
                pltpu.make_async_copy(R[own_q].at[i], R[head_w].at[part, sub], RS.at[w_base + 12]).start()

            return carry

        def weight_wait(n, carry):
            copy, here, _ = weight_copy(n)

            @pl.when(jnp.logical_not(here))
            def _():
                copy.wait_send()

            return carry

        def tile_copy(n):
            owner, i = owner_of(n)
            block = 2 * x + zh
            src, dst = R[tile_s].at[n // 4, n % 4], R[tile_r].at[i, block]
            device = (owner // 8, owner % 8)
            return remote(src, dst, t_base + n, device, t_base + 12), owner == me, (i, block)

        def tile_send(n, carry):
            copy, here, (i, block) = tile_copy(n)

            @pl.when(jnp.logical_not(here))
            def _():
                copy.start()

            @pl.when(here)
            def _():
                pltpu.make_async_copy(R[tile_s].at[n // 4, n % 4], R[tile_r].at[i, block], RS.at[t_base + 12]).start()

            return carry

        def tile_wait(n, carry):
            copy, here, _ = tile_copy(n)

            @pl.when(jnp.logical_not(here))
            def _():
                copy.wait_send()

            return carry

        s_base = [take(13), take(13)]

        def rank_of(c_, zl_, y_):
            return 4 * c_ + 2 * zl_ + y_

        top, low_rows = slice(0, tokens // 2), slice(tokens // 2, tokens)

        def s_copy(l, i):
            py, pz, pd = rank_of(c, zl, 1 - y), rank_of(c, 1 - zl, y), rank_of(c, 1 - zl, 1 - y)
            r = R[s_all[l]]
            ref, device = (
                (r.at[rank, top], y_dev),
                (r.at[rank, low_rows], y_dev),
                (r.at[rank, low_rows], z_dev),
                (r.at[rank, top], z_dev),
                (r.at[rank], c_dev),
                (r.at[py, top], z_dev),
                (r.at[pz, low_rows], y_dev),
                (r.at[py, top], c_dev),
                (r.at[py, low_rows], c_dev),
                (r.at[pz, low_rows], c_dev),
                (r.at[pz, top], c_dev),
                (r.at[pd, top], c_dev),
                (r.at[pd, low_rows], c_dev),
            )[i]
            return remote(ref, ref, s_base[l] + i, device)

        def s_start(l, *which):
            for i in which:
                s_copy(l, i).start()

        def s_got(l, *which):
            for i in which:
                s_copy(l, i).wait_recv()

        own_rank = R[s_all[0]].at[rank]
        swap_rank = R[s_all[0]].at[rank_of(1 - c, zl, y)]

        def swap_rows(rows, idx):
            return swap(in_ref.at[rows], swap_rank.at[rows], idx)

        @pl.when(swapped)
        def _():
            swap_rows(top, s_idx).start()
            swap_rows(low_rows, s2_idx).start()
            swap(R[p_out], R[p_in], p_idx).start()

        @pl.when(jnp.logical_not(swapped))
        def _():
            own_rank[...] = in_ref[...]
            R[p_in][...] = R[p_out][...]

        ag = {}
        for n in everything:
            ag[n] = (take(2), take(2), take(2), take(1))

        def ag_z(n, _):
            own = R[n.weight].at[:, x, c, zh, zl, y]
            cp = remote(own, own, ag[n][0], zz_dev)
            cp.start()
            sends.append(cp)
            return [cp]

        def ag_zz(n, waits):
            waits[0].wait_recv()
            part = R[n.weight].at[:, x, c, :, zl, y]
            cp = remote(part, part, ag[n][0] + 1, z_dev)
            cp.start()
            sends.append(cp)
            return [cp]

        def ag_a(n, waits):
            waits[0].wait_recv()
            w = R[n.weight]
            cps = []
            for h in range(n.halves):
                part = w.at[h, x, c, :, :, y]
                cps.append(remote(part, part, ag[n][1] + h, y_dev if n.y_first[h] else x_dev))
                cps[-1].start()
            sends.extend(cps)
            return cps

        def ag_b(n, waits):
            w = R[n.weight]
            cps = []
            for h in range(n.halves):
                waits[h].wait_recv()
                part = w.at[h, x, c] if n.y_first[h] else w.at[h, :, c, :, :, y]
                cps.append(remote(part, part, ag[n][2] + h, x_dev if n.y_first[h] else y_dev))
                cps[-1].start()
            sends.extend(cps)
            return cps

        def ag_c(n, waits):
            for cp in waits:
                cp.wait_recv()
            part = R[n.weight].at[:, :, c]
            cp = remote(part, part, ag[n][3], c_dev)
            cp.start()
            sends.append(cp)
            return [cp]

        state = {}

        def step(stage, n):
            state[n] = stage(n, state.get(n))

        def arrived(n):
            for cp in state[n]:
                cp.wait_recv()


        @pl.when(jnp.logical_not(swapped))
        def _():
            s_start(0, 0, 2, 1, 3, 4)

        all_in()

        @pl.when(swapped)
        def _():
            swap_rows(top, s_idx).wait()
            s_start(0, 0, 3)
            swap_rows(low_rows, s2_idx).wait()
            s_start(0, 2, 1, 4)
            swap(R[p_out], R[p_in], p_idx).wait()

        step(ag_z, g_up)
        step(ag_z, g_out)
        lax.fori_loop(0, 12, weight_send, 0)
        pltpu.make_async_copy(R[v_own], R[v_all].at[me], RS.at[v_base]).start()
        lax.fori_loop(1, 32, vec_out, 0)
        s_got(0, 0)
        s_start(0, 5, 7)
        s_got(0, 2)
        s_start(0, 6, 9)
        s_got(0, 1)
        s_start(0, 8)
        s_got(0, 3)
        s_start(0, 10)
        step(ag_zz, g_up)
        step(ag_zz, g_out)
        step(ag_z, g_down)
        s_got(0, 5)
        s_start(0, 11)
        s_got(0, 6)
        s_start(0, 12)
        step(ag_a, g_up)
        step(ag_zz, g_down)
        step(ag_a, g_out)
        R[x32][...] = own_rank[...].T.astype(F32)
        s_got(0, 4, 7, 8, 9, 10, 11, 12)
        whole_copy(head_w, w_base + 12).wait()
        whole_copy(v_all, v_base).wait()

        def weight(n, h):
            return R[n.weight][h].reshape(32 * n.rows, n.cols)

        def vec(i):
            return R[v_all][:, :, i : i + 1].reshape(d_model, 1).astype(F32)

        def up_bias(i):
            lanes = [
                R[v_all][8 * i : 8 * (i + 1), :, 8 + b : 9 + b].reshape(8, 1, 16, 1).astype(F32)
                for b in range(4)
            ]
            return jnp.concatenate(lanes, axis=1).reshape(chunk, 1)

        def spread(src, dst):
            base = take(8)
            cps = []
            for k in range(1, 8):
                device, other = peer(k)
                cps.append(remote(src.at[other], dst.at[rank], base + k, device))
                cps[-1].start()
            dst[rank] = src[rank]
            return cps

        def batch(src, dst, base, core):
            def go(ks):
                for k in ks:
                    device, other = peer(k)
                    remote(src.at[other], dst.at[rank], base + k, device).start()

            @pl.when(c == core)
            def _():
                go(range(1, 4))
                dst[rank] = src[rank]

            @pl.when(c != core)
            def _():
                go(range(4, 8))

        def sent(src, dst, base):
            for k in range(1, 8):
                remote(src.at[0], dst.at[0], base + k, peer(k)[0]).wait()

        def finish(cps):
            for cp in cps:
                cp.wait()

        def ext(qb):
            return max(fixed, qb + 1)

        def span(first, last=None):
            return slice(first * tokens, (first + 1 if last is None else last) * tokens)

        def masked(s, qb):
            if qb < fixed:
                kk = lax.broadcasted_iota(jnp.int32, s.shape, 0)
                qq = qb * tokens + lax.broadcasted_iota(jnp.int32, s.shape, 1)
                return jnp.where((kk <= qq) | (kk < R[p_in][0:1, 0:1]), s, NEGATIVE)
            low = s[qb * tokens :]
            kk = lax.broadcasted_iota(jnp.int32, low.shape, 0)
            qq = lax.broadcasted_iota(jnp.int32, low.shape, 1)
            low = jnp.where(kk <= qq, low, NEGATIVE)
            return jnp.concatenate([s[: qb * tokens], low], axis=0)

        def norm(r, gain, shift):
            centre = r - jnp.mean(r, axis=0, keepdims=True)
            inv = lax.rsqrt(jnp.mean(centre * centre, axis=0, keepdims=True) + EPSILON)
            xh = centre * inv
            return xh * gain + shift, xh, inv

        def forward(l):
            rows_all, qkv_all = R[s_all[l]], R[qr[l]]
            if l == 1:
                s_start(1, 0, 2, 1, 3, 4)
                s_got(1, 0)
                s_start(1, 5, 7)
                s_got(1, 2)
                s_start(1, 6, 9)
                s_got(1, 1)
                s_start(1, 8)
                s_got(1, 3)
                s_start(1, 10)
                s_got(1, 5)
                s_start(1, 11)
                s_got(1, 6)
                s_start(1, 12)
                s_got(1, 4, 7, 8, 9, 10, 11, 12)
                step(ag_z, g_qkv)

                @pl.when(swapped)
                def _():
                    swap(cot_ref, R[c_in], c_idx).start()

            packed = R[v_all][pl.ds(4 * rank, 4)]
            packed = packed.reshape(hd, 128).astype(F32)
            bias = jnp.concatenate([packed[:, 0:1], jnp.zeros((hd, 1), F32), packed[:, 1:2]], axis=0)
            w = R[head_w][...].reshape(three, d_model)
            for b in range(8):
                qkv_all[b] = (mm_nt(w, rows_all[b]) + bias).astype(BF16)
            for b in range(8):
                R[kt][span(b), :] = qkv_all[b, hd : 2 * hd, :].T
                R[vt][span(b), :] = qkv_all[b, 2 * hd :, :].T
            base = take(8)
            for qb in range(8):
                n = ext(qb)
                s = masked(mm_nn(R[kt][span(0, n), :], qkv_all[qb, 0:hd, :]) * EXP2_SCALE, qb)
                m = jnp.max(s, axis=0, keepdims=True)
                p = jnp.exp2(s - m)
                total = jnp.sum(p, axis=0, keepdims=True)
                o = mm_tn(p.astype(BF16), R[vt][span(0, n), :]).T / total
                R[o32[l]][qb] = o
                R[send1][qb] = o.astype(BF16)
                R[lse[l]][qb] = jnp.broadcast_to(m + jnp.log2(total), (8, tokens))
                if qb == 3:
                    batch(R[send1], R[ar[l]], base, 0)
                if l == 0 and qb == 1:
                    step(ag_b, g_up)
                    step(ag_a, g_down)
                if l == 0 and qb == 4:
                    step(ag_b, g_out)
                if l == 1 and qb == 4:
                    step(ag_zz, g_qkv)
            batch(R[send1], R[ar[l]], base, 1)
            if l == 0:
                step(ag_b, g_down)
                step(ag_c, g_up)
                step(ag_c, g_out)
                lax.fori_loop(0, 12, weight_wait, 0)
            sent(R[send1], R[ar[l]], base)
            if l == 1:
                step(ag_a, g_qkv)
            if l == 0:
                arrived(g_out)
            att = R[ar[l]][...].reshape(d_model, tokens)
            half = d_model // 2
            r1 = R[x32][...] + vec(2)
            r1 = r1 + mm_nn(weight(g_out, 0), att[:half]) + mm_nn(weight(g_out, 1), att[half:])
            h1, xh, inv = norm(r1, vec(4), vec(5))
            R[h1_][...] = h1
            R[xh1[l]][...] = xh
            R[rs1[l]][...] = jnp.broadcast_to(inv, (8, tokens))
            R[hlow[l]][...] = h1.astype(BF16)
            if l == 0:
                arrived(g_up)
            for i in range(4):
                rows = slice(i * chunk, (i + 1) * chunk)
                g = g_up
                f = up_bias(i)
                for h in range(2):
                    w = R[g_up.weight][h, i // 2, i % 2].reshape(chunk, g.cols)
                    f = f + mm_nn(w, R[hlow[l]][h * half : (h + 1) * half, :])
                cdf = 0.5 * (1.0 + lax.erf(f * ROOT_HALF))
                R[act[l]][rows, :] = (f * cdf).astype(BF16)
                R[slope[l]][rows, :] = cdf + f * (jnp.exp(-0.5 * f * f) * DENSITY_SCALE)
            if l == 0:
                step(ag_c, g_down)
                arrived(g_down)
            r2 = R[h1_][...] + vec(3)
            for h in range(2):
                r2 = r2 + mm_nn(weight(g_down, h), R[act[l]][h * d_ff // 2 : (h + 1) * d_ff // 2, :])
            out, xh, inv = norm(r2, vec(6), vec(7))
            R[xh2[l]][...] = xh
            R[rs2[l]][...] = jnp.broadcast_to(inv, (8, tokens))
            return out

        idx = {n: (take(1), take(2), take(2), take(2)) for n in everything[1:]}

        def rs_c(n, _):
            cp = remote(R[n.grad].at[:, :, 1 - c], R[n.recv1], idx[n][0], c_dev)
            cp.start()
            sends.append(cp)
            return [cp]

        def a_send(n, h):
            g_, r1 = R[n.grad], R[n.recv1]
            if n.x_first[h]:
                value, device = g_[h, 1 - x, c].astype(F32) + r1[h, 1 - x].astype(F32), x_dev
            else:
                value, device = g_[h, :, c, :, :, 1 - y].astype(F32) + r1[h, :, :, :, 1 - y].astype(F32), y_dev
            R[n.send2[h]][...] = value.astype(BF16)
            cp = remote(R[n.send2[h]], R[n.recv2[h]], idx[n][1] + h, device)
            cp.start()
            sends.append(cp)
            return cp

        def rs_a_first(n, waits):
            waits[0].wait_recv()
            return [a_send(n, 0)]

        def rs_a_second(n, waits):
            return waits + [a_send(n, 1)]

        def rs_a(n, waits):
            waits = rs_a_first(n, waits)
            return rs_a_second(n, waits) if n.halves == 2 else waits

        def rs_b(n, waits):
            g_, r1 = R[n.grad], R[n.recv1]
            cps = []
            for h in range(n.halves):
                waits[h].wait_recv()
                r2 = R[n.recv2[h]]
                if n.x_first[h]:
                    value, device = g_[h, x, c, :, :, 1 - y].astype(F32) + r1[h, x, :, :, 1 - y].astype(F32), y_dev
                    value = value + r2[:, :, 1 - y].astype(F32)
                else:
                    value, device = g_[h, 1 - x, c, :, :, y].astype(F32) + r1[h, 1 - x, :, :, y].astype(F32), x_dev
                    value = value + r2[1 - x].astype(F32)
                R[n.send3[h]][...] = value.astype(BF16)
                cps.append(remote(R[n.send3[h]], R[n.recv3[h]], idx[n][2] + h, device))
                cps[-1].start()
            sends.extend(cps)
            return cps

        def rs_z(n, waits):
            g_, r1, sum3 = R[n.grad], R[n.recv1], R[n.sum3]
            for h in range(n.halves):
                waits[h].wait_recv()
                r2 = R[n.recv2[h]]
                kept = r2[:, :, y] if n.x_first[h] else r2[x]
                sum3[:, :, h] = (
                    g_[h, x, c, :, :, y].astype(F32)
                    + r1[h, x, :, :, y].astype(F32)
                    + kept.astype(F32)
                    + R[n.recv3[h]][...].astype(F32)
                )
            R[n.send4][...] = sum3[:, 1 - zl].astype(BF16)
            cp = remote(R[n.send4], R[n.recv4], idx[n][3], z_dev)
            cp.start()
            sends.append(cp)
            return [cp]

        def rs_zz(n, waits):
            waits[0].wait_recv()
            R[n.sum4][...] = R[n.sum3][:, zl] + R[n.recv4][...].astype(F32)
            R[n.send5][...] = R[n.sum4][1 - zh].astype(BF16)
            cp = remote(R[n.send5], R[n.recv5], idx[n][3] + 1, zz_dev)
            cp.start()
            sends.append(cp)
            return [cp]

        def rs_end(n, waits):
            waits[0].wait_recv()
            return R[n.sum4][zh] + R[n.recv5][...].astype(F32)

        def pick(lane, count_=1):
            rows = lax.broadcasted_iota(jnp.int32, (128, tokens), 0)
            return jnp.where((rows >= lane) & (rows < lane + count_), 1.0, 0.0).astype(BF16)

        def low_sum(lane, value):
            return mm_nt(value, pick(lane))

        def full_sum(lane, value):
            high = value.astype(BF16)
            return low_sum(lane, high) + low_sum(lane, (value - high.astype(F32)).astype(BF16))

        def add_grad(n, h, value, l):
            value = value.reshape(n.whole[1:])
            if l == 0:
                value = value + R[n.grad][h].astype(F32)
            R[n.grad][h] = value.astype(BF16)

        def norm_grad(g, xh, inv, gain):
            s = g * gain
            return inv * (
                s - jnp.mean(s, axis=0, keepdims=True) - xh * jnp.mean(s * xh, axis=0, keepdims=True)
            )

        half = d_model // 2

        def out_grad(l):
            att = R[ar[l]][...].reshape(d_model, tokens)
            for h in range(2):
                add_grad(g_out, h, mm_nt(R[dz_][...], att[h * half : (h + 1) * half]), l)

        def up_grad(l):
            for h in range(2):
                add_grad(g_up, h, mm_nt(R[df_][...], R[hlow[l]][h * half : (h + 1) * half, :]), l)

        def down_grad(l):
            for h in range(2):
                add_grad(g_down, h, mm_nt(R[dz2_][...], R[act[l]][h * d_ff // 2 : (h + 1) * d_ff // 2, :]), l)

        def head_grad(l):
            rows_all, back = R[s_all[l]], R[send3]
            t = mm_nn(back[0], rows_all[0])
            sums = low_sum(0, back[0, 0:hd]) + low_sum(1, back[0, 2 * hd :])
            for b in range(1, 8):
                t = t + mm_nn(back[b], rows_all[b])
                sums = sums + low_sum(0, back[b, 0:hd]) + low_sum(1, back[b, 2 * hd :])
            R[gv][pl.ds(pl.multiple_of(rank * hd, hd), hd), :] += sums
            if l == 1:
                R[head_g][...] = t
            else:
                R[tile_s][...] = (R[head_g][...] + t).astype(BF16).reshape(3, 4, 16, d_model)

        def dense_sums(l):
            t = full_sum(6, R[g32][...] * R[xh2[l]][...]) + full_sum(7, R[g32][...])
            t = t + full_sum(4, R[dh32][...] * R[xh1[l]][...]) + full_sum(5, R[dh32][...])
            t = t + low_sum(3, R[dz2_][...]) + low_sum(2, R[dz_][...])
            R[gv][...] += t
            ones = pick(8, 4)
            lanes = lax.broadcasted_iota(jnp.int32, (8, 16, 128), 2)
            for i in range(4):
                sums = mm_nt(R[df_][i * chunk : (i + 1) * chunk, :], ones).reshape(8, 4, 16, 128)
                t = jnp.where(lanes == 8, sums[:, 0], 0.0)
                for b in range(1, 4):
                    t = jnp.where(lanes == 8 + b, sums[:, b], t)
                R[gv][i * 128 : (i + 1) * 128, :] += t.reshape(128, 128)

        def backward(l):
            dr2 = norm_grad(R[g32][...], R[xh2[l]][...], R[rs2[l]][0:1, :], vec(6))
            R[dz2_][...] = dr2.astype(BF16)
            R[x32][...] = dr2
            if l == 0:
                down_grad(l)
                step(rs_c, g_down)
            for i in range(4):
                rows = slice(i * chunk, (i + 1) * chunk)
                h, lo = i // 2, (i % 2) * chunk
                w = R[g_down.weight][h].reshape(d_model, d_ff // 2)[:, lo : lo + chunk]
                R[df_][rows, :] = (mm_tn(w, R[dz2_][...]) * R[slope[l]][rows, :]).astype(BF16)
            if l == 0:
                step(rs_a, g_down)
                up_grad(l)
                step(rs_c, g_up)
            for h in range(2):
                rows = slice(h * half, (h + 1) * half)
                R[dh32][rows, :] = R[x32][rows, :] + mm_tn(weight(g_up, h), R[df_][...])
            dr1 = norm_grad(R[dh32][...], R[xh1[l]][...], R[rs1[l]][0:1, :], vec(4))
            R[dz_][...] = dr1.astype(BF16)
            R[x32][...] = dr1
            for h in range(2):
                datt = mm_tn(weight(g_out, h), R[dz_][...]).astype(BF16)
                R[send1][h * 4 : (h + 1) * 4] = datt.reshape(4, hd, tokens)
            cps = spread(R[send1], R[dr[l]])
            if l == 1:
                down_grad(l)
                up_grad(l)
            else:
                step(rs_a_first, g_up)
            out_grad(l)
            if l == 0:
                step(rs_c, g_out)
            dense_sums(l)
            finish(cps)
            if l == 0:
                step(rs_a_second, g_up)
                step(rs_a, g_out)
            else:
                step(ag_b, g_qkv)

                @pl.when(swapped)
                def _():
                    swap(R[o_send], o_out, so_idx).start()

            qkv_all, datt_all = R[qr[l]], R[dr[l]]
            for b in range(8):
                R[qt][span(b), :] = qkv_all[b, 0:hd, :].T
                R[kt][span(b), :] = qkv_all[b, hd : 2 * hd, :].T
                R[vt][span(b), :] = qkv_all[b, 2 * hd :, :].T
                R[dt][span(b), :] = datt_all[b].T
            R[dk][...] = jnp.zeros((seq_len, hd), F32)
            R[dv][...] = jnp.zeros((seq_len, hd), F32)
            base = take(8)
            src, dst = R[send3], R[er[l]]

            def keys_out(b):
                src[b, hd : 2 * hd, :] = (R[dk][span(b), :] * SCORE_SCALE).T.astype(BF16)
                src[b, 2 * hd :, :] = R[dv][span(b), :].T.astype(BF16)

            for qb in range(7, -1, -1):
                n = ext(qb)
                keys = span(0, n)
                delta = jnp.sum(datt_all[qb].astype(F32) * R[o32[l]][qb], axis=0, keepdims=True)
                s = masked(mm_nn(R[kt][keys, :], qkv_all[qb, 0:hd, :]) * EXP2_SCALE, qb)
                p = jnp.exp2(s - R[lse[l]][qb, 0:1, :])
                dprob = mm_nn(R[vt][keys, :], datt_all[qb])
                dsc = (p * (dprob - delta)).astype(BF16)
                R[dv][keys, :] += mm_nn(p.astype(BF16), R[dt][span(qb), :])
                R[dk][keys, :] += mm_nn(dsc, R[qt][span(qb), :])
                src[qb, 0:hd, :] = (mm_tn(R[kt][keys, :], dsc) * SCORE_SCALE).astype(BF16)
                if qb == 4:
                    for b in range(4, 8):
                        keys_out(b)
                    batch(src, dst, base, 1)
            for b in range(4):
                keys_out(b)
            batch(src, dst, base, 0)
            if l == 1:
                step(ag_c, g_qkv)
            head_grad(l)
            if l == 0:
                lax.fori_loop(0, 12, tile_send, 0)
                R[v_send][...] = R[gv][...].astype(BF16).reshape(32, 16, 128)
                pltpu.make_async_copy(R[v_send].at[me], R[v_recv].at[me], RS.at[v_base + 1]).start()
                lax.fori_loop(1, 32, vec_back, 0)
                step(rs_b, g_down)
            else:
                arrived(g_qkv)
            sent(src, dst, base)
            back = R[er[l]]
            for h in range(2):
                w = weight(g_qkv, h)
                t = R[x32][h * half : (h + 1) * half, :]
                for part in range(3):
                    grad = back[:, part * hd : (part + 1) * hd, :].reshape(d_model, tokens)
                    t = t + mm_tn(w[part * d_model : (part + 1) * d_model], grad)
                R[g32][h * half : (h + 1) * half, :] = t

        mid = forward(0)
        R[x32][...] = mid
        R[s_all[1]][rank] = mid.astype(BF16).T
        last = forward(1)
        R[o_send][...] = last.astype(BF16).T

        @pl.when(swapped)
        def _():
            swap(cot_ref, R[c_in], c_idx).wait()

        @pl.when(jnp.logical_not(swapped))
        def _():
            o_out[...] = R[o_send][...]
            R[c_in][...] = cot_ref[...]

        R[gv][...] = jnp.zeros((d_model, 128), F32)
        R[g32][...] = R[c_in][...].T.astype(F32)
        backward(1)
        backward(0)
        R[i_send][...] = R[g32][...].astype(BF16).T

        @pl.when(swapped)
        def _():
            swap(R[i_send], R[i_recv], si_idx).start()

        @pl.when(jnp.logical_not(swapped))
        def _():
            o_ig[...] = R[g32][...].T

        step(rs_b, g_out)
        step(rs_z, g_down)
        step(rs_b, g_up)
        step(rs_z, g_out)
        step(rs_zz, g_down)
        step(rs_z, g_up)
        step(rs_zz, g_out)
        step(rs_zz, g_up)
        whole_copy(tile_r, t_base + 12).wait()
        lax.fori_loop(0, 12, tile_wait, 0)
        t = R[tile_r][:, 0].astype(F32)
        for block in range(1, 4):
            t = t + R[tile_r][:, block].astype(F32)
        o_qkv[...] = t.reshape(48, d_model)
        for n, ref in ((g_down, o_down), (g_up, o_up), (g_out, o_gout)):
            t = rs_end(n, state[n])
            ref[...] = jnp.concatenate([t[0], t[1]], axis=1)
        whole_copy(v_recv, v_base + 1).wait()
        t = R[v_recv][0].astype(F32)
        for i in range(1, 32):
            t = t + R[v_recv][i].astype(F32)
        t = t.T
        o_bias[...] = t[0:4]
        o_norms[...] = t[4:8]
        o_upb[...] = jnp.concatenate([t[8 + b : 9 + b] for b in range(4)], axis=1)

        @pl.when(swapped)
        def _():
            swap(R[o_send], o_out, so_idx).wait()
            swap(R[i_send], R[i_recv], si_idx).wait()
            o_ig[...] = R[i_recv][...].astype(F32)

        for cp in sends:
            cp.wait_send()
        for i in range(2):
            sent_vec = R[v_recv].at[0:31]
            pltpu.make_async_copy(sent_vec, sent_vec, SS.at[v_base + i]).wait()
        for l in range(2):
            for i in range(13):
                s_copy(l, i).wait_send()

    n_sems = 6 + 2 * 13 + 2 * 13 + 2 + 4 * 7 + 6 * 8 + 3 * 7

    def kernel(*refs):
        count[0] = 0
        body(refs[:10], refs[10:19], refs[19:-3], refs[-3], refs[-2], refs[-1])
        assert count[0] <= n_sems

    def hand_on(*refs):
        for src, dst in zip(refs[:9], refs[9:]):
            dst[...] = src[...]

    def call(inputs, qkv_w, out_w, up_w, down_w, biases, up_bias, norms, cotangent, prefix):
        weights = [w.T for w in (qkv_w, out_w, up_w, down_w)]
        small = [biases, up_bias.reshape(1, -1), norms]
        out_shape = (
            jax.ShapeDtypeStruct((tokens, d_model), BF16),
            jax.ShapeDtypeStruct((tokens, d_model), F32),
            *(jax.ShapeDtypeStruct(w.shape, F32) for w in weights + small),
        )
        vmem = pl.BlockSpec(memory_space=pltpu.VMEM)
        results = pl.pallas_call(
            kernel,
            out_shape=out_shape,
            in_specs=[vmem] * 9 + [pl.BlockSpec(memory_space=pltpu.SMEM)],
            out_specs=[vmem] * 9,
            scratch_shapes=[
                *scratch,
                pltpu.SemaphoreType.DMA((n_sems,)),
                pltpu.SemaphoreType.DMA((n_sems,)),
                pltpu.SemaphoreType.REGULAR((5,)),
            ],
            compiler_params=pltpu.CompilerParams(
                collective_id=0, has_side_effects=True, vmem_limit_bytes=62 * 2**20
            ),
        )(inputs, *weights, *small, cotangent, prefix)
        results = pl.pallas_call(
            hand_on, out_shape=out_shape, in_specs=[vmem] * 9, out_specs=[vmem] * 9
        )(*results)
        back = [w.T for w in results[2:6]]
        return (*results[:2], *back, results[6], results[7].reshape(up_bias.shape), results[8])

    return call


def fused_fits(mesh, args):
    if tuple(mesh.shape.items()) != (("dp", 4), ("seq", 8)) or HEADS != 8:
        return False
    total, d_model = args[0].shape
    d_ff = args[3].shape[1]
    return total % (32 * 128) == 0 and total // 32 == 256 and d_model == 512 and d_ff == 2048


def solution(mesh):
    specs = dict(
        mesh=mesh,
        in_specs=(
            P(("dp", "seq"), None),
            P(None, ("dp", "seq")),
            P(None, ("dp", "seq")),
            P(None, ("dp", "seq")),
            P(None, ("dp", "seq")),
            P(None, ("dp", "seq")),
            P(("dp", "seq")),
            P(None, ("dp", "seq")),
            P(("dp", "seq"), None),
            P("dp"),
        ),
        out_specs=(
            P(("dp", "seq"), None),
            P(("dp", "seq"), None),
            P(None, ("dp", "seq")),
            P(None, ("dp", "seq")),
            P(None, ("dp", "seq")),
            P(None, ("dp", "seq")),
            P(None, ("dp", "seq")),
            P(("dp", "seq")),
            P(None, ("dp", "seq")),
        ),
        check_vma=False,
    )

    def run(*args):
        if fused_fits(mesh, args):
            d_model = args[0].shape[1]
            step = fused_step(args[0].shape[0] // 32, d_model, args[3].shape[1], HEADS)
            return jax.shard_map(step, **specs)(*args)
        return jax.shard_map(local, **specs)(*args)

    return run
```

```python
import math

import jax
import jax.numpy as jnp
from jax import lax
from jax.experimental import pallas as pl
from jax.experimental.pallas import tpu as pltpu
from jax.sharding import PartitionSpec as P

HEADS = 8


EPSILON = 1e-05
NEGATIVE = -1e30
SCORE_SCALE = 0.125
ROOT_HALF = 1.0 / math.sqrt(2.0)
DENSITY_SCALE = 1.0 / math.sqrt(2.0 * math.pi)


def dot_rows(first_op, second_op):
    return lax.dot_general(
        first_op, second_op, (((1,), (1,)), ((), ())), preferred_element_type=jnp.float32
    )


def dot_cols(first_op, second_op):
    return lax.dot_general(
        first_op, second_op, (((0,), (0,)), ((), ())), preferred_element_type=jnp.float32
    )


def split_heads(tensor_in):
    return tensor_in.reshape(tensor_in.shape[0], HEADS, -1).transpose(1, 0, 2)


def merge_heads(stacked):
    return stacked.transpose(1, 0, 2).reshape(stacked.shape[1], -1)


def cast_all(masters):
    return tuple((tensor.astype(jnp.bfloat16) for tensor in masters))


def fetch_forward(masters):
    casted = cast_all(masters)
    return (
        lax.all_gather(casted[0], ("dp", "seq"), axis=1, tiled=True),
        lax.all_gather(casted[1], ("dp", "seq"), axis=1, tiled=True),
        lax.all_gather(casted[2], ("dp", "seq"), axis=1, tiled=True),
        lax.all_gather(casted[3], ("dp", "seq"), axis=1, tiled=True),
        lax.all_gather(casted[4], ("dp", "seq"), axis=1, tiled=True),
        lax.all_gather(casted[5], ("dp", "seq"), axis=0, tiled=True),
        lax.all_gather(casted[6], ("dp", "seq"), axis=1, tiled=True),
    )


def fetch_backward(masters):
    casted = cast_all(masters)
    return (
        lax.all_gather(casted[0], ("dp", "seq"), axis=1, tiled=True),
        lax.all_gather(casted[1], ("dp", "seq"), axis=1, tiled=True),
        lax.all_gather(casted[2], ("dp", "seq"), axis=1, tiled=True),
        lax.all_gather(casted[3], ("dp", "seq"), axis=1, tiled=True),
        lax.all_gather(casted[4], ("dp", "seq"), axis=1, tiled=True),
        lax.all_gather(casted[5], ("dp", "seq"), axis=0, tiled=True),
        lax.all_gather(casted[6], ("dp", "seq"), axis=1, tiled=True),
    )


def gelu_slope(values):
    normal_cdf = 0.5 * (1.0 + jax.scipy.special.erf(values * ROOT_HALF))
    return normal_cdf + values * jnp.exp(-0.5 * values * values) * DENSITY_SCALE


def layer_norm(values, gain_vec, shift_vec):
    centre = values - jnp.mean(values, axis=1, keepdims=True)
    inv_std = lax.rsqrt(jnp.mean(centre * centre, axis=1, keepdims=True) + EPSILON)
    centred = centre * inv_std
    return (centred * gain_vec + shift_vec, centred, inv_std)


def norm_back(grad_out, centred, inv_std, gain_vec):
    scaled = grad_out * gain_vec
    grad_gain = jnp.sum(grad_out * centred, axis=0)
    grad_shift = jnp.sum(grad_out, axis=0)
    grad_in = inv_std * (
        scaled
        - jnp.mean(scaled, axis=1, keepdims=True)
        - centred * jnp.mean(scaled * centred, axis=1, keepdims=True)
    )
    return (grad_in, grad_gain, grad_shift)


def attend_forward(queries, gathered, visible):
    features = queries.shape[1]
    head_q = split_heads(queries)
    head_k = split_heads(gathered[:, :features])
    head_v = split_heads(gathered[:, features:])

    def one_head(members):
        head_query, head_keys, head_values = members
        scores = jnp.where(visible, dot_rows(head_query, head_keys) * SCORE_SCALE, NEGATIVE)
        largest = jnp.max(scores, axis=1, keepdims=True)
        exponent = jnp.exp(scores - largest)
        row_total = jnp.sum(exponent, axis=1, keepdims=True)
        probability = (exponent / row_total).astype(jnp.bfloat16)
        head_out = jnp.dot(probability, head_values, preferred_element_type=jnp.float32)
        return (head_out, (largest + jnp.log(row_total))[:, 0])

    head_outs, log_totals = lax.map(one_head, (head_q, head_k, head_v))
    return (merge_heads(head_outs), log_totals)


def attend_backward(queries, gathered, visible, grad_att, log_totals):
    features = queries.shape[1]
    head_q = split_heads(queries)
    head_k = split_heads(gathered[:, :features])
    head_v = split_heads(gathered[:, features:])
    head_g = split_heads(grad_att)

    def one_head(members):
        head_query, head_keys, head_values, head_grad, head_logs = members
        scores = jnp.where(visible, dot_rows(head_query, head_keys) * SCORE_SCALE, NEGATIVE)
        probability = jnp.exp(scores - head_logs[:, None])
        grad_prob = dot_rows(head_grad, head_values)
        row_delta = jnp.sum(probability * grad_prob, axis=1)
        grad_score = (probability * (grad_prob - row_delta[:, None])).astype(jnp.bfloat16)
        grad_query = (
            jnp.dot(grad_score, head_keys, preferred_element_type=jnp.float32) * SCORE_SCALE
        )
        grad_keys = dot_cols(grad_score, head_query) * SCORE_SCALE
        grad_values = dot_cols(probability.astype(jnp.bfloat16), head_grad)
        return (grad_query, grad_keys, grad_values)

    results = lax.map(one_head, (head_q, head_k, head_v, head_g, log_totals))
    grad_query = merge_heads(results[0])
    return (grad_query, jnp.concatenate([merge_heads(results[1]), merge_heads(results[2])], axis=1))


def layer_forward(stream, weights, visible):
    w_qkv, w_out, w_up, w_down, vec_bias, b_up, vec_norm = weights
    vec_bias = vec_bias.astype(jnp.float32)
    b_up = b_up.astype(jnp.float32)
    vec_norm = vec_norm.astype(jnp.float32)
    features = stream.shape[1]
    stream_low = stream.astype(jnp.bfloat16)
    bias_row = jnp.concatenate([vec_bias[0], jnp.zeros_like(vec_bias[0]), vec_bias[1]])
    qkv = (jnp.dot(stream_low, w_qkv, preferred_element_type=jnp.float32) + bias_row).astype(
        jnp.bfloat16
    )
    queries = qkv[:, :features]
    local_kv = qkv[:, features:]
    gathered = lax.all_gather(local_kv, "seq", axis=0, tiled=True)
    attended, log_totals = attend_forward(queries, gathered, visible)
    att_low = attended.astype(jnp.bfloat16)
    branch = jnp.dot(att_low, w_out, preferred_element_type=jnp.float32) + vec_bias[2]
    normed, centred_one, inv_std_one = layer_norm(stream + branch, vec_norm[0], vec_norm[1])
    normed_low = normed.astype(jnp.bfloat16)
    hidden = jnp.dot(normed_low, w_up, preferred_element_type=jnp.float32) + b_up
    active = jax.nn.gelu(hidden, approximate=False).astype(jnp.bfloat16)
    second = jnp.dot(active, w_down, preferred_element_type=jnp.float32) + vec_bias[3]
    result, centred_two, inv_std_two = layer_norm(normed + second, vec_norm[2], vec_norm[3])
    cache = (
        stream_low,
        queries,
        local_kv,
        None,
        att_low,
        log_totals,
        centred_one,
        inv_std_one,
        normed_low,
        hidden,
        active,
        centred_two,
        inv_std_two,
    )
    return (result, cache)


def layer_backward(gradient, cache, weights, visible):
    w_qkv, w_out, w_up, w_down, vec_bias, b_up, vec_norm = weights
    vec_norm = vec_norm.astype(jnp.float32)
    (
        stream_low,
        queries,
        local_kv,
        kept_kv,
        att_low,
        log_totals,
        centred_one,
        inv_std_one,
        normed_low,
        hidden,
        active,
        centred_two,
        inv_std_two,
    ) = cache
    features = queries.shape[1]
    gathered = lax.all_gather(local_kv, "seq", axis=0, tiled=True)
    grad_two, gain_two, shift_two = norm_back(gradient, centred_two, inv_std_two, vec_norm[2])
    grad_second = grad_two.astype(jnp.bfloat16)
    bias_down = jnp.sum(grad_second.astype(jnp.float32), axis=0)
    grad_w_down = dot_cols(active, grad_second)
    grad_active = dot_rows(grad_second, w_down)
    grad_hidden = (grad_active * gelu_slope(hidden)).astype(jnp.bfloat16)
    bias_upper = jnp.sum(grad_hidden.astype(jnp.float32), axis=0)
    grad_w_up = dot_cols(normed_low, grad_hidden)
    grad_normed = grad_two + dot_rows(grad_hidden, w_up)
    grad_one, gain_one, shift_one = norm_back(grad_normed, centred_one, inv_std_one, vec_norm[0])
    grad_branch = grad_one.astype(jnp.bfloat16)
    bias_output = jnp.sum(grad_branch.astype(jnp.float32), axis=0)
    grad_w_out = dot_cols(att_low, grad_branch)
    grad_att = dot_rows(grad_branch, w_out).astype(jnp.bfloat16)
    grad_query, kv_terms = attend_backward(queries, gathered, visible, grad_att, log_totals)
    kv_grad = lax.psum_scatter(
        kv_terms.astype(jnp.bfloat16), "seq", scatter_dimension=0, tiled=True
    ).astype(jnp.float32)
    grad_qkv = jnp.concatenate([grad_query, kv_grad], axis=1).astype(jnp.bfloat16)
    qkv_sums = jnp.sum(grad_qkv.astype(jnp.float32), axis=0)
    grad_w_qkv = dot_cols(stream_low, grad_qkv)
    grad_stream = grad_one + dot_rows(grad_qkv, w_qkv)
    grad_bias = jnp.stack([qkv_sums[:features], qkv_sums[2 * features :], bias_output, bias_down])
    grad_norm = jnp.stack([gain_one, shift_one, gain_two, shift_two])
    return (
        grad_stream,
        (grad_w_qkv, grad_w_out, grad_w_up, grad_w_down, grad_bias, bias_upper, grad_norm),
    )


def local(
    inputs,
    qkv_weight,
    out_weight,
    up_weight,
    down_weight,
    biases,
    up_bias,
    norms,
    cotangent,
    prefix,
):
    masters = (qkv_weight, out_weight, up_weight, down_weight, biases, up_bias, norms)
    row_count = inputs.shape[0]
    key_count = row_count * lax.axis_size("seq")
    rows_here = lax.axis_index("seq") * row_count + jnp.arange(row_count, dtype=jnp.int32)
    all_index = jnp.arange(key_count, dtype=jnp.int32)
    visible = (all_index[None, :] <= rows_here[:, None]) | (all_index[None, :] < prefix[0])
    stream = inputs.astype(jnp.float32)
    caches = []
    for position in range(2):
        weights = fetch_forward(masters)
        stream, cache = layer_forward(stream, weights, visible)
        caches.append(cache)
    gradient = cotangent.astype(jnp.float32)
    accumulated = None
    for position in range(2):
        weights = fetch_backward(masters)
        gradient, grad_parts = layer_backward(gradient, caches[1 - position], weights, visible)
        if accumulated is None:
            accumulated = grad_parts
        else:
            accumulated = tuple((prior + fresh for prior, fresh in zip(accumulated, grad_parts)))
    reduced = (
        lax.psum_scatter(accumulated[0], ("dp", "seq"), scatter_dimension=1, tiled=True),
        lax.psum_scatter(accumulated[1], ("dp", "seq"), scatter_dimension=1, tiled=True),
        lax.psum_scatter(accumulated[2], ("dp", "seq"), scatter_dimension=1, tiled=True),
        lax.psum_scatter(accumulated[3], ("dp", "seq"), scatter_dimension=1, tiled=True),
        lax.psum_scatter(accumulated[4], ("dp", "seq"), scatter_dimension=1, tiled=True),
        lax.psum_scatter(accumulated[5], ("dp", "seq"), scatter_dimension=0, tiled=True),
        lax.psum_scatter(accumulated[6], ("dp", "seq"), scatter_dimension=1, tiled=True),
    )
    return (
        stream.astype(jnp.bfloat16),
        gradient,
        reduced[0],
        reduced[1],
        reduced[2],
        reduced[3],
        reduced[4],
        reduced[5],
        reduced[6],
    )


F32 = jnp.float32
BF16 = jnp.bfloat16
MESH = pl.DeviceIdType.MESH
LOG2E = math.log2(math.e)
EXP2_SCALE = SCORE_SCALE * LOG2E


def mm_nn(a, b):
    return lax.dot_general(a, b, (((1,), (0,)), ((), ())), preferred_element_type=F32)


def mm_nt(a, b):
    return lax.dot_general(a, b, (((1,), (1,)), ((), ())), preferred_element_type=F32)


def mm_tn(a, b):
    return lax.dot_general(a, b, (((0,), (0,)), ((), ())), preferred_element_type=F32)


def fused_step(tokens, d_model, d_ff, heads):
    hd = d_model // heads
    seq_len = tokens * 8
    fixed = (seq_len // 2) // tokens
    class Group:
        def __init__(self, rows, cols, x_first, y_first, reduced=True):
            halves = len(x_first)
            self.x_first = x_first
            self.y_first = y_first
            self.rows, self.cols, self.halves = rows, cols, halves
            self.whole = (halves, 2, 2, 2, 2, 2, rows, cols)
            self.weight = vm(self.whole, BF16)
            if not reduced:
                return
            self.grad = vm(self.whole, BF16)
            one = (halves, 2, 2, 2, 2, rows, cols)
            two = (2, 2, 2, rows, cols)
            self.recv1 = vm(one, BF16)
            self.send2, self.recv2 = [vm(two, BF16) for _ in x_first], [vm(two, BF16) for _ in x_first]
            two = (2, 2, rows, cols)
            self.send3, self.recv3 = [vm(two, BF16) for _ in x_first], [vm(two, BF16) for _ in x_first]
            self.sum3 = vm((2, 2, halves, rows, cols), F32)
            one = (2, halves, rows, cols)
            self.send4, self.recv4, self.sum4 = vm(one, BF16), vm(one, BF16), vm(one, F32)
            self.send5, self.recv5 = vm(one[1:], BF16), vm(one[1:], BF16)

    chunk = d_ff // 4
    three = 3 * hd
    scratch = []
    count = [0]

    def take(number):
        first = count[0]
        count[0] += number
        return first

    def vm(shape, dtype):
        scratch.append(pltpu.VMEM(shape, dtype))
        return len(scratch) - 1

    def per_layer(shape, dtype):
        return [vm(shape, dtype) for _ in range(2)]

    g_qkv = Group(3 * d_model // 32, d_model // 2, (True, True), (True, False), reduced=False)
    g_out = Group(d_model // 32, d_model // 2, (False, False), (True, False))
    g_up = Group(d_ff // 32, d_model // 2, (True, True), (True, False))
    g_down = Group(d_model // 32, d_ff // 2, (True, True), (True, False))
    v_own = vm((d_model // 32, 128), BF16)
    v_all, v_send, v_recv = (vm((32, d_model // 32, 128), BF16) for _ in range(3))
    everything = (g_qkv, g_out, g_up, g_down)
    own_q, head_w = vm((3, 16, d_model), BF16), vm((3, 4, 16, d_model), BF16)
    head_g = vm((three, d_model), F32)
    tile_s, tile_r = vm((3, 4, 16, d_model), BF16), vm((3, 4, 16, d_model), BF16)
    s_all = per_layer((8, tokens, d_model), BF16)
    pack = vm((128, 16), F32)
    c_in = vm((tokens, d_model), BF16)
    p_out, p_in = vm((8, 128), jnp.int32), vm((8, 128), jnp.int32)
    o_send, i_send, i_recv = (vm((tokens, d_model), BF16) for _ in range(3))
    x32, h1_ = vm((d_model, tokens), F32), vm((d_model, tokens), F32)
    hlow = per_layer((d_model, tokens), BF16)
    xh1, xh2 = per_layer((d_model, tokens), F32), per_layer((d_model, tokens), F32)
    rs1, rs2 = per_layer((8, tokens), F32), per_layer((8, tokens), F32)
    slope, act = per_layer((d_ff, tokens), F32), per_layer((d_ff, tokens), BF16)
    lse, o32 = per_layer((8, 8, tokens), F32), per_layer((8, hd, tokens), F32)
    send1, send3 = vm((8, hd, tokens), BF16), vm((8, three, tokens), BF16)
    qr, ar = per_layer((8, three, tokens), BF16), per_layer((8, hd, tokens), BF16)
    dr, er = per_layer((8, hd, tokens), BF16), per_layer((8, three, tokens), BF16)
    g32, dh32 = vm((d_model, tokens), F32), vm((d_model, tokens), F32)
    dz_, dz2_ = vm((d_model, tokens), BF16), vm((d_model, tokens), BF16)
    kt, vt, qt, dt = (vm((seq_len, hd), BF16) for _ in range(4))
    dk, dv = vm((seq_len, hd), F32), vm((seq_len, hd), F32)
    df_ = vm((d_ff, tokens), BF16)
    gv = vm((d_model, 128), F32)

    def body(ins, outs, R, SS, RS, word):
        (in_ref, wqkv, wout, wup, wdown, biases, upb, norms, cot_ref, pref_ref) = ins
        (o_out, o_ig, o_qkv, o_gout, o_up, o_down, o_bias, o_upb, o_norms) = outs
        dp, sq = lax.axis_index("dp"), lax.axis_index("seq")
        x, c = dp // 2, dp % 2
        z, y = sq // 2, sq % 2
        zh, zl = z // 2, z % 2
        rank = 4 * c + 2 * zl + y

        def dev(x_, c_, z_, y_):
            return (x_ * 2 + c_, z_ * 2 + y_)

        def remote(src, dst, idx, device, arrival=None):
            return pltpu.make_async_remote_copy(
                src_ref=src,
                dst_ref=dst,
                send_sem=SS.at[idx],
                recv_sem=RS.at[idx if arrival is None else arrival],
                device_id=device,
                device_id_type=MESH,
            )

        def peer(k):
            c_ = (c + k // 4) % 2
            zl_ = (zl + (k // 2) % 2) % 2
            y_ = (y + k % 2) % 2
            return dev(x, c_, 2 * zh + zl_, y_), 4 * c_ + 2 * zl_ + y_

        sends = []

        barrier = pltpu.get_barrier_semaphore()
        swap_dev = dev(x, 1 - c, 2 * (1 - zh) + zl, y)
        me = dp * 8 + sq

        x_dev, zz_dev = dev(1 - x, c, z, y), dev(x, c, (z + 2) % 4, y)
        y_dev, z_dev, c_dev = dev(x, c, z, 1 - y), dev(x, c, 2 * zh + 1 - zl, y), dev(x, 1 - c, z, y)
        near = (x_dev, y_dev, z_dev, zz_dev, c_dev, swap_dev)
        for device in near:
            pl.semaphore_signal(barrier, inc=1, device_id=device, device_id_type=MESH)

        def all_in():
            for i, device in enumerate((c_dev, y_dev, z_dev, x_dev, zz_dev)):
                pl.semaphore_signal(word.at[i], inc=1, device_id=device, device_id_type=MESH)
                pl.semaphore_wait(word.at[i], 1)

        def place(n, value):
            for h in range(n.halves):
                R[n.weight][h, x, c, zh, zl, y] = value[:, h * n.cols : (h + 1) * n.cols]

        R[own_q][...] = wqkv[...].astype(BF16).reshape(3, 16, d_model)
        place(g_qkv, wqkv[...].astype(BF16))
        R[pack][0:4, :] = biases[...]
        R[pack][4:8, :] = norms[...]
        for b in range(4):
            R[pack][8 + b : 9 + b, :] = upb[:, 16 * b : 16 * (b + 1)]
        R[pack][12:128, :] = jnp.zeros((116, 16), F32)
        R[v_own][...] = R[pack][...].T.astype(BF16)
        R[p_out][...] = jnp.full((8, 128), pref_ref[0], jnp.int32)
        place(g_out, wout[...].astype(BF16))
        place(g_up, wup[...].astype(BF16))
        place(g_down, wdown[...].astype(BF16))
        pl.semaphore_wait(barrier, len(near))

        swapped = c != zh

        def swap(src, dst, idx):
            return remote(src, dst, idx, swap_dev)

        s_idx, s2_idx, c_idx, p_idx, so_idx, si_idx = (take(1) for _ in range(6))

        w_base, t_base = take(13), take(13)

        def head_of(i, block):
            t = 3 * me + i
            h = (t % 32) // 4
            device = dev(block // 2, h // 4, 2 * (block % 2) + (h // 2) % 2, h % 2)
            return t, device, (h == rank) & (block == 2 * x + zh)

        def owner_of(n):
            t = (n // 4) * 32 + 4 * rank + n % 4
            return t // 3, t % 3

        def weight_copy(n):
            i, block = n // 4, n % 4
            t, device, here = head_of(i, block)
            part, sub = t // 32, t % 4
            dst = R[head_w].at[part, sub]
            return remote(R[own_q].at[i], dst, w_base + n, device, w_base + 12), here, (i, part, sub)

        v_base = take(2)

        def whole_copy(name, i):
            return pltpu.make_async_copy(R[name], R[name], RS.at[i])

        def vec_out(i, carry):
            other = (me + i) % 32
            remote(R[v_own], R[v_all].at[me], v_base, (other // 8, other % 8)).start()
            return carry

        def vec_back(i, carry):
            other = (me + i) % 32
            remote(R[v_send].at[other], R[v_recv].at[me], v_base + 1, (other // 8, other % 8)).start()
            return carry

        def weight_send(n, carry):
            copy, here, (i, part, sub) = weight_copy(n)

            @pl.when(jnp.logical_not(here))
            def _():
                copy.start()

            @pl.when(here)
            def _():
                pltpu.make_async_copy(R[own_q].at[i], R[head_w].at[part, sub], RS.at[w_base + 12]).start()

            return carry

        def weight_wait(n, carry):
            copy, here, _ = weight_copy(n)

            @pl.when(jnp.logical_not(here))
            def _():
                copy.wait_send()

            return carry

        def tile_copy(n):
            owner, i = owner_of(n)
            block = 2 * x + zh
            src, dst = R[tile_s].at[n // 4, n % 4], R[tile_r].at[i, block]
            device = (owner // 8, owner % 8)
            return remote(src, dst, t_base + n, device, t_base + 12), owner == me, (i, block)

        def tile_send(n, carry):
            copy, here, (i, block) = tile_copy(n)

            @pl.when(jnp.logical_not(here))
            def _():
                copy.start()

            @pl.when(here)
            def _():
                pltpu.make_async_copy(R[tile_s].at[n // 4, n % 4], R[tile_r].at[i, block], RS.at[t_base + 12]).start()

            return carry

        def tile_wait(n, carry):
            copy, here, _ = tile_copy(n)

            @pl.when(jnp.logical_not(here))
            def _():
                copy.wait_send()

            return carry

        s_base = [take(13), take(13)]

        def rank_of(c_, zl_, y_):
            return 4 * c_ + 2 * zl_ + y_

        top, low_rows = slice(0, tokens // 2), slice(tokens // 2, tokens)

        def s_copy(l, i):
            py, pz, pd = rank_of(c, zl, 1 - y), rank_of(c, 1 - zl, y), rank_of(c, 1 - zl, 1 - y)
            r = R[s_all[l]]
            ref, device = (
                (r.at[rank, top], y_dev),
                (r.at[rank, low_rows], y_dev),
                (r.at[rank, low_rows], z_dev),
                (r.at[rank, top], z_dev),
                (r.at[rank], c_dev),
                (r.at[py, top], z_dev),
                (r.at[pz, low_rows], y_dev),
                (r.at[py, top], c_dev),
                (r.at[py, low_rows], c_dev),
                (r.at[pz, low_rows], c_dev),
                (r.at[pz, top], c_dev),
                (r.at[pd, top], c_dev),
                (r.at[pd, low_rows], c_dev),
            )[i]
            return remote(ref, ref, s_base[l] + i, device)

        def s_start(l, *which):
            for i in which:
                s_copy(l, i).start()

        def s_got(l, *which):
            for i in which:
                s_copy(l, i).wait_recv()

        own_rank = R[s_all[0]].at[rank]
        swap_rank = R[s_all[0]].at[rank_of(1 - c, zl, y)]

        def swap_rows(rows, idx):
            return swap(in_ref.at[rows], swap_rank.at[rows], idx)

        @pl.when(swapped)
        def _():
            swap_rows(top, s_idx).start()
            swap_rows(low_rows, s2_idx).start()
            swap(R[p_out], R[p_in], p_idx).start()

        @pl.when(jnp.logical_not(swapped))
        def _():
            own_rank[...] = in_ref[...]
            R[p_in][...] = R[p_out][...]

        ag = {}
        for n in everything:
            ag[n] = (take(2), take(2), take(2), take(1))

        def ag_z(n, _):
            own = R[n.weight].at[:, x, c, zh, zl, y]
            cp = remote(own, own, ag[n][0], zz_dev)
            cp.start()
            sends.append(cp)
            return [cp]

        def ag_zz(n, waits):
            waits[0].wait_recv()
            part = R[n.weight].at[:, x, c, :, zl, y]
            cp = remote(part, part, ag[n][0] + 1, z_dev)
            cp.start()
            sends.append(cp)
            return [cp]

        def ag_a(n, waits):
            waits[0].wait_recv()
            w = R[n.weight]
            cps = []
            for h in range(n.halves):
                part = w.at[h, x, c, :, :, y]
                cps.append(remote(part, part, ag[n][1] + h, y_dev if n.y_first[h] else x_dev))
                cps[-1].start()
            sends.extend(cps)
            return cps

        def ag_b(n, waits):
            w = R[n.weight]
            cps = []
            for h in range(n.halves):
                waits[h].wait_recv()
                part = w.at[h, x, c] if n.y_first[h] else w.at[h, :, c, :, :, y]
                cps.append(remote(part, part, ag[n][2] + h, x_dev if n.y_first[h] else y_dev))
                cps[-1].start()
            sends.extend(cps)
            return cps

        def ag_c(n, waits):
            for cp in waits:
                cp.wait_recv()
            part = R[n.weight].at[:, :, c]
            cp = remote(part, part, ag[n][3], c_dev)
            cp.start()
            sends.append(cp)
            return [cp]

        state = {}

        def step(stage, n):
            state[n] = stage(n, state.get(n))

        def arrived(n):
            for cp in state[n]:
                cp.wait_recv()


        @pl.when(jnp.logical_not(swapped))
        def _():
            s_start(0, 0, 2, 1, 3, 4)

        all_in()

        @pl.when(swapped)
        def _():
            swap_rows(top, s_idx).wait()
            s_start(0, 0, 3)
            swap_rows(low_rows, s2_idx).wait()
            s_start(0, 2, 1, 4)
            swap(R[p_out], R[p_in], p_idx).wait()

        step(ag_z, g_up)
        step(ag_z, g_out)
        lax.fori_loop(0, 12, weight_send, 0)
        pltpu.make_async_copy(R[v_own], R[v_all].at[me], RS.at[v_base]).start()
        lax.fori_loop(1, 32, vec_out, 0)
        s_got(0, 0)
        s_start(0, 5, 7)
        s_got(0, 2)
        s_start(0, 6, 9)
        s_got(0, 1)
        s_start(0, 8)
        s_got(0, 3)
        s_start(0, 10)
        step(ag_zz, g_up)
        step(ag_zz, g_out)
        step(ag_z, g_down)
        s_got(0, 5)
        s_start(0, 11)
        s_got(0, 6)
        s_start(0, 12)
        step(ag_a, g_up)
        step(ag_zz, g_down)
        step(ag_a, g_out)
        R[x32][...] = own_rank[...].T.astype(F32)
        s_got(0, 4, 7, 8, 9, 10, 11, 12)
        whole_copy(head_w, w_base + 12).wait()
        whole_copy(v_all, v_base).wait()

        def weight(n, h):
            return R[n.weight][h].reshape(32 * n.rows, n.cols)

        def vec(i):
            return R[v_all][:, :, i : i + 1].reshape(d_model, 1).astype(F32)

        def up_bias(i):
            lanes = [
                R[v_all][8 * i : 8 * (i + 1), :, 8 + b : 9 + b].reshape(8, 1, 16, 1).astype(F32)
                for b in range(4)
            ]
            return jnp.concatenate(lanes, axis=1).reshape(chunk, 1)

        def spread(src, dst):
            base = take(8)
            cps = []
            for k in range(1, 8):
                device, other = peer(k)
                cps.append(remote(src.at[other], dst.at[rank], base + k, device))
                cps[-1].start()
            dst[rank] = src[rank]
            return cps

        def batch(src, dst, base, core):
            def go(ks):
                for k in ks:
                    device, other = peer(k)
                    remote(src.at[other], dst.at[rank], base + k, device).start()

            @pl.when(c == core)
            def _():
                go(range(1, 4))
                dst[rank] = src[rank]

            @pl.when(c != core)
            def _():
                go(range(4, 8))

        def sent(src, dst, base):
            for k in range(1, 8):
                remote(src.at[0], dst.at[0], base + k, peer(k)[0]).wait()

        def finish(cps):
            for cp in cps:
                cp.wait()

        def ext(qb):
            return max(fixed, qb + 1)

        def span(first, last=None):
            return slice(first * tokens, (first + 1 if last is None else last) * tokens)

        def masked(s, qb):
            if qb < fixed:
                kk = lax.broadcasted_iota(jnp.int32, s.shape, 0)
                qq = qb * tokens + lax.broadcasted_iota(jnp.int32, s.shape, 1)
                return jnp.where((kk <= qq) | (kk < R[p_in][0:1, 0:1]), s, NEGATIVE)
            low = s[qb * tokens :]
            kk = lax.broadcasted_iota(jnp.int32, low.shape, 0)
            qq = lax.broadcasted_iota(jnp.int32, low.shape, 1)
            low = jnp.where(kk <= qq, low, NEGATIVE)
            return jnp.concatenate([s[: qb * tokens], low], axis=0)

        def norm(r, gain, shift):
            centre = r - jnp.mean(r, axis=0, keepdims=True)
            inv = lax.rsqrt(jnp.mean(centre * centre, axis=0, keepdims=True) + EPSILON)
            xh = centre * inv
            return xh * gain + shift, xh, inv

        def forward(l):
            rows_all, qkv_all = R[s_all[l]], R[qr[l]]
            if l == 1:
                s_start(1, 0, 2, 1, 3, 4)
                s_got(1, 0)
                s_start(1, 5, 7)
                s_got(1, 2)
                s_start(1, 6, 9)
                s_got(1, 1)
                s_start(1, 8)
                s_got(1, 3)
                s_start(1, 10)
                s_got(1, 5)
                s_start(1, 11)
                s_got(1, 6)
                s_start(1, 12)
                s_got(1, 4, 7, 8, 9, 10, 11, 12)
                step(ag_z, g_qkv)

                @pl.when(swapped)
                def _():
                    swap(cot_ref, R[c_in], c_idx).start()

            packed = R[v_all][pl.ds(4 * rank, 4)]
            packed = packed.reshape(hd, 128).astype(F32)
            bias = jnp.concatenate([packed[:, 0:1], jnp.zeros((hd, 1), F32), packed[:, 1:2]], axis=0)
            w = R[head_w][...].reshape(three, d_model)
            for b in range(8):
                qkv_all[b] = (mm_nt(w, rows_all[b]) + bias).astype(BF16)
            if l == 0:
                step(ag_b, g_up)
                step(ag_a, g_down)
            for b in range(8):
                R[kt][span(b), :] = qkv_all[b, hd : 2 * hd, :].T
                R[vt][span(b), :] = qkv_all[b, 2 * hd :, :].T
            base = take(8)
            for qb in range(8):
                n = ext(qb)
                s = masked(mm_nn(R[kt][span(0, n), :], qkv_all[qb, 0:hd, :]) * EXP2_SCALE, qb)
                m = jnp.max(s, axis=0, keepdims=True)
                p = jnp.exp2(s - m)
                total = jnp.sum(p, axis=0, keepdims=True)
                o = mm_tn(p.astype(BF16), R[vt][span(0, n), :]).T / total
                R[o32[l]][qb] = o
                R[send1][qb] = o.astype(BF16)
                R[lse[l]][qb] = jnp.broadcast_to(m + jnp.log2(total), (8, tokens))
                if qb == 3:
                    batch(R[send1], R[ar[l]], base, 0)
                if l == 0 and qb == 1:
                    step(ag_b, g_out)
                if l == 1 and qb == 4:
                    step(ag_zz, g_qkv)
            batch(R[send1], R[ar[l]], base, 1)
            if l == 0:
                step(ag_b, g_down)
                step(ag_c, g_up)
                step(ag_c, g_out)
                lax.fori_loop(0, 12, weight_wait, 0)
            sent(R[send1], R[ar[l]], base)
            if l == 1:
                step(ag_a, g_qkv)
            if l == 0:
                arrived(g_out)
            att = R[ar[l]][...].reshape(d_model, tokens)
            half = d_model // 2
            r1 = R[x32][...] + vec(2)
            r1 = r1 + mm_nn(weight(g_out, 0), att[:half]) + mm_nn(weight(g_out, 1), att[half:])
            h1, xh, inv = norm(r1, vec(4), vec(5))
            R[h1_][...] = h1
            R[xh1[l]][...] = xh
            R[rs1[l]][...] = jnp.broadcast_to(inv, (8, tokens))
            R[hlow[l]][...] = h1.astype(BF16)
            if l == 0:
                arrived(g_up)
            for i in range(4):
                rows = slice(i * chunk, (i + 1) * chunk)
                g = g_up
                f = up_bias(i)
                for h in range(2):
                    w = R[g_up.weight][h, i // 2, i % 2].reshape(chunk, g.cols)
                    f = f + mm_nn(w, R[hlow[l]][h * half : (h + 1) * half, :])
                cdf = 0.5 * (1.0 + lax.erf(f * ROOT_HALF))
                R[act[l]][rows, :] = (f * cdf).astype(BF16)
                R[slope[l]][rows, :] = cdf + f * (jnp.exp(-0.5 * f * f) * DENSITY_SCALE)
            if l == 0:
                step(ag_c, g_down)
                arrived(g_down)
            r2 = R[h1_][...] + vec(3)
            for h in range(2):
                r2 = r2 + mm_nn(weight(g_down, h), R[act[l]][h * d_ff // 2 : (h + 1) * d_ff // 2, :])
            out, xh, inv = norm(r2, vec(6), vec(7))
            R[xh2[l]][...] = xh
            R[rs2[l]][...] = jnp.broadcast_to(inv, (8, tokens))
            return out

        idx = {n: (take(1), take(2), take(2), take(2)) for n in everything[1:]}

        def rs_c(n, _):
            cp = remote(R[n.grad].at[:, :, 1 - c], R[n.recv1], idx[n][0], c_dev)
            cp.start()
            sends.append(cp)
            return [cp]

        def a_send(n, h):
            g_, r1 = R[n.grad], R[n.recv1]
            if n.x_first[h]:
                value, device = g_[h, 1 - x, c].astype(F32) + r1[h, 1 - x].astype(F32), x_dev
            else:
                value, device = g_[h, :, c, :, :, 1 - y].astype(F32) + r1[h, :, :, :, 1 - y].astype(F32), y_dev
            R[n.send2[h]][...] = value.astype(BF16)
            cp = remote(R[n.send2[h]], R[n.recv2[h]], idx[n][1] + h, device)
            cp.start()
            sends.append(cp)
            return cp

        def rs_a_first(n, waits):
            waits[0].wait_recv()
            return [a_send(n, 0)]

        def rs_a_second(n, waits):
            return waits + [a_send(n, 1)]

        def rs_a(n, waits):
            waits = rs_a_first(n, waits)
            return rs_a_second(n, waits) if n.halves == 2 else waits

        def rs_b(n, waits):
            g_, r1 = R[n.grad], R[n.recv1]
            cps = []
            for h in range(n.halves):
                waits[h].wait_recv()
                r2 = R[n.recv2[h]]
                if n.x_first[h]:
                    value, device = g_[h, x, c, :, :, 1 - y].astype(F32) + r1[h, x, :, :, 1 - y].astype(F32), y_dev
                    value = value + r2[:, :, 1 - y].astype(F32)
                else:
                    value, device = g_[h, 1 - x, c, :, :, y].astype(F32) + r1[h, 1 - x, :, :, y].astype(F32), x_dev
                    value = value + r2[1 - x].astype(F32)
                R[n.send3[h]][...] = value.astype(BF16)
                cps.append(remote(R[n.send3[h]], R[n.recv3[h]], idx[n][2] + h, device))
                cps[-1].start()
            sends.extend(cps)
            return cps

        def rs_z(n, waits):
            g_, r1, sum3 = R[n.grad], R[n.recv1], R[n.sum3]
            for h in range(n.halves):
                waits[h].wait_recv()
                r2 = R[n.recv2[h]]
                kept = r2[:, :, y] if n.x_first[h] else r2[x]
                sum3[:, :, h] = (
                    g_[h, x, c, :, :, y].astype(F32)
                    + r1[h, x, :, :, y].astype(F32)
                    + kept.astype(F32)
                    + R[n.recv3[h]][...].astype(F32)
                )
            R[n.send4][...] = sum3[:, 1 - zl].astype(BF16)
            cp = remote(R[n.send4], R[n.recv4], idx[n][3], z_dev)
            cp.start()
            sends.append(cp)
            return [cp]

        def rs_zz(n, waits):
            waits[0].wait_recv()
            R[n.sum4][...] = R[n.sum3][:, zl] + R[n.recv4][...].astype(F32)
            R[n.send5][...] = R[n.sum4][1 - zh].astype(BF16)
            cp = remote(R[n.send5], R[n.recv5], idx[n][3] + 1, zz_dev)
            cp.start()
            sends.append(cp)
            return [cp]

        def rs_end(n, waits):
            waits[0].wait_recv()
            return R[n.sum4][zh] + R[n.recv5][...].astype(F32)

        def pick(lane, count_=1):
            rows = lax.broadcasted_iota(jnp.int32, (128, tokens), 0)
            return jnp.where((rows >= lane) & (rows < lane + count_), 1.0, 0.0).astype(BF16)

        def low_sum(lane, value):
            return mm_nt(value, pick(lane))

        def full_sum(lane, value):
            high = value.astype(BF16)
            return low_sum(lane, high) + low_sum(lane, (value - high.astype(F32)).astype(BF16))

        def add_grad(n, h, value, l):
            value = value.reshape(n.whole[1:])
            if l == 0:
                value = value + R[n.grad][h].astype(F32)
            R[n.grad][h] = value.astype(BF16)

        def norm_grad(g, xh, inv, gain):
            s = g * gain
            return inv * (
                s - jnp.mean(s, axis=0, keepdims=True) - xh * jnp.mean(s * xh, axis=0, keepdims=True)
            )

        half = d_model // 2

        def out_grad(l):
            att = R[ar[l]][...].reshape(d_model, tokens)
            for h in range(2):
                add_grad(g_out, h, mm_nt(R[dz_][...], att[h * half : (h + 1) * half]), l)

        def up_grad(l):
            for h in range(2):
                add_grad(g_up, h, mm_nt(R[df_][...], R[hlow[l]][h * half : (h + 1) * half, :]), l)

        def down_grad(l):
            for h in range(2):
                add_grad(g_down, h, mm_nt(R[dz2_][...], R[act[l]][h * d_ff // 2 : (h + 1) * d_ff // 2, :]), l)

        def head_grad(l):
            rows_all, back = R[s_all[l]], R[send3]
            t = mm_nn(back[0], rows_all[0])
            sums = low_sum(0, back[0, 0:hd]) + low_sum(1, back[0, 2 * hd :])
            for b in range(1, 8):
                t = t + mm_nn(back[b], rows_all[b])
                sums = sums + low_sum(0, back[b, 0:hd]) + low_sum(1, back[b, 2 * hd :])
            R[gv][pl.ds(pl.multiple_of(rank * hd, hd), hd), :] += sums
            if l == 1:
                R[head_g][...] = t
            else:
                R[tile_s][...] = (R[head_g][...] + t).astype(BF16).reshape(3, 4, 16, d_model)

        def dense_sums(l):
            t = full_sum(6, R[g32][...] * R[xh2[l]][...]) + full_sum(7, R[g32][...])
            t = t + full_sum(4, R[dh32][...] * R[xh1[l]][...]) + full_sum(5, R[dh32][...])
            t = t + low_sum(3, R[dz2_][...]) + low_sum(2, R[dz_][...])
            R[gv][...] += t
            ones = pick(8, 4)
            lanes = lax.broadcasted_iota(jnp.int32, (8, 16, 128), 2)
            for i in range(4):
                sums = mm_nt(R[df_][i * chunk : (i + 1) * chunk, :], ones).reshape(8, 4, 16, 128)
                t = jnp.where(lanes == 8, sums[:, 0], 0.0)
                for b in range(1, 4):
                    t = jnp.where(lanes == 8 + b, sums[:, b], t)
                R[gv][i * 128 : (i + 1) * 128, :] += t.reshape(128, 128)

        def backward(l):
            dr2 = norm_grad(R[g32][...], R[xh2[l]][...], R[rs2[l]][0:1, :], vec(6))
            R[dz2_][...] = dr2.astype(BF16)
            R[x32][...] = dr2
            if l == 0:
                down_grad(l)
                step(rs_c, g_down)
            for i in range(4):
                rows = slice(i * chunk, (i + 1) * chunk)
                h, lo = i // 2, (i % 2) * chunk
                w = R[g_down.weight][h].reshape(d_model, d_ff // 2)[:, lo : lo + chunk]
                R[df_][rows, :] = (mm_tn(w, R[dz2_][...]) * R[slope[l]][rows, :]).astype(BF16)
            if l == 0:
                step(rs_a, g_down)
                up_grad(l)
                step(rs_c, g_up)
            for h in range(2):
                rows = slice(h * half, (h + 1) * half)
                R[dh32][rows, :] = R[x32][rows, :] + mm_tn(weight(g_up, h), R[df_][...])
            dr1 = norm_grad(R[dh32][...], R[xh1[l]][...], R[rs1[l]][0:1, :], vec(4))
            R[dz_][...] = dr1.astype(BF16)
            R[x32][...] = dr1
            for h in range(2):
                datt = mm_tn(weight(g_out, h), R[dz_][...]).astype(BF16)
                R[send1][h * 4 : (h + 1) * 4] = datt.reshape(4, hd, tokens)
            cps = spread(R[send1], R[dr[l]])
            if l == 1:
                down_grad(l)
                up_grad(l)
            else:
                step(rs_a_first, g_up)
            out_grad(l)
            if l == 0:
                step(rs_c, g_out)
            dense_sums(l)
            finish(cps)
            if l == 0:
                step(rs_a_second, g_up)
                step(rs_a, g_out)
            else:
                step(ag_b, g_qkv)

                @pl.when(swapped)
                def _():
                    swap(R[o_send], o_out, so_idx).start()

            qkv_all, datt_all = R[qr[l]], R[dr[l]]
            for b in range(8):
                R[qt][span(b), :] = qkv_all[b, 0:hd, :].T
                R[kt][span(b), :] = qkv_all[b, hd : 2 * hd, :].T
                R[vt][span(b), :] = qkv_all[b, 2 * hd :, :].T
                R[dt][span(b), :] = datt_all[b].T
            R[dk][...] = jnp.zeros((seq_len, hd), F32)
            R[dv][...] = jnp.zeros((seq_len, hd), F32)
            base = take(8)
            src, dst = R[send3], R[er[l]]

            def keys_out(b):
                src[b, hd : 2 * hd, :] = (R[dk][span(b), :] * SCORE_SCALE).T.astype(BF16)
                src[b, 2 * hd :, :] = R[dv][span(b), :].T.astype(BF16)

            for qb in range(7, -1, -1):
                n = ext(qb)
                keys = span(0, n)
                delta = jnp.sum(datt_all[qb].astype(F32) * R[o32[l]][qb], axis=0, keepdims=True)
                s = masked(mm_nn(R[kt][keys, :], qkv_all[qb, 0:hd, :]) * EXP2_SCALE, qb)
                p = jnp.exp2(s - R[lse[l]][qb, 0:1, :])
                dprob = mm_nn(R[vt][keys, :], datt_all[qb])
                dsc = (p * (dprob - delta)).astype(BF16)
                R[dv][keys, :] += mm_nn(p.astype(BF16), R[dt][span(qb), :])
                R[dk][keys, :] += mm_nn(dsc, R[qt][span(qb), :])
                src[qb, 0:hd, :] = (mm_tn(R[kt][keys, :], dsc) * SCORE_SCALE).astype(BF16)
                if qb == 4:
                    for b in range(4, 8):
                        keys_out(b)
                    batch(src, dst, base, 1)
            for b in range(4):
                keys_out(b)
            batch(src, dst, base, 0)
            if l == 1:
                step(ag_c, g_qkv)
            if l == 0:
                step(rs_b, g_down)
            head_grad(l)
            if l == 0:
                lax.fori_loop(0, 12, tile_send, 0)
                R[v_send][...] = R[gv][...].astype(BF16).reshape(32, 16, 128)
                pltpu.make_async_copy(R[v_send].at[me], R[v_recv].at[me], RS.at[v_base + 1]).start()
                lax.fori_loop(1, 32, vec_back, 0)
            else:
                arrived(g_qkv)
            sent(src, dst, base)
            back = R[er[l]]
            for h in range(2):
                w = weight(g_qkv, h)
                t = R[x32][h * half : (h + 1) * half, :]
                for part in range(3):
                    grad = back[:, part * hd : (part + 1) * hd, :].reshape(d_model, tokens)
                    t = t + mm_tn(w[part * d_model : (part + 1) * d_model], grad)
                R[g32][h * half : (h + 1) * half, :] = t

        mid = forward(0)
        R[x32][...] = mid
        R[s_all[1]][rank] = mid.astype(BF16).T
        last = forward(1)
        R[o_send][...] = last.astype(BF16).T

        @pl.when(swapped)
        def _():
            swap(cot_ref, R[c_in], c_idx).wait()

        @pl.when(jnp.logical_not(swapped))
        def _():
            o_out[...] = R[o_send][...]
            R[c_in][...] = cot_ref[...]

        R[gv][...] = jnp.zeros((d_model, 128), F32)
        R[g32][...] = R[c_in][...].T.astype(F32)
        backward(1)
        backward(0)
        R[i_send][...] = R[g32][...].astype(BF16).T

        @pl.when(swapped)
        def _():
            swap(R[i_send], R[i_recv], si_idx).start()

        @pl.when(jnp.logical_not(swapped))
        def _():
            o_ig[...] = R[g32][...].T

        step(rs_b, g_out)
        step(rs_z, g_down)
        step(rs_b, g_up)
        step(rs_z, g_out)
        step(rs_zz, g_down)
        step(rs_z, g_up)
        step(rs_zz, g_out)
        step(rs_zz, g_up)
        whole_copy(tile_r, t_base + 12).wait()
        lax.fori_loop(0, 12, tile_wait, 0)
        t = R[tile_r][:, 0].astype(F32)
        for block in range(1, 4):
            t = t + R[tile_r][:, block].astype(F32)
        o_qkv[...] = t.reshape(48, d_model)
        for n, ref in ((g_down, o_down), (g_up, o_up), (g_out, o_gout)):
            t = rs_end(n, state[n])
            ref[...] = jnp.concatenate([t[0], t[1]], axis=1)
        whole_copy(v_recv, v_base + 1).wait()
        t = R[v_recv][0].astype(F32)
        for i in range(1, 32):
            t = t + R[v_recv][i].astype(F32)
        t = t.T
        o_bias[...] = t[0:4]
        o_norms[...] = t[4:8]
        o_upb[...] = jnp.concatenate([t[8 + b : 9 + b] for b in range(4)], axis=1)

        @pl.when(swapped)
        def _():
            swap(R[o_send], o_out, so_idx).wait()
            swap(R[i_send], R[i_recv], si_idx).wait()
            o_ig[...] = R[i_recv][...].astype(F32)

        for cp in sends:
            cp.wait_send()
        for i in range(2):
            sent_vec = R[v_recv].at[0:31]
            pltpu.make_async_copy(sent_vec, sent_vec, SS.at[v_base + i]).wait()
        for l in range(2):
            for i in range(13):
                s_copy(l, i).wait_send()

    n_sems = 6 + 2 * 13 + 2 * 13 + 2 + 4 * 7 + 6 * 8 + 3 * 7

    def kernel(*refs):
        count[0] = 0
        body(refs[:10], refs[10:19], refs[19:-3], refs[-3], refs[-2], refs[-1])
        assert count[0] <= n_sems

    def hand_on(*refs):
        for src, dst in zip(refs[:9], refs[9:]):
            dst[...] = src[...]

    def call(inputs, qkv_w, out_w, up_w, down_w, biases, up_bias, norms, cotangent, prefix):
        weights = [w.T for w in (qkv_w, out_w, up_w, down_w)]
        small = [biases, up_bias.reshape(1, -1), norms]
        out_shape = (
            jax.ShapeDtypeStruct((tokens, d_model), BF16),
            jax.ShapeDtypeStruct((tokens, d_model), F32),
            *(jax.ShapeDtypeStruct(w.shape, F32) for w in weights + small),
        )
        vmem = pl.BlockSpec(memory_space=pltpu.VMEM)
        results = pl.pallas_call(
            kernel,
            out_shape=out_shape,
            in_specs=[vmem] * 9 + [pl.BlockSpec(memory_space=pltpu.SMEM)],
            out_specs=[vmem] * 9,
            scratch_shapes=[
                *scratch,
                pltpu.SemaphoreType.DMA((n_sems,)),
                pltpu.SemaphoreType.DMA((n_sems,)),
                pltpu.SemaphoreType.REGULAR((5,)),
            ],
            compiler_params=pltpu.CompilerParams(
                collective_id=0, has_side_effects=True, vmem_limit_bytes=62 * 2**20
            ),
        )(inputs, *weights, *small, cotangent, prefix)
        results = pl.pallas_call(
            hand_on, out_shape=out_shape, in_specs=[vmem] * 9, out_specs=[vmem] * 9
        )(*results)
        back = [w.T for w in results[2:6]]
        return (*results[:2], *back, results[6], results[7].reshape(up_bias.shape), results[8])

    return call


def fused_fits(mesh, args):
    if tuple(mesh.shape.items()) != (("dp", 4), ("seq", 8)) or HEADS != 8:
        return False
    total, d_model = args[0].shape
    d_ff = args[3].shape[1]
    return total % (32 * 128) == 0 and total // 32 == 256 and d_model == 512 and d_ff == 2048


def solution(mesh):
    specs = dict(
        mesh=mesh,
        in_specs=(
            P(("dp", "seq"), None),
            P(None, ("dp", "seq")),
            P(None, ("dp", "seq")),
            P(None, ("dp", "seq")),
            P(None, ("dp", "seq")),
            P(None, ("dp", "seq")),
            P(("dp", "seq")),
            P(None, ("dp", "seq")),
            P(("dp", "seq"), None),
            P("dp"),
        ),
        out_specs=(
            P(("dp", "seq"), None),
            P(("dp", "seq"), None),
            P(None, ("dp", "seq")),
            P(None, ("dp", "seq")),
            P(None, ("dp", "seq")),
            P(None, ("dp", "seq")),
            P(None, ("dp", "seq")),
            P(("dp", "seq")),
            P(None, ("dp", "seq")),
        ),
        check_vma=False,
    )

    def run(*args):
        if fused_fits(mesh, args):
            d_model = args[0].shape[1]
            step = fused_step(args[0].shape[0] // 32, d_model, args[3].shape[1], HEADS)
            return jax.shard_map(step, **specs)(*args)
        return jax.shard_map(local, **specs)(*args)

    return run
```

```python
import math

import jax
import jax.numpy as jnp
from jax import lax
from jax.experimental import pallas as pl
from jax.experimental.pallas import tpu as pltpu
from jax.sharding import PartitionSpec as P

HEADS = 8


EPSILON = 1e-05
NEGATIVE = -1e30
SCORE_SCALE = 0.125
ROOT_HALF = 1.0 / math.sqrt(2.0)
DENSITY_SCALE = 1.0 / math.sqrt(2.0 * math.pi)


def dot_rows(first_op, second_op):
    return lax.dot_general(
        first_op, second_op, (((1,), (1,)), ((), ())), preferred_element_type=jnp.float32
    )


def dot_cols(first_op, second_op):
    return lax.dot_general(
        first_op, second_op, (((0,), (0,)), ((), ())), preferred_element_type=jnp.float32
    )


def split_heads(tensor_in):
    return tensor_in.reshape(tensor_in.shape[0], HEADS, -1).transpose(1, 0, 2)


def merge_heads(stacked):
    return stacked.transpose(1, 0, 2).reshape(stacked.shape[1], -1)


def cast_all(masters):
    return tuple((tensor.astype(jnp.bfloat16) for tensor in masters))


def fetch_forward(masters):
    casted = cast_all(masters)
    return (
        lax.all_gather(casted[0], ("dp", "seq"), axis=1, tiled=True),
        lax.all_gather(casted[1], ("dp", "seq"), axis=1, tiled=True),
        lax.all_gather(casted[2], ("dp", "seq"), axis=1, tiled=True),
        lax.all_gather(casted[3], ("dp", "seq"), axis=1, tiled=True),
        lax.all_gather(casted[4], ("dp", "seq"), axis=1, tiled=True),
        lax.all_gather(casted[5], ("dp", "seq"), axis=0, tiled=True),
        lax.all_gather(casted[6], ("dp", "seq"), axis=1, tiled=True),
    )


def fetch_backward(masters):
    casted = cast_all(masters)
    return (
        lax.all_gather(casted[0], ("dp", "seq"), axis=1, tiled=True),
        lax.all_gather(casted[1], ("dp", "seq"), axis=1, tiled=True),
        lax.all_gather(casted[2], ("dp", "seq"), axis=1, tiled=True),
        lax.all_gather(casted[3], ("dp", "seq"), axis=1, tiled=True),
        lax.all_gather(casted[4], ("dp", "seq"), axis=1, tiled=True),
        lax.all_gather(casted[5], ("dp", "seq"), axis=0, tiled=True),
        lax.all_gather(casted[6], ("dp", "seq"), axis=1, tiled=True),
    )


def gelu_slope(values):
    normal_cdf = 0.5 * (1.0 + jax.scipy.special.erf(values * ROOT_HALF))
    return normal_cdf + values * jnp.exp(-0.5 * values * values) * DENSITY_SCALE


def layer_norm(values, gain_vec, shift_vec):
    centre = values - jnp.mean(values, axis=1, keepdims=True)
    inv_std = lax.rsqrt(jnp.mean(centre * centre, axis=1, keepdims=True) + EPSILON)
    centred = centre * inv_std
    return (centred * gain_vec + shift_vec, centred, inv_std)


def norm_back(grad_out, centred, inv_std, gain_vec):
    scaled = grad_out * gain_vec
    grad_gain = jnp.sum(grad_out * centred, axis=0)
    grad_shift = jnp.sum(grad_out, axis=0)
    grad_in = inv_std * (
        scaled
        - jnp.mean(scaled, axis=1, keepdims=True)
        - centred * jnp.mean(scaled * centred, axis=1, keepdims=True)
    )
    return (grad_in, grad_gain, grad_shift)


def attend_forward(queries, gathered, visible):
    features = queries.shape[1]
    head_q = split_heads(queries)
    head_k = split_heads(gathered[:, :features])
    head_v = split_heads(gathered[:, features:])

    def one_head(members):
        head_query, head_keys, head_values = members
        scores = jnp.where(visible, dot_rows(head_query, head_keys) * SCORE_SCALE, NEGATIVE)
        largest = jnp.max(scores, axis=1, keepdims=True)
        exponent = jnp.exp(scores - largest)
        row_total = jnp.sum(exponent, axis=1, keepdims=True)
        probability = (exponent / row_total).astype(jnp.bfloat16)
        head_out = jnp.dot(probability, head_values, preferred_element_type=jnp.float32)
        return (head_out, (largest + jnp.log(row_total))[:, 0])

    head_outs, log_totals = lax.map(one_head, (head_q, head_k, head_v))
    return (merge_heads(head_outs), log_totals)


def attend_backward(queries, gathered, visible, grad_att, log_totals):
    features = queries.shape[1]
    head_q = split_heads(queries)
    head_k = split_heads(gathered[:, :features])
    head_v = split_heads(gathered[:, features:])
    head_g = split_heads(grad_att)

    def one_head(members):
        head_query, head_keys, head_values, head_grad, head_logs = members
        scores = jnp.where(visible, dot_rows(head_query, head_keys) * SCORE_SCALE, NEGATIVE)
        probability = jnp.exp(scores - head_logs[:, None])
        grad_prob = dot_rows(head_grad, head_values)
        row_delta = jnp.sum(probability * grad_prob, axis=1)
        grad_score = (probability * (grad_prob - row_delta[:, None])).astype(jnp.bfloat16)
        grad_query = (
            jnp.dot(grad_score, head_keys, preferred_element_type=jnp.float32) * SCORE_SCALE
        )
        grad_keys = dot_cols(grad_score, head_query) * SCORE_SCALE
        grad_values = dot_cols(probability.astype(jnp.bfloat16), head_grad)
        return (grad_query, grad_keys, grad_values)

    results = lax.map(one_head, (head_q, head_k, head_v, head_g, log_totals))
    grad_query = merge_heads(results[0])
    return (grad_query, jnp.concatenate([merge_heads(results[1]), merge_heads(results[2])], axis=1))


def layer_forward(stream, weights, visible):
    w_qkv, w_out, w_up, w_down, vec_bias, b_up, vec_norm = weights
    vec_bias = vec_bias.astype(jnp.float32)
    b_up = b_up.astype(jnp.float32)
    vec_norm = vec_norm.astype(jnp.float32)
    features = stream.shape[1]
    stream_low = stream.astype(jnp.bfloat16)
    bias_row = jnp.concatenate([vec_bias[0], jnp.zeros_like(vec_bias[0]), vec_bias[1]])
    qkv = (jnp.dot(stream_low, w_qkv, preferred_element_type=jnp.float32) + bias_row).astype(
        jnp.bfloat16
    )
    queries = qkv[:, :features]
    local_kv = qkv[:, features:]
    gathered = lax.all_gather(local_kv, "seq", axis=0, tiled=True)
    attended, log_totals = attend_forward(queries, gathered, visible)
    att_low = attended.astype(jnp.bfloat16)
    branch = jnp.dot(att_low, w_out, preferred_element_type=jnp.float32) + vec_bias[2]
    normed, centred_one, inv_std_one = layer_norm(stream + branch, vec_norm[0], vec_norm[1])
    normed_low = normed.astype(jnp.bfloat16)
    hidden = jnp.dot(normed_low, w_up, preferred_element_type=jnp.float32) + b_up
    active = jax.nn.gelu(hidden, approximate=False).astype(jnp.bfloat16)
    second = jnp.dot(active, w_down, preferred_element_type=jnp.float32) + vec_bias[3]
    result, centred_two, inv_std_two = layer_norm(normed + second, vec_norm[2], vec_norm[3])
    cache = (
        stream_low,
        queries,
        local_kv,
        None,
        att_low,
        log_totals,
        centred_one,
        inv_std_one,
        normed_low,
        hidden,
        active,
        centred_two,
        inv_std_two,
    )
    return (result, cache)


def layer_backward(gradient, cache, weights, visible):
    w_qkv, w_out, w_up, w_down, vec_bias, b_up, vec_norm = weights
    vec_norm = vec_norm.astype(jnp.float32)
    (
        stream_low,
        queries,
        local_kv,
        kept_kv,
        att_low,
        log_totals,
        centred_one,
        inv_std_one,
        normed_low,
        hidden,
        active,
        centred_two,
        inv_std_two,
    ) = cache
    features = queries.shape[1]
    gathered = lax.all_gather(local_kv, "seq", axis=0, tiled=True)
    grad_two, gain_two, shift_two = norm_back(gradient, centred_two, inv_std_two, vec_norm[2])
    grad_second = grad_two.astype(jnp.bfloat16)
    bias_down = jnp.sum(grad_second.astype(jnp.float32), axis=0)
    grad_w_down = dot_cols(active, grad_second)
    grad_active = dot_rows(grad_second, w_down)
    grad_hidden = (grad_active * gelu_slope(hidden)).astype(jnp.bfloat16)
    bias_upper = jnp.sum(grad_hidden.astype(jnp.float32), axis=0)
    grad_w_up = dot_cols(normed_low, grad_hidden)
    grad_normed = grad_two + dot_rows(grad_hidden, w_up)
    grad_one, gain_one, shift_one = norm_back(grad_normed, centred_one, inv_std_one, vec_norm[0])
    grad_branch = grad_one.astype(jnp.bfloat16)
    bias_output = jnp.sum(grad_branch.astype(jnp.float32), axis=0)
    grad_w_out = dot_cols(att_low, grad_branch)
    grad_att = dot_rows(grad_branch, w_out).astype(jnp.bfloat16)
    grad_query, kv_terms = attend_backward(queries, gathered, visible, grad_att, log_totals)
    kv_grad = lax.psum_scatter(
        kv_terms.astype(jnp.bfloat16), "seq", scatter_dimension=0, tiled=True
    ).astype(jnp.float32)
    grad_qkv = jnp.concatenate([grad_query, kv_grad], axis=1).astype(jnp.bfloat16)
    qkv_sums = jnp.sum(grad_qkv.astype(jnp.float32), axis=0)
    grad_w_qkv = dot_cols(stream_low, grad_qkv)
    grad_stream = grad_one + dot_rows(grad_qkv, w_qkv)
    grad_bias = jnp.stack([qkv_sums[:features], qkv_sums[2 * features :], bias_output, bias_down])
    grad_norm = jnp.stack([gain_one, shift_one, gain_two, shift_two])
    return (
        grad_stream,
        (grad_w_qkv, grad_w_out, grad_w_up, grad_w_down, grad_bias, bias_upper, grad_norm),
    )


def local(
    inputs,
    qkv_weight,
    out_weight,
    up_weight,
    down_weight,
    biases,
    up_bias,
    norms,
    cotangent,
    prefix,
):
    masters = (qkv_weight, out_weight, up_weight, down_weight, biases, up_bias, norms)
    row_count = inputs.shape[0]
    key_count = row_count * lax.axis_size("seq")
    rows_here = lax.axis_index("seq") * row_count + jnp.arange(row_count, dtype=jnp.int32)
    all_index = jnp.arange(key_count, dtype=jnp.int32)
    visible = (all_index[None, :] <= rows_here[:, None]) | (all_index[None, :] < prefix[0])
    stream = inputs.astype(jnp.float32)
    caches = []
    for position in range(2):
        weights = fetch_forward(masters)
        stream, cache = layer_forward(stream, weights, visible)
        caches.append(cache)
    gradient = cotangent.astype(jnp.float32)
    accumulated = None
    for position in range(2):
        weights = fetch_backward(masters)
        gradient, grad_parts = layer_backward(gradient, caches[1 - position], weights, visible)
        if accumulated is None:
            accumulated = grad_parts
        else:
            accumulated = tuple((prior + fresh for prior, fresh in zip(accumulated, grad_parts)))
    reduced = (
        lax.psum_scatter(accumulated[0], ("dp", "seq"), scatter_dimension=1, tiled=True),
        lax.psum_scatter(accumulated[1], ("dp", "seq"), scatter_dimension=1, tiled=True),
        lax.psum_scatter(accumulated[2], ("dp", "seq"), scatter_dimension=1, tiled=True),
        lax.psum_scatter(accumulated[3], ("dp", "seq"), scatter_dimension=1, tiled=True),
        lax.psum_scatter(accumulated[4], ("dp", "seq"), scatter_dimension=1, tiled=True),
        lax.psum_scatter(accumulated[5], ("dp", "seq"), scatter_dimension=0, tiled=True),
        lax.psum_scatter(accumulated[6], ("dp", "seq"), scatter_dimension=1, tiled=True),
    )
    return (
        stream.astype(jnp.bfloat16),
        gradient,
        reduced[0],
        reduced[1],
        reduced[2],
        reduced[3],
        reduced[4],
        reduced[5],
        reduced[6],
    )


F32 = jnp.float32
BF16 = jnp.bfloat16
MESH = pl.DeviceIdType.MESH
LOG2E = math.log2(math.e)
EXP2_SCALE = SCORE_SCALE * LOG2E


def mm_nn(a, b):
    return lax.dot_general(a, b, (((1,), (0,)), ((), ())), preferred_element_type=F32)


def mm_nt(a, b):
    return lax.dot_general(a, b, (((1,), (1,)), ((), ())), preferred_element_type=F32)


def mm_tn(a, b):
    return lax.dot_general(a, b, (((0,), (0,)), ((), ())), preferred_element_type=F32)


def fused_step(tokens, d_model, d_ff, heads):
    hd = d_model // heads
    seq_len = tokens * 8
    fixed = (seq_len // 2) // tokens
    class Group:
        def __init__(self, rows, cols, x_first, y_first, reduced=True):
            halves = len(x_first)
            self.x_first = x_first
            self.y_first = y_first
            self.rows, self.cols, self.halves = rows, cols, halves
            self.whole = (halves, 2, 2, 2, 2, 2, rows, cols)
            self.weight = vm(self.whole, BF16)
            if not reduced:
                return
            self.grad = vm(self.whole, BF16)
            one = (halves, 2, 2, 2, 2, rows, cols)
            two = (2, 2, 2, rows, cols)
            self.recv1 = vm(one, BF16)
            self.send2, self.recv2 = [vm(two, BF16) for _ in x_first], [vm(two, BF16) for _ in x_first]
            two = (2, 2, rows, cols)
            self.send3, self.recv3 = [vm(two, BF16) for _ in x_first], [vm(two, BF16) for _ in x_first]
            self.sum3 = vm((2, 2, halves, rows, cols), F32)
            one = (2, halves, rows, cols)
            self.send4, self.recv4, self.sum4 = vm(one, BF16), vm(one, BF16), vm(one, F32)
            self.send5, self.recv5 = vm(one[1:], BF16), vm(one[1:], BF16)

    chunk = d_ff // 4
    three = 3 * hd
    scratch = []
    count = [0]

    def take(number):
        first = count[0]
        count[0] += number
        return first

    def vm(shape, dtype):
        scratch.append(pltpu.VMEM(shape, dtype))
        return len(scratch) - 1

    def per_layer(shape, dtype):
        return [vm(shape, dtype) for _ in range(2)]

    g_qkv = Group(3 * d_model // 32, d_model // 2, (True, True), (True, False), reduced=False)
    g_out = Group(d_model // 32, d_model // 2, (False, False), (True, False))
    g_up = Group(d_ff // 32, d_model // 2, (True, True), (True, False))
    g_down = Group(d_model // 32, d_ff // 2, (True, True), (True, False))
    v_own = vm((d_model // 32, 128), BF16)
    v_all, v_send, v_recv = (vm((32, d_model // 32, 128), BF16) for _ in range(3))
    everything = (g_qkv, g_out, g_up, g_down)
    own_q, head_w = vm((3, 16, d_model), BF16), vm((3, 4, 16, d_model), BF16)
    head_g = vm((three, d_model), F32)
    tile_s, tile_r = vm((3, 4, 16, d_model), BF16), vm((3, 4, 16, d_model), BF16)
    s_all = per_layer((8, tokens, d_model), BF16)
    pack = vm((128, 16), F32)
    c_in = vm((tokens, d_model), BF16)
    p_out, p_in = vm((8, 128), jnp.int32), vm((8, 128), jnp.int32)
    o_send, i_send, i_recv = (vm((tokens, d_model), BF16) for _ in range(3))
    x32, h1_ = vm((d_model, tokens), F32), vm((d_model, tokens), F32)
    hlow = per_layer((d_model, tokens), BF16)
    xh1, xh2 = per_layer((d_model, tokens), F32), per_layer((d_model, tokens), F32)
    rs1, rs2 = per_layer((8, tokens), F32), per_layer((8, tokens), F32)
    slope, act = per_layer((d_ff, tokens), F32), per_layer((d_ff, tokens), BF16)
    lse, o32 = per_layer((8, 8, tokens), F32), per_layer((8, hd, tokens), F32)
    send1, send3 = vm((8, hd, tokens), BF16), vm((8, three, tokens), BF16)
    qr, ar = per_layer((8, three, tokens), BF16), per_layer((8, hd, tokens), BF16)
    dr, er = per_layer((8, hd, tokens), BF16), per_layer((8, three, tokens), BF16)
    g32, dh32 = vm((d_model, tokens), F32), vm((d_model, tokens), F32)
    dz_, dz2_ = vm((d_model, tokens), BF16), vm((d_model, tokens), BF16)
    kt, vt, qt, dt = (vm((seq_len, hd), BF16) for _ in range(4))
    dk, dv = vm((seq_len, hd), F32), vm((seq_len, hd), F32)
    df_ = vm((d_ff, tokens), BF16)
    gv = vm((d_model, 128), F32)

    def body(ins, outs, R, SS, RS, word):
        (in_ref, wqkv, wout, wup, wdown, biases, upb, norms, cot_ref, pref_ref) = ins
        (o_out, o_ig, o_qkv, o_gout, o_up, o_down, o_bias, o_upb, o_norms) = outs
        dp, sq = lax.axis_index("dp"), lax.axis_index("seq")
        x, c = dp // 2, dp % 2
        z, y = sq // 2, sq % 2
        zh, zl = z // 2, z % 2
        rank = 4 * c + 2 * zl + y

        def dev(x_, c_, z_, y_):
            return (x_ * 2 + c_, z_ * 2 + y_)

        def remote(src, dst, idx, device, arrival=None):
            return pltpu.make_async_remote_copy(
                src_ref=src,
                dst_ref=dst,
                send_sem=SS.at[idx],
                recv_sem=RS.at[idx if arrival is None else arrival],
                device_id=device,
                device_id_type=MESH,
            )

        def peer(k):
            c_ = (c + k // 4) % 2
            zl_ = (zl + (k // 2) % 2) % 2
            y_ = (y + k % 2) % 2
            return dev(x, c_, 2 * zh + zl_, y_), 4 * c_ + 2 * zl_ + y_

        sends = []

        barrier = pltpu.get_barrier_semaphore()
        swap_dev = dev(x, 1 - c, 2 * (1 - zh) + zl, y)
        me = dp * 8 + sq

        x_dev, zz_dev = dev(1 - x, c, z, y), dev(x, c, (z + 2) % 4, y)
        y_dev, z_dev, c_dev = dev(x, c, z, 1 - y), dev(x, c, 2 * zh + 1 - zl, y), dev(x, 1 - c, z, y)
        near = (x_dev, y_dev, z_dev, zz_dev, c_dev, swap_dev)
        for device in near:
            pl.semaphore_signal(barrier, inc=1, device_id=device, device_id_type=MESH)

        def all_in():
            for i, device in enumerate((c_dev, y_dev, z_dev, x_dev, zz_dev)):
                pl.semaphore_signal(word.at[i], inc=1, device_id=device, device_id_type=MESH)
                pl.semaphore_wait(word.at[i], 1)

        def place(n, value):
            for h in range(n.halves):
                R[n.weight][h, x, c, zh, zl, y] = value[:, h * n.cols : (h + 1) * n.cols]

        R[own_q][...] = wqkv[...].astype(BF16).reshape(3, 16, d_model)
        place(g_qkv, wqkv[...].astype(BF16))
        R[pack][0:4, :] = biases[...]
        R[pack][4:8, :] = norms[...]
        for b in range(4):
            R[pack][8 + b : 9 + b, :] = upb[:, 16 * b : 16 * (b + 1)]
        R[pack][12:128, :] = jnp.zeros((116, 16), F32)
        R[v_own][...] = R[pack][...].T.astype(BF16)
        R[p_out][...] = jnp.full((8, 128), pref_ref[0], jnp.int32)
        place(g_out, wout[...].astype(BF16))
        place(g_up, wup[...].astype(BF16))
        place(g_down, wdown[...].astype(BF16))
        pl.semaphore_wait(barrier, len(near))

        swapped = c != zh

        def swap(src, dst, idx):
            return remote(src, dst, idx, swap_dev)

        s_idx, s2_idx, c_idx, p_idx, so_idx, si_idx = (take(1) for _ in range(6))

        w_base, t_base = take(13), take(13)

        def head_of(i, block):
            t = 3 * me + i
            h = (t % 32) // 4
            device = dev(block // 2, h // 4, 2 * (block % 2) + (h // 2) % 2, h % 2)
            return t, device, (h == rank) & (block == 2 * x + zh)

        def owner_of(n):
            t = (n // 4) * 32 + 4 * rank + n % 4
            return t // 3, t % 3

        def weight_copy(n):
            i, block = n // 4, n % 4
            t, device, here = head_of(i, block)
            part, sub = t // 32, t % 4
            dst = R[head_w].at[part, sub]
            return remote(R[own_q].at[i], dst, w_base + n, device, w_base + 12), here, (i, part, sub)

        v_base = take(2)

        def whole_copy(name, i):
            return pltpu.make_async_copy(R[name], R[name], RS.at[i])

        def vec_out(i, carry):
            other = (me + i) % 32
            remote(R[v_own], R[v_all].at[me], v_base, (other // 8, other % 8)).start()
            return carry

        def vec_back(i, carry):
            other = (me + i) % 32
            remote(R[v_send].at[other], R[v_recv].at[me], v_base + 1, (other // 8, other % 8)).start()
            return carry

        def weight_send(n, carry):
            copy, here, (i, part, sub) = weight_copy(n)

            @pl.when(jnp.logical_not(here))
            def _():
                copy.start()

            @pl.when(here)
            def _():
                pltpu.make_async_copy(R[own_q].at[i], R[head_w].at[part, sub], RS.at[w_base + 12]).start()

            return carry

        def weight_wait(n, carry):
            copy, here, _ = weight_copy(n)

            @pl.when(jnp.logical_not(here))
            def _():
                copy.wait_send()

            return carry

        def tile_copy(n):
            owner, i = owner_of(n)
            block = 2 * x + zh
            src, dst = R[tile_s].at[n // 4, n % 4], R[tile_r].at[i, block]
            device = (owner // 8, owner % 8)
            return remote(src, dst, t_base + n, device, t_base + 12), owner == me, (i, block)

        def tile_send(n, carry):
            copy, here, (i, block) = tile_copy(n)

            @pl.when(jnp.logical_not(here))
            def _():
                copy.start()

            @pl.when(here)
            def _():
                pltpu.make_async_copy(R[tile_s].at[n // 4, n % 4], R[tile_r].at[i, block], RS.at[t_base + 12]).start()

            return carry

        def tile_wait(n, carry):
            copy, here, _ = tile_copy(n)

            @pl.when(jnp.logical_not(here))
            def _():
                copy.wait_send()

            return carry

        s_base = [take(13), take(13)]

        def rank_of(c_, zl_, y_):
            return 4 * c_ + 2 * zl_ + y_

        top, low_rows = slice(0, tokens // 2), slice(tokens // 2, tokens)

        def s_copy(l, i):
            py, pz, pd = rank_of(c, zl, 1 - y), rank_of(c, 1 - zl, y), rank_of(c, 1 - zl, 1 - y)
            r = R[s_all[l]]
            ref, device = (
                (r.at[rank, top], y_dev),
                (r.at[rank, low_rows], y_dev),
                (r.at[rank, low_rows], z_dev),
                (r.at[rank, top], z_dev),
                (r.at[rank], c_dev),
                (r.at[py, top], z_dev),
                (r.at[pz, low_rows], y_dev),
                (r.at[py, top], c_dev),
                (r.at[py, low_rows], c_dev),
                (r.at[pz, low_rows], c_dev),
                (r.at[pz, top], c_dev),
                (r.at[pd, top], c_dev),
                (r.at[pd, low_rows], c_dev),
            )[i]
            return remote(ref, ref, s_base[l] + i, device)

        def s_start(l, *which):
            for i in which:
                s_copy(l, i).start()

        def s_got(l, *which):
            for i in which:
                s_copy(l, i).wait_recv()

        own_rank = R[s_all[0]].at[rank]
        swap_rank = R[s_all[0]].at[rank_of(1 - c, zl, y)]

        def swap_rows(rows, idx):
            return swap(in_ref.at[rows], swap_rank.at[rows], idx)

        @pl.when(swapped)
        def _():
            swap_rows(top, s_idx).start()
            swap_rows(low_rows, s2_idx).start()
            swap(R[p_out], R[p_in], p_idx).start()

        @pl.when(jnp.logical_not(swapped))
        def _():
            own_rank[...] = in_ref[...]
            R[p_in][...] = R[p_out][...]

        ag = {}
        for n in everything:
            ag[n] = (take(2), take(2), take(2), take(1))

        def ag_z(n, _):
            own = R[n.weight].at[:, x, c, zh, zl, y]
            cp = remote(own, own, ag[n][0], zz_dev)
            cp.start()
            sends.append(cp)
            return [cp]

        def ag_zz(n, waits):
            waits[0].wait_recv()
            part = R[n.weight].at[:, x, c, :, zl, y]
            cp = remote(part, part, ag[n][0] + 1, z_dev)
            cp.start()
            sends.append(cp)
            return [cp]

        def ag_a(n, waits):
            waits[0].wait_recv()
            w = R[n.weight]
            cps = []
            for h in range(n.halves):
                part = w.at[h, x, c, :, :, y]
                cps.append(remote(part, part, ag[n][1] + h, y_dev if n.y_first[h] else x_dev))
                cps[-1].start()
            sends.extend(cps)
            return cps

        def ag_b(n, waits):
            w = R[n.weight]
            cps = []
            for h in range(n.halves):
                waits[h].wait_recv()
                part = w.at[h, x, c] if n.y_first[h] else w.at[h, :, c, :, :, y]
                cps.append(remote(part, part, ag[n][2] + h, x_dev if n.y_first[h] else y_dev))
                cps[-1].start()
            sends.extend(cps)
            return cps

        def ag_c(n, waits):
            for cp in waits:
                cp.wait_recv()
            part = R[n.weight].at[:, :, c]
            cp = remote(part, part, ag[n][3], c_dev)
            cp.start()
            sends.append(cp)
            return [cp]

        state = {}

        def step(stage, n):
            state[n] = stage(n, state.get(n))

        def arrived(n):
            for cp in state[n]:
                cp.wait_recv()


        @pl.when(jnp.logical_not(swapped))
        def _():
            s_start(0, 0, 2, 1, 3, 4)

        all_in()

        @pl.when(swapped)
        def _():
            swap_rows(top, s_idx).wait()
            s_start(0, 0, 3)
            swap_rows(low_rows, s2_idx).wait()
            s_start(0, 2, 1, 4)
            swap(R[p_out], R[p_in], p_idx).wait()

        step(ag_z, g_up)
        step(ag_z, g_out)
        lax.fori_loop(0, 12, weight_send, 0)
        pltpu.make_async_copy(R[v_own], R[v_all].at[me], RS.at[v_base]).start()
        lax.fori_loop(1, 32, vec_out, 0)
        s_got(0, 0)
        s_start(0, 5, 7)
        s_got(0, 2)
        s_start(0, 6, 9)
        s_got(0, 1)
        s_start(0, 8)
        s_got(0, 3)
        s_start(0, 10)
        step(ag_zz, g_up)
        step(ag_zz, g_out)
        step(ag_z, g_down)
        s_got(0, 5)
        s_start(0, 11)
        s_got(0, 6)
        s_start(0, 12)
        step(ag_a, g_up)
        step(ag_zz, g_down)
        step(ag_a, g_out)
        R[x32][...] = own_rank[...].T.astype(F32)
        s_got(0, 4, 7, 8, 9, 10, 11, 12)
        whole_copy(head_w, w_base + 12).wait()
        whole_copy(v_all, v_base).wait()

        def weight(n, h):
            return R[n.weight][h].reshape(32 * n.rows, n.cols)

        def vec(i):
            return R[v_all][:, :, i : i + 1].reshape(d_model, 1).astype(F32)

        def up_bias(i):
            lanes = [
                R[v_all][8 * i : 8 * (i + 1), :, 8 + b : 9 + b].reshape(8, 1, 16, 1).astype(F32)
                for b in range(4)
            ]
            return jnp.concatenate(lanes, axis=1).reshape(chunk, 1)

        def spread(src, dst):
            base = take(8)
            cps = []
            for k in range(1, 8):
                device, other = peer(k)
                cps.append(remote(src.at[other], dst.at[rank], base + k, device))
                cps[-1].start()
            dst[rank] = src[rank]
            return cps

        def batch(src, dst, base, core):
            def go(ks):
                for k in ks:
                    device, other = peer(k)
                    remote(src.at[other], dst.at[rank], base + k, device).start()

            @pl.when(c == core)
            def _():
                go(range(1, 4))
                dst[rank] = src[rank]

            @pl.when(c != core)
            def _():
                go(range(4, 8))

        def sent(src, dst, base):
            for k in range(1, 8):
                remote(src.at[0], dst.at[0], base + k, peer(k)[0]).wait()

        def finish(cps):
            for cp in cps:
                cp.wait()

        def ext(qb):
            return max(fixed, qb + 1)

        def span(first, last=None):
            return slice(first * tokens, (first + 1 if last is None else last) * tokens)

        def masked(s, qb):
            if qb < fixed:
                kk = lax.broadcasted_iota(jnp.int32, s.shape, 0)
                qq = qb * tokens + lax.broadcasted_iota(jnp.int32, s.shape, 1)
                return jnp.where((kk <= qq) | (kk < R[p_in][0:1, 0:1]), s, NEGATIVE)
            low = s[qb * tokens :]
            kk = lax.broadcasted_iota(jnp.int32, low.shape, 0)
            qq = lax.broadcasted_iota(jnp.int32, low.shape, 1)
            low = jnp.where(kk <= qq, low, NEGATIVE)
            return jnp.concatenate([s[: qb * tokens], low], axis=0)

        def norm(r, gain, shift):
            centre = r - jnp.mean(r, axis=0, keepdims=True)
            inv = lax.rsqrt(jnp.mean(centre * centre, axis=0, keepdims=True) + EPSILON)
            xh = centre * inv
            return xh * gain + shift, xh, inv

        def forward(l):
            rows_all, qkv_all = R[s_all[l]], R[qr[l]]
            if l == 1:
                s_start(1, 0, 2, 1, 3, 4)
                s_got(1, 0)
                s_start(1, 5, 7)
                s_got(1, 2)
                s_start(1, 6, 9)
                s_got(1, 1)
                s_start(1, 8)
                s_got(1, 3)
                s_start(1, 10)
                s_got(1, 5)
                s_start(1, 11)
                s_got(1, 6)
                s_start(1, 12)
                s_got(1, 4, 7, 8, 9, 10, 11, 12)
                step(ag_z, g_qkv)

                @pl.when(swapped)
                def _():
                    swap(cot_ref, R[c_in], c_idx).start()

            packed = R[v_all][pl.ds(4 * rank, 4)]
            packed = packed.reshape(hd, 128).astype(F32)
            bias = jnp.concatenate([packed[:, 0:1], jnp.zeros((hd, 1), F32), packed[:, 1:2]], axis=0)
            w = R[head_w][...].reshape(three, d_model)
            for b in range(8):
                qkv_all[b] = (mm_nt(w, rows_all[b]) + bias).astype(BF16)
            if l == 0:
                step(ag_b, g_up)
                step(ag_a, g_down)
            for b in range(8):
                R[kt][span(b), :] = qkv_all[b, hd : 2 * hd, :].T
                R[vt][span(b), :] = qkv_all[b, 2 * hd :, :].T
            base = take(8)
            for qb in range(8):
                n = ext(qb)
                s = masked(mm_nn(R[kt][span(0, n), :], qkv_all[qb, 0:hd, :]) * EXP2_SCALE, qb)
                m = jnp.max(s, axis=0, keepdims=True)
                p = jnp.exp2(s - m)
                total = jnp.sum(p, axis=0, keepdims=True)
                o = mm_tn(p.astype(BF16), R[vt][span(0, n), :]).T / total
                R[o32[l]][qb] = o
                R[send1][qb] = o.astype(BF16)
                R[lse[l]][qb] = jnp.broadcast_to(m + jnp.log2(total), (8, tokens))
                if qb == 3:
                    batch(R[send1], R[ar[l]], base, 0)
                if l == 0 and qb == 1:
                    step(ag_b, g_out)
                if l == 1 and qb == 4:
                    step(ag_zz, g_qkv)
            batch(R[send1], R[ar[l]], base, 1)
            if l == 0:
                step(ag_b, g_down)
                step(ag_c, g_up)
                step(ag_c, g_out)
                lax.fori_loop(0, 12, weight_wait, 0)
            sent(R[send1], R[ar[l]], base)
            if l == 1:
                step(ag_a, g_qkv)
            if l == 0:
                arrived(g_out)
            att = R[ar[l]][...].reshape(d_model, tokens)
            half = d_model // 2
            r1 = R[x32][...] + vec(2)
            r1 = r1 + mm_nn(weight(g_out, 0), att[:half]) + mm_nn(weight(g_out, 1), att[half:])
            h1, xh, inv = norm(r1, vec(4), vec(5))
            R[h1_][...] = h1
            R[xh1[l]][...] = xh
            R[rs1[l]][...] = jnp.broadcast_to(inv, (8, tokens))
            R[hlow[l]][...] = h1.astype(BF16)
            if l == 0:
                arrived(g_up)
            for i in range(4):
                rows = slice(i * chunk, (i + 1) * chunk)
                g = g_up
                f = up_bias(i)
                for h in range(2):
                    w = R[g_up.weight][h, i // 2, i % 2].reshape(chunk, g.cols)
                    f = f + mm_nn(w, R[hlow[l]][h * half : (h + 1) * half, :])
                cdf = 0.5 * (1.0 + lax.erf(f * ROOT_HALF))
                R[act[l]][rows, :] = (f * cdf).astype(BF16)
                R[slope[l]][rows, :] = cdf + f * (jnp.exp(-0.5 * f * f) * DENSITY_SCALE)
            if l == 0:
                step(ag_c, g_down)
                arrived(g_down)
            r2 = R[h1_][...] + vec(3)
            for h in range(2):
                r2 = r2 + mm_nn(weight(g_down, h), R[act[l]][h * d_ff // 2 : (h + 1) * d_ff // 2, :])
            out, xh, inv = norm(r2, vec(6), vec(7))
            R[xh2[l]][...] = xh
            R[rs2[l]][...] = jnp.broadcast_to(inv, (8, tokens))
            return out

        idx = {n: (take(1), take(2), take(2), take(2)) for n in everything[1:]}

        def rs_c(n, _):
            cp = remote(R[n.grad].at[:, :, 1 - c], R[n.recv1], idx[n][0], c_dev)
            cp.start()
            sends.append(cp)
            return [cp]

        def a_send(n, h):
            g_, r1 = R[n.grad], R[n.recv1]
            if n.x_first[h]:
                value, device = g_[h, 1 - x, c].astype(F32) + r1[h, 1 - x].astype(F32), x_dev
            else:
                value, device = g_[h, :, c, :, :, 1 - y].astype(F32) + r1[h, :, :, :, 1 - y].astype(F32), y_dev
            R[n.send2[h]][...] = value.astype(BF16)
            cp = remote(R[n.send2[h]], R[n.recv2[h]], idx[n][1] + h, device)
            cp.start()
            sends.append(cp)
            return cp

        def rs_a_first(n, waits):
            waits[0].wait_recv()
            return [a_send(n, 0)]

        def rs_a_second(n, waits):
            return waits + [a_send(n, 1)]

        def rs_a(n, waits):
            waits = rs_a_first(n, waits)
            return rs_a_second(n, waits) if n.halves == 2 else waits

        def rs_b(n, waits):
            g_, r1 = R[n.grad], R[n.recv1]
            cps = []
            for h in range(n.halves):
                waits[h].wait_recv()
                r2 = R[n.recv2[h]]
                if n.x_first[h]:
                    value, device = g_[h, x, c, :, :, 1 - y].astype(F32) + r1[h, x, :, :, 1 - y].astype(F32), y_dev
                    value = value + r2[:, :, 1 - y].astype(F32)
                else:
                    value, device = g_[h, 1 - x, c, :, :, y].astype(F32) + r1[h, 1 - x, :, :, y].astype(F32), x_dev
                    value = value + r2[1 - x].astype(F32)
                R[n.send3[h]][...] = value.astype(BF16)
                cps.append(remote(R[n.send3[h]], R[n.recv3[h]], idx[n][2] + h, device))
                cps[-1].start()
            sends.extend(cps)
            return cps

        def rs_z(n, waits):
            g_, r1, sum3 = R[n.grad], R[n.recv1], R[n.sum3]
            for h in range(n.halves):
                waits[h].wait_recv()
                r2 = R[n.recv2[h]]
                kept = r2[:, :, y] if n.x_first[h] else r2[x]
                sum3[:, :, h] = (
                    g_[h, x, c, :, :, y].astype(F32)
                    + r1[h, x, :, :, y].astype(F32)
                    + kept.astype(F32)
                    + R[n.recv3[h]][...].astype(F32)
                )
            R[n.send4][...] = sum3[:, 1 - zl].astype(BF16)
            cp = remote(R[n.send4], R[n.recv4], idx[n][3], z_dev)
            cp.start()
            sends.append(cp)
            return [cp]

        def rs_zz(n, waits):
            waits[0].wait_recv()
            R[n.sum4][...] = R[n.sum3][:, zl] + R[n.recv4][...].astype(F32)
            R[n.send5][...] = R[n.sum4][1 - zh].astype(BF16)
            cp = remote(R[n.send5], R[n.recv5], idx[n][3] + 1, zz_dev)
            cp.start()
            sends.append(cp)
            return [cp]

        def rs_end(n, waits):
            waits[0].wait_recv()
            return R[n.sum4][zh] + R[n.recv5][...].astype(F32)

        def pick(lane, count_=1):
            rows = lax.broadcasted_iota(jnp.int32, (128, tokens), 0)
            return jnp.where((rows >= lane) & (rows < lane + count_), 1.0, 0.0).astype(BF16)

        def low_sum(lane, value):
            return mm_nt(value, pick(lane))

        def full_sum(lane, value):
            high = value.astype(BF16)
            return low_sum(lane, high) + low_sum(lane, (value - high.astype(F32)).astype(BF16))

        def add_grad(n, h, value, l):
            value = value.reshape(n.whole[1:])
            if l == 0:
                value = value + R[n.grad][h].astype(F32)
            R[n.grad][h] = value.astype(BF16)

        def norm_grad(g, xh, inv, gain):
            s = g * gain
            return inv * (
                s - jnp.mean(s, axis=0, keepdims=True) - xh * jnp.mean(s * xh, axis=0, keepdims=True)
            )

        half = d_model // 2

        def out_grad(l):
            att = R[ar[l]][...].reshape(d_model, tokens)
            for h in range(2):
                add_grad(g_out, h, mm_nt(R[dz_][...], att[h * half : (h + 1) * half]), l)

        def up_grad(l):
            for h in range(2):
                add_grad(g_up, h, mm_nt(R[df_][...], R[hlow[l]][h * half : (h + 1) * half, :]), l)

        def down_grad(l):
            for h in range(2):
                add_grad(g_down, h, mm_nt(R[dz2_][...], R[act[l]][h * d_ff // 2 : (h + 1) * d_ff // 2, :]), l)

        def head_grad(l):
            rows_all, back = R[s_all[l]], R[send3]
            t = mm_nn(back[0], rows_all[0])
            sums = low_sum(0, back[0, 0:hd]) + low_sum(1, back[0, 2 * hd :])
            for b in range(1, 8):
                t = t + mm_nn(back[b], rows_all[b])
                sums = sums + low_sum(0, back[b, 0:hd]) + low_sum(1, back[b, 2 * hd :])
            R[gv][pl.ds(pl.multiple_of(rank * hd, hd), hd), :] += sums
            if l == 1:
                R[head_g][...] = t
            else:
                R[tile_s][...] = (R[head_g][...] + t).astype(BF16).reshape(3, 4, 16, d_model)

        def dense_sums(l):
            t = full_sum(6, R[g32][...] * R[xh2[l]][...]) + full_sum(7, R[g32][...])
            t = t + full_sum(4, R[dh32][...] * R[xh1[l]][...]) + full_sum(5, R[dh32][...])
            t = t + low_sum(3, R[dz2_][...]) + low_sum(2, R[dz_][...])
            R[gv][...] += t
            ones = pick(8, 4)
            lanes = lax.broadcasted_iota(jnp.int32, (8, 16, 128), 2)
            for i in range(4):
                sums = mm_nt(R[df_][i * chunk : (i + 1) * chunk, :], ones).reshape(8, 4, 16, 128)
                t = jnp.where(lanes == 8, sums[:, 0], 0.0)
                for b in range(1, 4):
                    t = jnp.where(lanes == 8 + b, sums[:, b], t)
                R[gv][i * 128 : (i + 1) * 128, :] += t.reshape(128, 128)

        def backward(l):
            dr2 = norm_grad(R[g32][...], R[xh2[l]][...], R[rs2[l]][0:1, :], vec(6))
            R[dz2_][...] = dr2.astype(BF16)
            R[x32][...] = dr2
            if l == 0:
                down_grad(l)
                step(rs_c, g_down)
            for i in range(4):
                rows = slice(i * chunk, (i + 1) * chunk)
                h, lo = i // 2, (i % 2) * chunk
                w = R[g_down.weight][h].reshape(d_model, d_ff // 2)[:, lo : lo + chunk]
                R[df_][rows, :] = (mm_tn(w, R[dz2_][...]) * R[slope[l]][rows, :]).astype(BF16)
            if l == 0:
                step(rs_a, g_down)
                up_grad(l)
                step(rs_c, g_up)
            for h in range(2):
                rows = slice(h * half, (h + 1) * half)
                R[dh32][rows, :] = R[x32][rows, :] + mm_tn(weight(g_up, h), R[df_][...])
            dr1 = norm_grad(R[dh32][...], R[xh1[l]][...], R[rs1[l]][0:1, :], vec(4))
            R[dz_][...] = dr1.astype(BF16)
            R[x32][...] = dr1
            for h in range(2):
                datt = mm_tn(weight(g_out, h), R[dz_][...]).astype(BF16)
                R[send1][h * 4 : (h + 1) * 4] = datt.reshape(4, hd, tokens)
            cps = spread(R[send1], R[dr[l]])
            if l == 1:
                down_grad(l)
                up_grad(l)
            else:
                step(rs_a_first, g_up)
            out_grad(l)
            if l == 0:
                step(rs_c, g_out)
            dense_sums(l)
            finish(cps)
            if l == 0:
                step(rs_a_second, g_up)
                step(rs_a, g_out)
            else:
                step(ag_b, g_qkv)

                @pl.when(swapped)
                def _():
                    swap(R[o_send], o_out, so_idx).start()

            qkv_all, datt_all = R[qr[l]], R[dr[l]]
            for b in range(8):
                R[qt][span(b), :] = qkv_all[b, 0:hd, :].T
                R[kt][span(b), :] = qkv_all[b, hd : 2 * hd, :].T
                R[vt][span(b), :] = qkv_all[b, 2 * hd :, :].T
                R[dt][span(b), :] = datt_all[b].T
            R[dk][...] = jnp.zeros((seq_len, hd), F32)
            R[dv][...] = jnp.zeros((seq_len, hd), F32)
            base = take(8)
            src, dst = R[send3], R[er[l]]

            def keys_out(b):
                src[b, hd : 2 * hd, :] = (R[dk][span(b), :] * SCORE_SCALE).T.astype(BF16)
                src[b, 2 * hd :, :] = R[dv][span(b), :].T.astype(BF16)

            for qb in range(7, -1, -1):
                n = ext(qb)
                keys = span(0, n)
                delta = jnp.sum(datt_all[qb].astype(F32) * R[o32[l]][qb], axis=0, keepdims=True)
                s = masked(mm_nn(R[kt][keys, :], qkv_all[qb, 0:hd, :]) * EXP2_SCALE, qb)
                p = jnp.exp2(s - R[lse[l]][qb, 0:1, :])
                dprob = mm_nn(R[vt][keys, :], datt_all[qb])
                dsc = (p * (dprob - delta)).astype(BF16)
                R[dv][keys, :] += mm_nn(p.astype(BF16), R[dt][span(qb), :])
                R[dk][keys, :] += mm_nn(dsc, R[qt][span(qb), :])
                src[qb, 0:hd, :] = (mm_tn(R[kt][keys, :], dsc) * SCORE_SCALE).astype(BF16)
                if qb == 4:
                    for b in range(4, 8):
                        keys_out(b)
                    batch(src, dst, base, 1)
            for b in range(4):
                keys_out(b)
            batch(src, dst, base, 0)
            if l == 1:
                step(ag_c, g_qkv)
            if l == 0:
                step(rs_b, g_down)
            head_grad(l)
            if l == 0:
                lax.fori_loop(0, 12, tile_send, 0)
                R[v_send][...] = R[gv][...].astype(BF16).reshape(32, 16, 128)
                pltpu.make_async_copy(R[v_send].at[me], R[v_recv].at[me], RS.at[v_base + 1]).start()
                lax.fori_loop(1, 32, vec_back, 0)
            else:
                arrived(g_qkv)
            if l == 0:
                step(rs_b, g_out)
            sent(src, dst, base)
            back = R[er[l]]
            for h in range(2):
                w = weight(g_qkv, h)
                t = R[x32][h * half : (h + 1) * half, :]
                for part in range(3):
                    grad = back[:, part * hd : (part + 1) * hd, :].reshape(d_model, tokens)
                    t = t + mm_tn(w[part * d_model : (part + 1) * d_model], grad)
                R[g32][h * half : (h + 1) * half, :] = t

        mid = forward(0)
        R[x32][...] = mid
        R[s_all[1]][rank] = mid.astype(BF16).T
        last = forward(1)
        R[o_send][...] = last.astype(BF16).T

        @pl.when(swapped)
        def _():
            swap(cot_ref, R[c_in], c_idx).wait()

        @pl.when(jnp.logical_not(swapped))
        def _():
            o_out[...] = R[o_send][...]
            R[c_in][...] = cot_ref[...]

        R[gv][...] = jnp.zeros((d_model, 128), F32)
        R[g32][...] = R[c_in][...].T.astype(F32)
        backward(1)
        backward(0)
        R[i_send][...] = R[g32][...].astype(BF16).T

        @pl.when(swapped)
        def _():
            swap(R[i_send], R[i_recv], si_idx).start()

        @pl.when(jnp.logical_not(swapped))
        def _():
            o_ig[...] = R[g32][...].T

        step(rs_z, g_down)
        step(rs_b, g_up)
        step(rs_z, g_out)
        step(rs_zz, g_down)
        step(rs_z, g_up)
        step(rs_zz, g_out)
        step(rs_zz, g_up)
        whole_copy(tile_r, t_base + 12).wait()
        lax.fori_loop(0, 12, tile_wait, 0)
        t = R[tile_r][:, 0].astype(F32)
        for block in range(1, 4):
            t = t + R[tile_r][:, block].astype(F32)
        o_qkv[...] = t.reshape(48, d_model)
        for n, ref in ((g_down, o_down), (g_up, o_up), (g_out, o_gout)):
            t = rs_end(n, state[n])
            ref[...] = jnp.concatenate([t[0], t[1]], axis=1)
        whole_copy(v_recv, v_base + 1).wait()
        t = R[v_recv][0].astype(F32)
        for i in range(1, 32):
            t = t + R[v_recv][i].astype(F32)
        t = t.T
        o_bias[...] = t[0:4]
        o_norms[...] = t[4:8]
        o_upb[...] = jnp.concatenate([t[8 + b : 9 + b] for b in range(4)], axis=1)

        @pl.when(swapped)
        def _():
            swap(R[o_send], o_out, so_idx).wait()
            swap(R[i_send], R[i_recv], si_idx).wait()
            o_ig[...] = R[i_recv][...].astype(F32)

        for cp in sends:
            cp.wait_send()
        for i in range(2):
            sent_vec = R[v_recv].at[0:31]
            pltpu.make_async_copy(sent_vec, sent_vec, SS.at[v_base + i]).wait()
        for l in range(2):
            for i in range(13):
                s_copy(l, i).wait_send()

    n_sems = 6 + 2 * 13 + 2 * 13 + 2 + 4 * 7 + 6 * 8 + 3 * 7

    def kernel(*refs):
        count[0] = 0
        body(refs[:10], refs[10:19], refs[19:-3], refs[-3], refs[-2], refs[-1])
        assert count[0] <= n_sems

    def hand_on(*refs):
        for src, dst in zip(refs[:9], refs[9:]):
            dst[...] = src[...]

    def call(inputs, qkv_w, out_w, up_w, down_w, biases, up_bias, norms, cotangent, prefix):
        weights = [w.T for w in (qkv_w, out_w, up_w, down_w)]
        small = [biases, up_bias.reshape(1, -1), norms]
        out_shape = (
            jax.ShapeDtypeStruct((tokens, d_model), BF16),
            jax.ShapeDtypeStruct((tokens, d_model), F32),
            *(jax.ShapeDtypeStruct(w.shape, F32) for w in weights + small),
        )
        vmem = pl.BlockSpec(memory_space=pltpu.VMEM)
        results = pl.pallas_call(
            kernel,
            out_shape=out_shape,
            in_specs=[vmem] * 9 + [pl.BlockSpec(memory_space=pltpu.SMEM)],
            out_specs=[vmem] * 9,
            scratch_shapes=[
                *scratch,
                pltpu.SemaphoreType.DMA((n_sems,)),
                pltpu.SemaphoreType.DMA((n_sems,)),
                pltpu.SemaphoreType.REGULAR((5,)),
            ],
            compiler_params=pltpu.CompilerParams(
                collective_id=0, has_side_effects=True, vmem_limit_bytes=62 * 2**20
            ),
        )(inputs, *weights, *small, cotangent, prefix)
        results = pl.pallas_call(
            hand_on, out_shape=out_shape, in_specs=[vmem] * 9, out_specs=[vmem] * 9
        )(*results)
        back = [w.T for w in results[2:6]]
        return (*results[:2], *back, results[6], results[7].reshape(up_bias.shape), results[8])

    return call


def fused_fits(mesh, args):
    if tuple(mesh.shape.items()) != (("dp", 4), ("seq", 8)) or HEADS != 8:
        return False
    total, d_model = args[0].shape
    d_ff = args[3].shape[1]
    return total % (32 * 128) == 0 and total // 32 == 256 and d_model == 512 and d_ff == 2048


def solution(mesh):
    specs = dict(
        mesh=mesh,
        in_specs=(
            P(("dp", "seq"), None),
            P(None, ("dp", "seq")),
            P(None, ("dp", "seq")),
            P(None, ("dp", "seq")),
            P(None, ("dp", "seq")),
            P(None, ("dp", "seq")),
            P(("dp", "seq")),
            P(None, ("dp", "seq")),
            P(("dp", "seq"), None),
            P("dp"),
        ),
        out_specs=(
            P(("dp", "seq"), None),
            P(("dp", "seq"), None),
            P(None, ("dp", "seq")),
            P(None, ("dp", "seq")),
            P(None, ("dp", "seq")),
            P(None, ("dp", "seq")),
            P(None, ("dp", "seq")),
            P(("dp", "seq")),
            P(None, ("dp", "seq")),
        ),
        check_vma=False,
    )

    def run(*args):
        if fused_fits(mesh, args):
            d_model = args[0].shape[1]
            step = fused_step(args[0].shape[0] // 32, d_model, args[3].shape[1], HEADS)
            return jax.shard_map(step, **specs)(*args)
        return jax.shard_map(local, **specs)(*args)

    return run
```
